32 devices in a mesh: pre: 4 (over z), row: 8 (over y, x, core).
Axes of the slice: x: 2, y: 2, z: 4, core: 2. Of those that a mesh axis runs over, the one named last changes fastest.
Arguments:
- hidden_in: bfloat16 [4096, 8192], P('row'), may hold values from -6 to 6
- frozen_query_base: bfloat16 [4096, 1024], P('row'), may hold values from -10 to 10
- k_prefix: bfloat16 [8192, 128], P('pre'), may hold values from -6 to 6
- v_prefix: bfloat16 [8192, 128], P('pre'), may hold values from -6 to 6
- tree_mask: int32 [8, 64], P(None, 'pre'), may hold values from 0 to 1, as said below
- adapter_ids: int32 [8], replicated, may hold values from 0 to 7, each once
- a_down: bfloat16 [8192, 128], P('row'), may hold values from -0.0625 to 0.0625
- up_weight_matrix: bfloat16 [128, 1024], replicated, may hold values from -0.75 to 0.75
- cotangent: bfloat16 [4096, 1024], P('row'), may hold values from -6 to 6
Outputs:
- attended: bfloat16 [4096, 1024], P('row')
- grad_a: float32 [8192, 128], P('row')
- up_weight_gradient: float32 [128, 1024], replicated
The draws below stay inside these ranges and needn't reach their ends.
Inputs may be any that keep to these rules, and one draw needn't show every extreme that they name: `tree_mask`: every student reads mask block 0. The blocks that a student reads lie on one path of a tree of branches shared by the students: blocks near the start of the prefix are read by more students than blocks near its end.
All inputs are finite; a program needn't handle non-finite values.
Results may differ from the reference program's by a relative error of at most 0.014.
Values may be sent and summed in bfloat16 or wider, within the bound.
No kernel may reach another device: no remote copies, remote signals or barrier semaphores. Data moves between devices by JAX's collectives and lax.ppermute only.
A program may use at most 64 MiB of HBM per device.

```python
import math
import jax
import jax.numpy as jnp
from jax import lax

D = 8192
HQ = 8
HD = 128
RANK = 16
S = 8
CONT = 512
MB = 128
PREFIX = 8192
TOKENS = 4096
NA = 8


def draw_k_prefix(key, part):
    base = jnp.clip(jax.random.normal(jax.random.fold_in(key, 1), (PREFIX, HD), jnp.float32), -6.0, 6.0)
    return base.astype(jnp.bfloat16)


def draw_frozen_query_base(key, part):
    base = jnp.clip(2.5 * jax.random.normal(jax.random.fold_in(key, 2), (TOKENS, HQ * HD), jnp.float32), -10.0, 10.0)
    return base.astype(jnp.bfloat16)


def draw_tree_mask(key, part):
    block_total = PREFIX // MB
    blocks = jnp.arange(block_total)
    bounds = [0, block_total // 4, block_total // 2, 3 * block_total // 4, block_total]
    reads = jnp.broadcast_to((blocks < bounds[1])[None, :], (S, block_total))
    for level in range(1, 4):
        branches = 2 ** level
        begin = bounds[level]
        finish = bounds[level + 1]
        span = finish - begin
        widths = jax.random.randint(jax.random.fold_in(key, 11 + level), (branches,), 1, 4)
        cuts = begin + jnp.cumsum(widths) * span // jnp.sum(widths)
        branch_of = jnp.sum((blocks[:, None] >= cuts[None, :-1]).astype(jnp.int32), axis=1)
        inside = (blocks >= begin) & (blocks < finish)
        student_branch = jnp.arange(S) * branches // S
        reads = reads | inside[None, :] & (branch_of[None, :] == student_branch[:, None])
    return reads.astype(jnp.int32)


def levels(own_key, extent, split, low, largest):
    gain, own = 1.0, jax.random.fold_in(own_key, 6)
    for position, parts in split:
        steps = jnp.exp(jax.random.uniform(jax.random.fold_in(own, position), (parts,), jnp.float32, low / len(split), largest / len(split)))
        gain = gain * jnp.repeat(steps, extent[position] // parts).reshape([-1 if axis == position else 1 for axis in range(len(extent))])
    return gain


def noise(key, extent, spread, reach, shards=(), held_as=jnp.bfloat16):
    values = jax.random.normal(key, extent, jnp.float32) * spread
    if len(shards) > 0:
        values = levels(key, extent, shards, -0.22, 0.18) * values
    return jnp.clip(values, min=-reach, max=reach).astype(held_as)


def setup_inputs(seed: int = 0) -> dict:
    splits = jax.random.split(jax.random.key(seed), 10)
    hidden_in = noise(splits[0], (TOKENS, D), 1.0, 6.0, ((0, 8),))
    frozen_query_base = draw_frozen_query_base(jax.random.fold_in(splits[9], 71), 0)
    k_prefix = draw_k_prefix(jax.random.fold_in(splits[9], 71), 0)
    v_prefix = noise(splits[3], (PREFIX, HD), 1.0, 6.0, ((0, 4),))
    tree_mask = draw_tree_mask(jax.random.fold_in(splits[9], 71), 0)
    adapter_ids = jax.random.permutation(splits[5], S).astype(jnp.int32)
    a_down = noise(splits[6], (D, NA * RANK), D ** -0.5, 0.0625, ((0, 8),))
    up_weight_matrix = noise(splits[7], (NA * RANK, HQ * HD), (4 * RANK) ** -0.5, 0.75)
    cotangent = noise(splits[8], (TOKENS, HQ * HD), 1.0, 6.0, ((0, 8),))
    return {"hidden_in": hidden_in, "frozen_query_base": frozen_query_base, "k_prefix": k_prefix, "v_prefix": v_prefix, "tree_mask": tree_mask, "adapter_ids": adapter_ids, "a_down": a_down, "up_weight_matrix": up_weight_matrix, "cotangent": cotangent}


ADAPTER_SCALE = 2.0

def reference(hidden_in, frozen_query_base, k_prefix, v_prefix, tree_mask, adapter_ids, a_down, up_weight_matrix, cotangent):
    score_scale = 1.0 / math.sqrt(HD)
    latent_full = jnp.dot(hidden_in, a_down, preferred_element_type=jnp.float32)
    student_of = (jnp.arange(TOKENS) // CONT).astype(jnp.int32)
    token_adapter = adapter_ids[student_of]
    column_mask = (jnp.arange(NA * RANK) // RANK)[None, :] == token_adapter[:, None]
    low_rank_code = jnp.where(column_mask, latent_full, jnp.float32(0.0)).astype(jnp.bfloat16)
    raised_query = jnp.dot(low_rank_code, up_weight_matrix, preferred_element_type=jnp.float32)
    student_queries = (frozen_query_base.astype(jnp.float32) + ADAPTER_SCALE * raised_query).astype(jnp.bfloat16)
    query_groups = student_queries.reshape(S, CONT, HQ, HD).transpose(0, 2, 1, 3).reshape(S * HQ, CONT, HD)
    upstream_groups = cotangent.reshape(S, CONT, HQ, HD).transpose(0, 2, 1, 3).reshape(S * HQ, CONT, HD)
    live_all = jnp.repeat(tree_mask > 0, MB, axis=1)
    group_student = (jnp.arange(S * HQ) // HQ).astype(jnp.int32)

    def per_group(inputs):
        query_rows, upstream, owner = inputs
        live_keys = live_all[owner][None, :]
        scores = jnp.dot(query_rows, k_prefix.T, preferred_element_type=jnp.float32) * score_scale
        row_max = lax.optimization_barrier(jnp.max(jnp.where(live_keys, scores, -jnp.inf), axis=1))
        expo = jnp.where(live_keys, jnp.exp(scores - row_max[:, None]), jnp.float32(0.0))
        row_sum = lax.optimization_barrier(jnp.sum(expo, axis=1))
        weights = expo.astype(jnp.bfloat16)
        summed = jnp.dot(weights, v_prefix, preferred_element_type=jnp.float32)
        attended_rows = (summed / row_sum[:, None]).astype(jnp.bfloat16)
        log_total = row_max + jnp.log(row_sum)
        probs = jnp.where(live_keys, jnp.exp(scores - log_total[:, None]), jnp.float32(0.0))
        row_delta = lax.optimization_barrier(jnp.sum(upstream.astype(jnp.float32) * attended_rows.astype(jnp.float32), axis=1))
        grad_probs = jnp.dot(upstream, v_prefix.T, preferred_element_type=jnp.float32)
        grad_scores = (probs * (grad_probs - row_delta[:, None])).astype(jnp.bfloat16)
        grad_rows = jnp.dot(grad_scores, k_prefix, preferred_element_type=jnp.float32) * score_scale
        return (attended_rows, grad_rows)
    attended_groups, grad_groups = lax.map(per_group, (query_groups, upstream_groups, group_student))
    attended = attended_groups.reshape(S, HQ, CONT, HD).transpose(0, 2, 1, 3).reshape(TOKENS, HQ * HD)
    query_gradient = grad_groups.reshape(S, HQ, CONT, HD).transpose(0, 2, 1, 3).reshape(TOKENS, HQ * HD).astype(jnp.bfloat16)
    backward_low_rank = ADAPTER_SCALE * jnp.dot(query_gradient, up_weight_matrix.T, preferred_element_type=jnp.float32)
    grad_latent = jnp.where(column_mask, backward_low_rank, jnp.float32(0.0)).astype(jnp.bfloat16)
    grad_a = jnp.dot(hidden_in.T, grad_latent, preferred_element_type=jnp.float32)
    up_weight_gradient = ADAPTER_SCALE * jnp.dot(low_rank_code.T, query_gradient, preferred_element_type=jnp.float32)
    return (attended, grad_a, up_weight_gradient)
```

```python
import functools
import math

import jax
import jax.numpy as jnp
from jax import lax
from jax.experimental import pallas as pl
from jax.experimental.pallas import tpu as pltpu
from jax.sharding import PartitionSpec as P

HD = 128
RANK = 16
CONT = 512
MB = 128
CHUNK = 512
ROW_TILE = 256
MIN_TOKENS = 16
ADAPTER_SCALE = 2.0
VERY_LOW = -1e30
LOG2E = 1.4426950408889634
MIB = 1 << 20

NT = (((1,), (1,)), ((), ()))
VMEM = pl.BlockSpec(memory_space=pltpu.VMEM)
SMEM = pl.BlockSpec(memory_space=pltpu.SMEM)
ANY = pl.BlockSpec(memory_space=pl.ANY)


def dot(a, b):
    return jnp.dot(a, b, preferred_element_type=jnp.float32)


def dot_nt(a, b):
    return lax.dot_general(a, b, NT, preferred_element_type=jnp.float32)


def swap(x, axis, mask):
    if mask == 0:
        return x
    return lax.ppermute(x, axis, [(s, s ^ mask) for s in range(lax.axis_size(axis))])


def params(mib):
    return pltpu.CompilerParams(vmem_limit_bytes=mib * MIB)


def adapter_of(info, row, tokens):
    return info[3 + row * tokens // CONT]


def pick_kernel(n_row, tokens, info, a_ref, *rest):
    outs, at = rest[:n_row], rest[n_row]
    at[...] = a_ref[...].astype(jnp.float32).T
    for i in range(n_row):
        first = pl.multiple_of(adapter_of(info, info[1] ^ i, tokens) * RANK, RANK)
        outs[i][...] = at[pl.ds(first, RANK), :].astype(jnp.bfloat16)


def query_kernel(n_row, tokens, info, hidden, base, up_ref, *rest):
    pieces = rest[:n_row]
    q_ref, latt_ref, hid, frozen, sems = rest[n_row:]
    slot_tokens = q_ref.shape[0]
    depth = pieces[0].shape[1]
    start = pl.multiple_of(info[2] * slot_tokens, slot_tokens)
    get_hidden = pltpu.make_async_copy(hidden.at[pl.ds(start, slot_tokens), :], hid, sems.at[0])
    get_base = pltpu.make_async_copy(base.at[pl.ds(start, slot_tokens), :], frozen, sems.at[1])
    get_hidden.start()
    get_base.start()
    get_hidden.wait()
    latent = jnp.zeros((slot_tokens, RANK), jnp.float32)
    latent_t = jnp.zeros((RANK, slot_tokens), jnp.float32)
    for i in range(n_row):
        at = pl.multiple_of((info[1] ^ i) * depth, depth)
        block = hid[:, pl.ds(at, depth)]
        latent += dot_nt(block, pieces[i][...])
        latent_t += dot_nt(pieces[i][...], block)
    latt_ref[...] = latent_t.astype(jnp.bfloat16)
    first = pl.multiple_of(adapter_of(info, info[1], tokens) * RANK, RANK)
    raised = dot(latent.astype(jnp.bfloat16), up_ref[pl.ds(first, RANK), :])
    get_base.wait()
    q_ref[...] = (frozen[...].astype(jnp.float32) + ADAPTER_SCALE * raised).astype(jnp.bfloat16)


def attention_kernel(n_pre, slices, drop, tokens, info, *refs):
    masks, refs = refs[:n_pre], refs[n_pre:]
    q_ref, cot_hbm, latt_ref, up_ref, k_own, v_own = refs[:6]
    k_parts, v_parts, refs = refs[6 : 6 + slices], refs[6 + slices : 6 + 2 * slices], refs[6 + 2 * slices :]
    att_ref, sent_ref, kv, q, cot, top, total, acc, cot_in, grads, sem = refs
    slot_tokens, width = q_ref.shape
    heads = width // HD
    rows = heads * slot_tokens
    tile = min(ROW_TILE, rows)
    scale = 1.0 / math.sqrt(HD)
    factor = scale * LOG2E

    start = pl.multiple_of(info[2] * slot_tokens, slot_tokens)
    get_cot = pltpu.make_async_copy(cot_hbm.at[pl.ds(start, slot_tokens), :], cot_in, sem)
    get_cot.start()

    student = info[1] * tokens // CONT
    part_rows = k_parts[0].shape[1]
    per_part = part_rows // MB

    def keep(count, live, key_block, value_block):
        @pl.when(live)
        def _():
            at = pl.ds(pl.multiple_of(count * MB, MB), MB)
            kv[at, :HD] = value_block()
            kv[at, HD:] = key_block()

        return count + live.astype(jnp.int32)

    def own_block(b, count):
        at = pl.ds(pl.multiple_of(b * MB, MB), MB)
        return keep(count, masks[0][student, b] > 0, lambda: k_own[at, :], lambda: v_own[at, :])

    count = lax.fori_loop(0, k_own.shape[0] // MB, own_block, jnp.int32(0))
    for i in range(slices):
        piece = (info[1] >> drop) ^ i
        for j in range(1, n_pre):
            for u in range(per_part):
                at = pl.ds(u * MB, MB)
                count = keep(
                    count,
                    masks[j][student, piece * per_part + u] > 0,
                    lambda: k_parts[i][j - 1, at, :],
                    lambda: v_parts[i][j - 1, at, :],
                )

    get_cot.wait()
    for h in range(heads):
        at = pl.ds(h * slot_tokens, slot_tokens)
        q[at, :] = q_ref[:, h * HD : (h + 1) * HD]
        cot[at, :] = cot_in[:, h * HD : (h + 1) * HD]
    top[...] = jnp.full_like(top, VERY_LOW)
    total[...] = jnp.zeros_like(total)
    acc[...] = jnp.zeros_like(acc)

    def step(first, size):
        both = kv[pl.ds(pl.multiple_of(first, MB), size), :]
        values, keys = both[:, :HD], both[:, HD:]
        lanes = size // HD
        for r0 in range(0, rows, tile):
            at = pl.ds(r0, tile)
            scores = dot_nt(q[at, :], keys)
            old = top[at, :]
            new = jnp.maximum(old, jnp.max(scores, axis=1, keepdims=True))
            top[at, :] = new
            weights = jnp.exp2((scores - jnp.concatenate([new] * lanes, axis=1)) * factor)
            shrink = jnp.exp2((old - new) * factor)
            partial = weights[:, :HD]
            for c in range(1, lanes):
                partial = partial + weights[:, c * HD : (c + 1) * HD]
            total[at, :] = total[at, :] * shrink + partial
            grad_weights = (weights * dot_nt(cot[at, :], values)).astype(jnp.bfloat16)
            first_two = dot(weights.astype(jnp.bfloat16), both)
            last = dot(grad_weights, keys)
            acc[at, :HD] = acc[at, :HD] * shrink + first_two[:, :HD]
            acc[at, HD : 2 * HD] = acc[at, HD : 2 * HD] * shrink + first_two[:, HD:]
            acc[at, 2 * HD :] = acc[at, 2 * HD :] * shrink + last

    per_chunk = CHUNK // MB
    full = count // per_chunk

    def full_step(c, carry):
        step(c * CHUNK, CHUNK)
        return carry

    def rest_step(c, carry):
        step((full * per_chunk + c) * MB, MB)
        return carry

    lax.fori_loop(0, full, full_step, 0)
    lax.fori_loop(0, count - full * per_chunk, rest_step, 0)

    for h in range(heads):
        at = pl.ds(h * slot_tokens, slot_tokens)
        inverse = 1.0 / jnp.sum(total[at, :], axis=1, keepdims=True)
        attended = (acc[at, :HD] * inverse).astype(jnp.bfloat16)
        att_ref[:, h * HD : (h + 1) * HD] = attended
        delta = jnp.sum(
            cot[at, :].astype(jnp.float32) * attended.astype(jnp.float32), axis=1, keepdims=True
        )
        grad = (acc[at, 2 * HD :] - delta * acc[at, HD : 2 * HD]) * (inverse * scale)
        grads[:, h * HD : (h + 1) * HD] = grad.astype(jnp.bfloat16)
    first = pl.multiple_of(adapter_of(info, info[1], tokens) * RANK, RANK)
    query_gradient = grads[...]
    up = up_ref[pl.ds(first, RANK), :]
    sent_ref[:, :width] = (ADAPTER_SCALE * dot(latt_ref[...], query_gradient)).astype(jnp.bfloat16)
    sent_ref[:, width:] = (ADAPTER_SCALE * dot_nt(up, query_gradient)).astype(jnp.bfloat16)


def down_kernel(n_slots, n_row, width, info, *refs):
    parts, hidden, refs = refs[:n_slots], refs[n_slots], refs[n_slots + 1 :]
    outs, hid, sems = refs[:n_row], refs[n_row], refs[n_row + 1]
    depth = hid.shape[2]
    slot_tokens = parts[0].shape[1] - width
    copies = []
    for i in range(n_row):
        at = pl.multiple_of((info[1] ^ i) * depth, depth)
        copies.append(pltpu.make_async_copy(hidden.at[:, pl.ds(at, depth)], hid.at[i], sems.at[i]))
        copies[-1].start()
    up = parts[0][:, :width].astype(jnp.float32)
    for part in parts[1:]:
        up = up + part[:, :width].astype(jnp.float32)
    up = up.astype(jnp.bfloat16)
    for i in range(n_row):
        outs[i][:, depth:] = up
        copies[i].wait()
        grad = jnp.zeros((RANK, depth), jnp.float32)
        for j in range(n_slots):
            at = pl.multiple_of((info[2] ^ j) * slot_tokens, slot_tokens)
            grad += dot(parts[j][:, width:], hid[i, pl.ds(at, slot_tokens), :])
        outs[i][:, :depth] = grad.astype(jnp.bfloat16)


def finish_kernel(n_slots, n_row, tokens, info, *refs):
    parts, refs = refs[:n_row], refs[n_row:]
    att, refs = refs[:n_slots], refs[n_slots:]
    att_out, down_ref, up_ref, down, sems = refs
    slot_tokens = att[0].shape[0]
    depth = down.shape[1]
    copies = []
    for j in range(n_slots):
        at = pl.multiple_of((info[2] ^ j) * slot_tokens, slot_tokens)
        copies.append(pltpu.make_async_copy(att[j], att_out.at[pl.ds(at, slot_tokens), :], sems.at[j]))
        copies[-1].start()
    down[...] = jnp.zeros_like(down)
    up_ref[...] = jnp.zeros_like(up_ref)
    for i in range(n_row):
        first = pl.multiple_of(adapter_of(info, info[1] ^ i, tokens) * RANK, RANK)
        at = pl.ds(first, RANK)
        down[at, :] += parts[i][:, :depth].astype(jnp.float32)
        up_ref[at, :] += parts[i][:, depth:].astype(jnp.float32)
    down_ref[...] = down[...].T
    for copy in copies:
        copy.wait()


def shards(
    hidden_in,
    frozen_query_base,
    k_prefix,
    v_prefix,
    tree_mask,
    adapter_ids,
    a_down,
    up_weight_matrix,
    cotangent,
):
    tokens, model = hidden_in.shape
    width = frozen_query_base.shape[1]
    heads = width // HD
    depth, rank_cols = a_down.shape
    local_keys = k_prefix.shape[0]
    n_pre, n_row = lax.axis_size("pre"), lax.axis_size("row")
    n_slots = min(n_pre, tokens // MIN_TOKENS)
    slot_tokens = tokens // n_slots
    pre, row = lax.axis_index("pre"), lax.axis_index("row")
    info = jnp.concatenate([jnp.stack([pre, row, pre % n_slots]), adapter_ids]).astype(jnp.int32)
    bf16, f32 = jnp.bfloat16, jnp.float32

    slices = min(n_row, local_keys // MB)
    drop = (n_row // slices).bit_length() - 1
    part_rows = local_keys // slices
    begin = (row >> drop) * part_rows
    key_slice = lax.dynamic_slice_in_dim(k_prefix, begin, part_rows, 0)
    value_slice = lax.dynamic_slice_in_dim(v_prefix, begin, part_rows, 0)
    masks = [swap(tree_mask, "pre", j) for j in range(n_pre)]

    bits = list(range(drop, n_row.bit_length() - 1))
    core, far = bits[: 1 - min(drop, 1)], bits[1 - min(drop, 1) :][::-1]
    half = len(far) // 2

    def spread(piece, order):
        away = jnp.stack([swap(piece, "pre", j) for j in range(1, n_pre)])
        held = [(0, away)]
        for bit in order:
            held += [(mask | 1 << bit, swap(part, "row", 1 << bit)) for mask, part in held]
        return [part for _, part in sorted(held, key=lambda item: item[0])]

    key_parts = spread(key_slice, far + core)
    value_parts = spread(value_slice, far[half:] + far[:half] + core)

    picked = pl.pallas_call(
        functools.partial(pick_kernel, n_row, tokens),
        out_shape=[jax.ShapeDtypeStruct((RANK, depth), bf16)] * n_row,
        in_specs=[SMEM, VMEM],
        out_specs=[VMEM] * n_row,
        scratch_shapes=[pltpu.VMEM((rank_cols, depth), f32)],
        compiler_params=params(16),
        name="pick",
    )(info, a_down)
    pieces = [swap(part, "row", i) for i, part in enumerate(picked)]

    queries, latent_t = pl.pallas_call(
        functools.partial(query_kernel, n_row, tokens),
        out_shape=[
            jax.ShapeDtypeStruct((slot_tokens, width), bf16),
            jax.ShapeDtypeStruct((RANK, slot_tokens), bf16),
        ],
        in_specs=[SMEM, ANY, ANY, VMEM] + [VMEM] * n_row,
        out_specs=[VMEM] * 2,
        scratch_shapes=[
            pltpu.VMEM((slot_tokens, model), bf16),
            pltpu.VMEM((slot_tokens, width), bf16),
            pltpu.SemaphoreType.DMA((2,)),
        ],
        compiler_params=params(16),
        name="queries",
    )(info, hidden_in, frozen_query_base, up_weight_matrix, *pieces)

    rows = heads * slot_tokens
    attended, sent = pl.pallas_call(
        functools.partial(attention_kernel, n_pre, slices, drop, tokens),
        out_shape=[
            jax.ShapeDtypeStruct((slot_tokens, width), bf16),
            jax.ShapeDtypeStruct((RANK, width + slot_tokens), bf16),
        ],
        in_specs=[SMEM] * (1 + n_pre) + [VMEM, ANY, VMEM, VMEM, VMEM, VMEM] + [VMEM] * (2 * slices),
        out_specs=[VMEM] * 2,
        scratch_shapes=[
            pltpu.VMEM((local_keys * n_pre, 2 * HD), bf16),
            pltpu.VMEM((rows, HD), bf16),
            pltpu.VMEM((rows, HD), bf16),
            pltpu.VMEM((rows, HD), f32),
            pltpu.VMEM((rows, HD), f32),
            pltpu.VMEM((rows, 3 * HD), f32),
            pltpu.VMEM((slot_tokens, width), bf16),
            pltpu.VMEM((slot_tokens, width), bf16),
            pltpu.SemaphoreType.DMA,
        ],
        compiler_params=params(48),
        name="attention",
    )(
        info,
        *masks,
        queries,
        cotangent,
        latent_t,
        up_weight_matrix,
        k_prefix,
        v_prefix,
        *key_parts,
        *value_parts,
    )

    shared = [swap(sent, "pre", j) for j in range(n_slots)]
    attended_parts = [swap(attended, "pre", j) for j in range(n_slots)]

    down_parts = pl.pallas_call(
        functools.partial(down_kernel, n_slots, n_row, width),
        out_shape=[jax.ShapeDtypeStruct((RANK, depth + width), bf16)] * n_row,
        in_specs=[SMEM] + [VMEM] * n_slots + [ANY],
        out_specs=[VMEM] * n_row,
        scratch_shapes=[
            pltpu.VMEM((n_row, tokens, depth), bf16),
            pltpu.SemaphoreType.DMA((n_row,)),
        ],
        compiler_params=params(32),
        name="down",
    )(info, *shared, hidden_in)
    down_parts = [swap(part, "row", i) for i, part in enumerate(down_parts)]

    return pl.pallas_call(
        functools.partial(finish_kernel, n_slots, n_row, tokens),
        out_shape=[
            jax.ShapeDtypeStruct((tokens, width), bf16),
            jax.ShapeDtypeStruct((depth, rank_cols), f32),
            jax.ShapeDtypeStruct((rank_cols, width), f32),
        ],
        in_specs=[SMEM] + [VMEM] * (n_row + n_slots),
        out_specs=[ANY, VMEM, VMEM],
        scratch_shapes=[
            pltpu.VMEM((rank_cols, depth), f32),
            pltpu.SemaphoreType.DMA((n_slots,)),
        ],
        compiler_params=params(16),
        name="finish",
    )(info, *down_parts, *attended_parts)


def solution(mesh):
    in_specs = (
        P("row", None),
        P("row", None),
        P("pre", None),
        P("pre", None),
        P(None, "pre"),
        P(),
        P("row", None),
        P(),
        P("row", None),
    )
    out_specs = (P("row", None), P("row", None), P())
    return jax.shard_map(shards, mesh=mesh, in_specs=in_specs, out_specs=out_specs, check_vma=False)
```

```python
import functools
import math

import jax
import jax.numpy as jnp
from jax import lax
from jax.experimental import pallas as pl
from jax.experimental.pallas import tpu as pltpu
from jax.sharding import PartitionSpec as P

HD = 128
RANK = 16
CONT = 512
MB = 128
CHUNK = 512
ROW_TILE = 256
MIN_TOKENS = 16
ADAPTER_SCALE = 2.0
VERY_LOW = -1e30
LOG2E = 1.4426950408889634
MIB = 1 << 20

NT = (((1,), (1,)), ((), ()))
VMEM = pl.BlockSpec(memory_space=pltpu.VMEM)
SMEM = pl.BlockSpec(memory_space=pltpu.SMEM)
ANY = pl.BlockSpec(memory_space=pl.ANY)


def dot(a, b):
    return jnp.dot(a, b, preferred_element_type=jnp.float32)


def dot_nt(a, b):
    return lax.dot_general(a, b, NT, preferred_element_type=jnp.float32)


def swap(x, axis, mask):
    if mask == 0:
        return x
    return lax.ppermute(x, axis, [(s, s ^ mask) for s in range(lax.axis_size(axis))])


def params(mib):
    return pltpu.CompilerParams(vmem_limit_bytes=mib * MIB)


def adapter_of(info, row, tokens):
    return info[4 + row * tokens // CONT]


def mask_rows(mask):
    return -(-mask.shape[0] // 16) * 16


def pack_kernel(n_row, tokens, info, k_ref, v_ref, mask_ref, a_ref, z_ref, even_ref, odd_ref, at):
    depth = a_ref.shape[0]
    cols = depth // HD
    part_rows = (z_ref.shape[0] - mask_rows(mask_ref)) // 2
    begin = pl.ds(pl.multiple_of(info[3] * part_rows, part_rows), part_rows)
    z_ref[:part_rows, :] = k_ref[begin, :]
    z_ref[part_rows : 2 * part_rows, :] = v_ref[begin, :]
    students, blocks = mask_ref.shape
    z_ref[2 * part_rows :, :] = jnp.zeros_like(z_ref[2 * part_rows :, :])
    z_ref[2 * part_rows : 2 * part_rows + students, :blocks] = mask_ref[...].astype(jnp.bfloat16)
    at[...] = a_ref[...].astype(jnp.float32).T
    for i in range(n_row):
        first = pl.multiple_of(adapter_of(info, info[1] ^ i, tokens) * RANK, RANK)
        piece = at[pl.ds(first, RANK), :].astype(jnp.bfloat16)
        out = odd_ref if i & 1 else even_ref
        for c in range(cols):
            out[i >> 1, c * RANK : (c + 1) * RANK, :] = piece[:, c * HD : (c + 1) * HD]


def query_kernel(n_row, tokens, info, hidden, base, up_ref, low_ref, high_ref, q_ref, latt_ref):
    slot_tokens = q_ref.shape[0]
    halves = (low_ref, high_ref)
    cols = low_ref.shape[0] // n_row // RANK
    at = pl.ds(pl.multiple_of(info[2] * slot_tokens, slot_tokens), slot_tokens)
    latent = jnp.zeros((slot_tokens, RANK), jnp.float32)
    latent_t = jnp.zeros((RANK, slot_tokens), jnp.float32)
    for i in range(n_row):
        for half, ref in enumerate(halves):
            piece = jnp.concatenate(
                [ref[(i * cols + c) * RANK : (i * cols + c + 1) * RANK, :] for c in range(cols)], axis=1
            )
            span = cols * HD
            first = pl.multiple_of(((info[1] ^ i) * 2 + half) * span, span)
            block = hidden[at, pl.ds(first, span)]
            latent += dot_nt(block, piece)
            latent_t += dot_nt(piece, block)
    latt_ref[...] = latent_t.astype(jnp.bfloat16)
    first = pl.multiple_of(adapter_of(info, info[1], tokens) * RANK, RANK)
    raised = dot(latent.astype(jnp.bfloat16), up_ref[pl.ds(first, RANK), :])
    q_ref[...] = (base[at, :].astype(jnp.float32) + ADAPTER_SCALE * raised).astype(jnp.bfloat16)


def attention_kernel(n_pre, key_places, value_places, part_rows, tokens, info, masks, *refs):
    q_ref, cot_ref, latt_ref, up_ref, k_own, v_own = refs[:6]
    sources, refs = refs[6:-9], refs[-9:]
    att_ref, sent_ref, kv, q, cot, top, total, acc, grads = refs
    slot_tokens, width = q_ref.shape
    heads = width // HD
    rows = heads * slot_tokens
    tile = min(ROW_TILE, rows)
    scale = 1.0 / math.sqrt(HD)
    factor = scale * LOG2E

    student = info[1] * tokens // CONT
    per_part = part_rows // MB

    def keep(count, live, key_block, value_block):
        @pl.when(live)
        def _():
            at = pl.ds(pl.multiple_of(count * MB, MB), MB)
            kv[at, :HD] = value_block()
            kv[at, HD:] = key_block()

        return count + live.astype(jnp.int32)

    def own_block(b, count):
        at = pl.ds(pl.multiple_of(b * MB, MB), MB)
        return keep(count, masks[0, student, b] > 0, lambda: k_own[at, :], lambda: v_own[at, :])

    def block_of(place, u):
        source, first = place
        return lambda: sources[source][first + u * MB : first + (u + 1) * MB, :]

    count = lax.fori_loop(0, k_own.shape[0] // MB, own_block, jnp.int32(0))
    for i in range(len(key_places)):
        for j in range(1, n_pre):
            for u in range(per_part):
                count = keep(
                    count,
                    masks[j, student, (info[3] ^ i) * per_part + u] > 0,
                    block_of(key_places[i][j - 1], u),
                    block_of(value_places[i][j - 1], u),
                )

    own_tokens = pl.ds(pl.multiple_of(info[2] * slot_tokens, slot_tokens), slot_tokens)
    for h in range(heads):
        at = pl.ds(h * slot_tokens, slot_tokens)
        q[at, :] = q_ref[:, h * HD : (h + 1) * HD]
        cot[at, :] = cot_ref[own_tokens, h * HD : (h + 1) * HD]
    top[...] = jnp.full_like(top, VERY_LOW)
    total[...] = jnp.zeros_like(total)
    acc[...] = jnp.zeros_like(acc)

    def step(first, size):
        both = kv[pl.ds(pl.multiple_of(first, MB), size), :]
        values, keys = both[:, :HD], both[:, HD:]
        lanes = size // HD
        for r0 in range(0, rows, tile):
            at = pl.ds(r0, tile)
            scores = dot_nt(q[at, :], keys)
            old = top[at, :]
            new = jnp.maximum(old, jnp.max(scores, axis=1, keepdims=True))
            top[at, :] = new
            weights = jnp.exp2((scores - jnp.concatenate([new] * lanes, axis=1)) * factor)
            shrink = jnp.exp2((old - new) * factor)
            partial = weights[:, :HD]
            for c in range(1, lanes):
                partial = partial + weights[:, c * HD : (c + 1) * HD]
            total[at, :] = total[at, :] * shrink + partial
            grad_weights = (weights * dot_nt(cot[at, :], values)).astype(jnp.bfloat16)
            first_two = dot(weights.astype(jnp.bfloat16), both)
            last = dot(grad_weights, keys)
            acc[at, :HD] = acc[at, :HD] * shrink + first_two[:, :HD]
            acc[at, HD : 2 * HD] = acc[at, HD : 2 * HD] * shrink + first_two[:, HD:]
            acc[at, 2 * HD :] = acc[at, 2 * HD :] * shrink + last

    per_chunk = CHUNK // MB
    full = count // per_chunk

    def full_step(c, carry):
        step(c * CHUNK, CHUNK)
        return carry

    def rest_step(c, carry):
        step((full * per_chunk + c) * MB, MB)
        return carry

    lax.fori_loop(0, full, full_step, 0)
    lax.fori_loop(0, count - full * per_chunk, rest_step, 0)

    for h in range(heads):
        at = pl.ds(h * slot_tokens, slot_tokens)
        inverse = 1.0 / jnp.sum(total[at, :], axis=1, keepdims=True)
        attended = (acc[at, :HD] * inverse).astype(jnp.bfloat16)
        att_ref[:, h * HD : (h + 1) * HD] = attended
        delta = jnp.sum(
            cot[at, :].astype(jnp.float32) * attended.astype(jnp.float32), axis=1, keepdims=True
        )
        grad = (acc[at, 2 * HD :] - delta * acc[at, HD : 2 * HD]) * (inverse * scale)
        grads[:, h * HD : (h + 1) * HD] = grad.astype(jnp.bfloat16)
    first = pl.multiple_of(adapter_of(info, info[1], tokens) * RANK, RANK)
    query_gradient = grads[...]
    up = up_ref[pl.ds(first, RANK), :]
    sent_ref[:, :width] = (ADAPTER_SCALE * dot(latt_ref[...], query_gradient)).astype(jnp.bfloat16)
    sent_ref[:, width:] = (ADAPTER_SCALE * dot_nt(up, query_gradient)).astype(jnp.bfloat16)


def down_kernel(n_slots, n_row, width, info, *refs):
    parts, hidden, even_ref, odd_ref = refs[:n_slots], refs[n_slots], *refs[n_slots + 1 :]
    depth = even_ref.shape[1] - width
    slot_tokens = parts[0].shape[1] - width
    up = parts[0][:, :width].astype(jnp.float32)
    for part in parts[1:]:
        up = up + part[:, :width].astype(jnp.float32)
    up = up.astype(jnp.bfloat16)
    firsts = [pl.multiple_of((info[2] ^ j) * slot_tokens, slot_tokens) for j in range(n_slots)]
    for i in range(n_row):
        out = odd_ref if i & 1 else even_ref
        rows = slice((i >> 1) * RANK, ((i >> 1) + 1) * RANK)
        cols = pl.ds(pl.multiple_of((info[1] ^ i) * depth, depth), depth)
        grad = jnp.zeros((RANK, depth), jnp.float32)
        for j in range(n_slots):
            grad += dot(parts[j][:, width:], hidden[pl.ds(firsts[j], slot_tokens), cols])
        out[rows, :depth] = grad.astype(jnp.bfloat16)
        out[rows, depth:] = up


def finish_kernel(n_slots, n_row, tokens, info, *refs):
    pairs, refs = refs[: n_row // 2], refs[n_row // 2 :]
    att, refs = refs[:n_slots], refs[n_slots:]
    att_out, down_ref, up_ref, down, sems = refs
    slot_tokens = att[0].shape[0]
    depth = down.shape[1]
    copies = []
    for j in range(n_slots):
        at = pl.multiple_of((info[2] ^ j) * slot_tokens, slot_tokens)
        copies.append(pltpu.make_async_copy(att[j], att_out.at[pl.ds(at, slot_tokens), :], sems.at[j]))
        copies[-1].start()
    down[...] = jnp.zeros_like(down)
    up_ref[...] = jnp.zeros_like(up_ref)
    for i in range(n_row):
        first = pl.multiple_of(adapter_of(info, info[1] ^ i, tokens) * RANK, RANK)
        at = pl.ds(first, RANK)
        part = pairs[i >> 1][(i & 1) * RANK : ((i & 1) + 1) * RANK, :]
        down[at, :] += part[:, :depth].astype(jnp.float32)
        up_ref[at, :] += part[:, depth:].astype(jnp.float32)
    down_ref[...] = down[...].T
    for copy in copies:
        copy.wait()


def shards(
    hidden_in,
    frozen_query_base,
    k_prefix,
    v_prefix,
    tree_mask,
    adapter_ids,
    a_down,
    up_weight_matrix,
    cotangent,
):
    tokens, model = hidden_in.shape
    width = frozen_query_base.shape[1]
    heads = width // HD
    depth, rank_cols = a_down.shape
    local_keys = k_prefix.shape[0]
    n_pre, n_row = lax.axis_size("pre"), lax.axis_size("row")
    n_slots = min(n_pre, tokens // MIN_TOKENS)
    slot_tokens = tokens // n_slots
    pre, row = lax.axis_index("pre"), lax.axis_index("row")
    slices = min(n_row, local_keys // MB)
    drop = (n_row // slices).bit_length() - 1
    part_rows = local_keys // slices
    info = jnp.concatenate([jnp.stack([pre, row, pre % n_slots, row >> drop]), adapter_ids]).astype(jnp.int32)
    bf16, f32 = jnp.bfloat16, jnp.float32

    students, blocks = tree_mask.shape
    pairs, piece_rows = n_row // 2, depth // HD * RANK
    away, even, odd = pl.pallas_call(
        functools.partial(pack_kernel, n_row, tokens),
        out_shape=[
            jax.ShapeDtypeStruct((2 * part_rows + mask_rows(tree_mask), HD), bf16),
            jax.ShapeDtypeStruct((pairs, piece_rows, HD), bf16),
            jax.ShapeDtypeStruct((pairs, piece_rows, HD), bf16),
        ],
        in_specs=[SMEM] + [VMEM] * 4,
        out_specs=[VMEM] * 3,
        scratch_shapes=[pltpu.VMEM((rank_cols, depth), f32)],
        compiler_params=params(16),
        name="pack",
    )(info, k_prefix, v_prefix, tree_mask, a_down)
    planes = [swap(away, "pre", j) for j in range(1, n_pre)]
    odd = swap(odd, "row", 1)
    masks = jnp.stack(
        [tree_mask]
        + [plane[2 * part_rows : 2 * part_rows + students, :blocks].astype(jnp.int32) for plane in planes]
    )

    far = list(range(1, n_row.bit_length() - 1))[::-1]
    half = len(far) // 2
    half_rows = piece_rows // 2
    sources = list(planes)

    def spread(order, offset, column_rows):
        columns = {2 * m: even[m, column_rows] for m in range(pairs)}
        columns |= {2 * m + 1: odd[m, column_rows] for m in range(pairs)}
        held = jnp.concatenate([plane[offset : offset + part_rows] for plane in planes])
        places = {0: [(j, offset) for j in range(n_pre - 1)]}
        parts = {0: held}
        for bit in order + [0]:
            mask, moved = 1 << bit, [i for i in columns if i >> bit & 1 and bit > 0]
            keys = list(parts) if bit >= drop else []
            if not keys and not moved:
                continue
            got = swap(
                jnp.concatenate([parts[m] for m in keys] + [columns[i] for i in moved]), "row", mask
            )
            sources.append(got)
            at = 0
            for m in keys:
                parts[m | mask] = got[at : at + held.shape[0]]
                places[m | mask] = [
                    (len(sources) - 1, at + j * part_rows) for j in range(n_pre - 1)
                ]
                at += held.shape[0]
            for i in moved:
                columns[i] = got[at : at + half_rows]
                at += half_rows
        columns = jnp.concatenate([columns[i] for i in range(n_row)])
        return columns, [places[i << drop] for i in range(slices)]

    low, key_places = spread(far, 0, slice(0, half_rows))
    high, value_places = spread(far[half:] + far[:half], part_rows, slice(half_rows, None))

    queries, latent_t = pl.pallas_call(
        functools.partial(query_kernel, n_row, tokens),
        out_shape=[
            jax.ShapeDtypeStruct((slot_tokens, width), bf16),
            jax.ShapeDtypeStruct((RANK, slot_tokens), bf16),
        ],
        in_specs=[SMEM] + [VMEM] * 5,
        out_specs=[VMEM] * 2,
        compiler_params=params(16),
        name="queries",
    )(info, hidden_in, frozen_query_base, up_weight_matrix, low, high)

    rows = heads * slot_tokens
    keys_bytes = local_keys * n_pre * HD * 2
    attended, sent = pl.pallas_call(
        functools.partial(attention_kernel, n_pre, key_places, value_places, part_rows, tokens),
        out_shape=[
            jax.ShapeDtypeStruct((slot_tokens, width), bf16),
            jax.ShapeDtypeStruct((RANK, width + slot_tokens), bf16),
        ],
        in_specs=[SMEM] * 2 + [VMEM] * (6 + len(sources)),
        out_specs=[VMEM] * 2,
        scratch_shapes=[
            pltpu.VMEM((local_keys * n_pre, 2 * HD), bf16),
            pltpu.VMEM((rows, HD), bf16),
            pltpu.VMEM((rows, HD), bf16),
            pltpu.VMEM((rows, HD), f32),
            pltpu.VMEM((rows, HD), f32),
            pltpu.VMEM((rows, 3 * HD), f32),
            pltpu.VMEM((slot_tokens, width), bf16),
        ],
        compiler_params=params(16 + 4 * keys_bytes // MIB),
        name="attention",
    )(
        info,
        masks,
        queries,
        cotangent,
        latent_t,
        up_weight_matrix,
        k_prefix,
        v_prefix,
        *sources,
    )

    shared = [swap(sent, "pre", j) for j in range(n_slots)]
    attended_parts = [swap(attended, "pre", j) for j in range(n_slots)]

    even, odd = pl.pallas_call(
        functools.partial(down_kernel, n_slots, n_row, width),
        out_shape=[jax.ShapeDtypeStruct((pairs * RANK, depth + width), bf16)] * 2,
        in_specs=[SMEM] + [VMEM] * (n_slots + 1),
        out_specs=[VMEM] * 2,
        compiler_params=params(16),
        name="down",
    )(info, *shared, hidden_in)
    odd = swap(odd, "row", 1)
    pieces = [
        swap(jnp.concatenate([x[m * RANK : (m + 1) * RANK] for x in (even, odd)]), "row", 2 * m)
        for m in range(pairs)
    ]

    return pl.pallas_call(
        functools.partial(finish_kernel, n_slots, n_row, tokens),
        out_shape=[
            jax.ShapeDtypeStruct((tokens, width), bf16),
            jax.ShapeDtypeStruct((depth, rank_cols), f32),
            jax.ShapeDtypeStruct((rank_cols, width), f32),
        ],
        in_specs=[SMEM] + [VMEM] * (pairs + n_slots),
        out_specs=[ANY, VMEM, VMEM],
        scratch_shapes=[
            pltpu.VMEM((rank_cols, depth), f32),
            pltpu.SemaphoreType.DMA((n_slots,)),
        ],
        compiler_params=params(16),
        name="finish",
    )(info, *pieces, *attended_parts)


def solution(mesh):
    in_specs = (
        P("row", None),
        P("row", None),
        P("pre", None),
        P("pre", None),
        P(None, "pre"),
        P(),
        P("row", None),
        P(),
        P("row", None),
    )
    out_specs = (P("row", None), P("row", None), P())
    return jax.shard_map(shards, mesh=mesh, in_specs=in_specs, out_specs=out_specs, check_vma=False)
```

```python
import functools
import math

import jax
import jax.numpy as jnp
from jax import lax
from jax.experimental import pallas as pl
from jax.experimental.pallas import tpu as pltpu
from jax.sharding import PartitionSpec as P

HD = 128
RANK = 16
CONT = 512
MB = 128
CHUNK = 512
ROW_TILE = 256
MIN_TOKENS = 16
ADAPTER_SCALE = 2.0
VERY_LOW = -1e30
LOG2E = 1.4426950408889634
MIB = 1 << 20

NT = (((1,), (1,)), ((), ()))
VMEM = pl.BlockSpec(memory_space=pltpu.VMEM)
SMEM = pl.BlockSpec(memory_space=pltpu.SMEM)
HBM = pl.BlockSpec(memory_space=pltpu.HBM)


def dot(a, b):
    return jnp.dot(a, b, preferred_element_type=jnp.float32)


def dot_nt(a, b):
    return lax.dot_general(a, b, NT, preferred_element_type=jnp.float32)


def swap(x, axis, mask):
    if mask == 0:
        return x
    return lax.ppermute(x, axis, [(s, s ^ mask) for s in range(lax.axis_size(axis))])


def params(mib):
    return pltpu.CompilerParams(vmem_limit_bytes=mib * MIB)


def adapter_of(ids, row, tokens):
    return pl.multiple_of(ids[row * tokens // CONT] * RANK, RANK)


def slot_of(slot_tokens, n_slots, offset=0):
    slot = lax.rem(lax.axis_index("pre"), n_slots) ^ offset
    return pl.ds(pl.multiple_of(slot * slot_tokens, slot_tokens), slot_tokens)


def fetch(pairs, sems):
    copies = [pltpu.make_async_copy(src, dst, sems.at[i]) for i, (src, dst) in enumerate(pairs)]
    for copy in copies:
        copy.start()
    return copies


def mask_rows(mask):
    return -(-mask.shape[0] // 16) * 16


def away_kernel(drop, part_rows, k_ref, v_ref, mask_ref, out_ref, mask_in, sems):
    half = part_rows // 2
    begin = (lax.axis_index("row") >> drop) * part_rows
    pairs = [(mask_ref, mask_in)]
    for a in range(2):
        at = pl.ds(pl.multiple_of(begin + a * half, half), half)
        pairs.append((k_ref.at[at, :], out_ref.at[pl.ds(2 * a * half, half), :]))
        pairs.append((v_ref.at[at, :], out_ref.at[pl.ds((2 * a + 1) * half, half), :]))
    copies = fetch(pairs, sems)
    students, blocks = mask_in.shape
    copies[0].wait()
    out_ref[2 * part_rows :, :] = jnp.zeros_like(out_ref[2 * part_rows :, :])
    out_ref[2 * part_rows : 2 * part_rows + students, :blocks] = mask_in[...].astype(jnp.bfloat16)
    for copy in copies[1:]:
        copy.wait()


def pick_kernel(n_row, tokens, ids, a_ref, even_ref, odd_ref, at):
    row = lax.axis_index("row")
    at[...] = a_ref[...].astype(jnp.float32).T
    for i in range(n_row):
        out = odd_ref if i & 1 else even_ref
        piece = at[pl.ds(adapter_of(ids, row ^ i, tokens), RANK), :]
        out[(i >> 1) * RANK : ((i >> 1) + 1) * RANK, :] = piece.astype(jnp.bfloat16)


def query_kernel(n_row, n_slots, tokens, ids, hidden, base, up_ref, *refs):
    pairs = refs[: n_row // 2]
    q_ref, latt_ref, hid, frozen, sems = refs[n_row // 2 :]
    row = lax.axis_index("row")
    slot_tokens = q_ref.shape[0]
    depth = pairs[0].shape[1]
    own = slot_of(slot_tokens, n_slots)
    copies = fetch([(hidden.at[own, :], hid), (base.at[own, :], frozen)], sems)
    latent = jnp.zeros((slot_tokens, RANK), jnp.float32)
    latent_t = jnp.zeros((RANK, slot_tokens), jnp.float32)
    copies[0].wait()
    for i in range(n_row):
        piece = pairs[i >> 1][(i & 1) * RANK : ((i & 1) + 1) * RANK, :]
        block = hid[:, pl.ds(pl.multiple_of((row ^ i) * depth, depth), depth)]
        latent += dot_nt(block, piece)
        latent_t += dot_nt(piece, block)
    latt_ref[...] = latent_t.astype(jnp.bfloat16)
    up = up_ref[pl.ds(adapter_of(ids, row, tokens), RANK), :]
    raised = dot(latent.astype(jnp.bfloat16), up)
    copies[1].wait()
    q_ref[...] = (frozen[...].astype(jnp.float32) + ADAPTER_SCALE * raised).astype(jnp.bfloat16)


def attention_kernel(n_pre, n_slots, drop, part_rows, places, tokens, ids, masks, *refs):
    q_ref, cot_hbm, latt_ref, up_ref, k_own, v_own = refs[:6]
    sources, refs = refs[6:-11], refs[-11:]
    att_ref, sent_ref, kv, q, cot, top, total, acc, grads, cot_in, sems = refs
    row = lax.axis_index("row")
    slot_tokens, width = q_ref.shape
    heads = width // HD
    rows = heads * slot_tokens
    tile = min(ROW_TILE, rows)
    scale = 1.0 / math.sqrt(HD)
    factor = scale * LOG2E

    (copy,) = fetch([(cot_hbm.at[slot_of(slot_tokens, n_slots), :], cot_in)], sems)
    student = row * tokens // CONT
    half = part_rows // 2
    unit = min(MB, half)

    def keep(count, live, key_block, value_block):
        @pl.when(live)
        def _():
            at = pl.ds(pl.multiple_of(count * unit, unit), unit)
            kv[at, :HD] = value_block()
            kv[at, HD:] = key_block()

        return count + live.astype(jnp.int32)

    def own_block(b, count):
        at = pl.ds(pl.multiple_of(b * unit, unit), unit)
        live = masks[0, student, b * unit // MB] > 0
        return keep(count, live, lambda: k_own[at, :], lambda: v_own[at, :])

    def block_of(source, first):
        return lambda: sources[source][first : first + unit, :]

    count = lax.fori_loop(0, k_own.shape[0] // unit, own_block, jnp.int32(0))
    for a in range(2):
        for i, place in enumerate(places[a]):
            piece = (row >> drop) ^ i
            for j in range(1, n_pre):
                source, first = place[j - 1]
                for u in range(half // unit):
                    block = (piece * part_rows + a * half + u * unit) // MB
                    count = keep(
                        count,
                        masks[j, student, block] > 0,
                        block_of(source, first + u * unit),
                        block_of(source, first + half + u * unit),
                    )

    copy.wait()
    for h in range(heads):
        at = pl.ds(h * slot_tokens, slot_tokens)
        q[at, :] = q_ref[:, h * HD : (h + 1) * HD]
        cot[at, :] = cot_in[:, h * HD : (h + 1) * HD]
    top[...] = jnp.full_like(top, VERY_LOW)
    total[...] = jnp.zeros_like(total)
    acc[...] = jnp.zeros_like(acc)

    def step(first, size):
        both = kv[pl.ds(pl.multiple_of(first, unit), size), :]
        values, keys = both[:, :HD], both[:, HD:]
        lane = min(size, HD)
        lanes = size // lane
        for r0 in range(0, rows, tile):
            at = pl.ds(r0, tile)
            scores = dot_nt(q[at, :], keys)
            old = top[at, :]
            new = jnp.maximum(old, jnp.max(scores, axis=1, keepdims=True))
            top[at, :] = new
            weights = jnp.exp2((scores - jnp.concatenate([new[:, :lane]] * lanes, axis=1)) * factor)
            shrink = jnp.exp2((old - new) * factor)
            partial = weights[:, :lane]
            for c in range(1, lanes):
                partial = partial + weights[:, c * lane : (c + 1) * lane]
            total[at, :] *= shrink
            total[at, :lane] += partial
            grad_weights = (weights * dot_nt(cot[at, :], values)).astype(jnp.bfloat16)
            first_two = dot(weights.astype(jnp.bfloat16), both)
            last = dot(grad_weights, keys)
            acc[at, :HD] = acc[at, :HD] * shrink + first_two[:, :HD]
            acc[at, HD : 2 * HD] = acc[at, HD : 2 * HD] * shrink + first_two[:, HD:]
            acc[at, 2 * HD :] = acc[at, 2 * HD :] * shrink + last

    per_chunk = CHUNK // unit
    full = count // per_chunk

    def full_step(c, carry):
        step(c * CHUNK, CHUNK)
        return carry

    def rest_step(c, carry):
        step((full * per_chunk + c) * unit, unit)
        return carry

    lax.fori_loop(0, full, full_step, 0)
    lax.fori_loop(0, count - full * per_chunk, rest_step, 0)

    for h in range(heads):
        at = pl.ds(h * slot_tokens, slot_tokens)
        inverse = 1.0 / jnp.sum(total[at, :], axis=1, keepdims=True)
        attended = (acc[at, :HD] * inverse).astype(jnp.bfloat16)
        att_ref[:, h * HD : (h + 1) * HD] = attended
        delta = jnp.sum(
            cot[at, :].astype(jnp.float32) * attended.astype(jnp.float32), axis=1, keepdims=True
        )
        grad = (acc[at, 2 * HD :] - delta * acc[at, HD : 2 * HD]) * (inverse * scale)
        grads[:, h * HD : (h + 1) * HD] = grad.astype(jnp.bfloat16)
    query_gradient = grads[...]
    up = up_ref[pl.ds(adapter_of(ids, row, tokens), RANK), :]
    sent_ref[:, :width] = (ADAPTER_SCALE * dot(latt_ref[...], query_gradient)).astype(jnp.bfloat16)
    sent_ref[:, width:] = (ADAPTER_SCALE * dot_nt(up, query_gradient)).astype(jnp.bfloat16)


def down_kernel(n_slots, n_row, width, *refs):
    parts, hidden, even_ref, odd_ref = refs[:n_slots], refs[n_slots], *refs[n_slots + 1 :]
    row = lax.axis_index("row")
    depth = even_ref.shape[1] - width
    slot_tokens = parts[0].shape[1] - width
    up = parts[0][:, :width].astype(jnp.float32)
    for part in parts[1:]:
        up = up + part[:, :width].astype(jnp.float32)
    up = up.astype(jnp.bfloat16)
    slots = [slot_of(slot_tokens, n_slots, j) for j in range(n_slots)]
    for i in range(n_row):
        out = odd_ref if i & 1 else even_ref
        rows = slice((i >> 1) * RANK, ((i >> 1) + 1) * RANK)
        cols = pl.ds(pl.multiple_of((row ^ i) * depth, depth), depth)
        grad = jnp.zeros((RANK, depth), jnp.float32)
        for j in range(n_slots):
            grad += dot(parts[j][:, width:], hidden[slots[j], cols])
        out[rows, :depth] = grad.astype(jnp.bfloat16)
        out[rows, depth:] = up


def finish_kernel(n_row, tokens, ids, *refs):
    pairs, (down_ref, up_ref, down) = refs[: n_row // 2], refs[n_row // 2 :]
    row = lax.axis_index("row")
    depth = down.shape[1]
    down[...] = jnp.zeros_like(down)
    up_ref[...] = jnp.zeros_like(up_ref)
    for i in range(n_row):
        at = pl.ds(adapter_of(ids, row ^ i, tokens), RANK)
        part = pairs[i >> 1][(i & 1) * RANK : ((i & 1) + 1) * RANK, :]
        down[at, :] += part[:, :depth].astype(jnp.float32)
        up_ref[at, :] += part[:, depth:].astype(jnp.float32)
    down_ref[...] = down[...].T


def exchange_pieces(even, odd):
    odd = swap(odd, "row", 1)
    rows = [slice(m * RANK, (m + 1) * RANK) for m in range(even.shape[0] // RANK)]
    return [swap(jnp.concatenate([even[at], odd[at]]), "row", 2 * m) for m, at in enumerate(rows)]


def shards(
    hidden_in,
    frozen_query_base,
    k_prefix,
    v_prefix,
    tree_mask,
    adapter_ids,
    a_down,
    up_weight_matrix,
    cotangent,
):
    tokens, model = hidden_in.shape
    width = frozen_query_base.shape[1]
    heads = width // HD
    depth, rank_cols = a_down.shape
    local_keys = k_prefix.shape[0]
    n_pre, n_row = lax.axis_size("pre"), lax.axis_size("row")
    n_slots = min(n_pre, tokens // MIN_TOKENS)
    slot_tokens = tokens // n_slots
    bf16, f32 = jnp.bfloat16, jnp.float32
    pairs = n_row // 2

    slices = min(n_row, local_keys // MB)
    drop = (n_row // slices).bit_length() - 1
    part_rows = local_keys // slices
    students, blocks = tree_mask.shape
    away = pl.pallas_call(
        functools.partial(away_kernel, drop, part_rows),
        out_shape=jax.ShapeDtypeStruct((2 * part_rows + mask_rows(tree_mask), HD), bf16),
        in_specs=[HBM] * 3,
        out_specs=VMEM,
        scratch_shapes=[pltpu.VMEM((students, blocks), jnp.int32), pltpu.SemaphoreType.DMA((5,))],
        compiler_params=params(16),
        name="away",
    )(k_prefix, v_prefix, tree_mask)
    planes = [swap(away, "pre", j) for j in range(1, n_pre)]
    masks = jnp.stack(
        [tree_mask]
        + [plane[2 * part_rows : 2 * part_rows + students, :blocks].astype(jnp.int32) for plane in planes]
    )

    even, odd = pl.pallas_call(
        functools.partial(pick_kernel, n_row, tokens),
        out_shape=[jax.ShapeDtypeStruct((pairs * RANK, depth), bf16)] * 2,
        in_specs=[SMEM, VMEM],
        out_specs=[VMEM] * 2,
        scratch_shapes=[pltpu.VMEM((rank_cols, depth), f32)],
        compiler_params=params(16),
        name="pick",
    )(adapter_ids, a_down)
    columns = exchange_pieces(even, odd)

    far = list(range(max(drop, 1), n_row.bit_length() - 1))[::-1]
    turn = len(far) // 2
    core = [0] if drop == 0 else []
    sources = list(planes)

    def spread(order, offset):
        held = jnp.concatenate([plane[offset : offset + part_rows] for plane in planes])
        places = {0: [(j, offset) for j in range(n_pre - 1)]}
        parts = {0: held}
        for bit in order:
            mask, keys = 1 << bit, list(parts)
            got = swap(jnp.concatenate([parts[m] for m in keys]), "row", mask)
            sources.append(got)
            for k, m in enumerate(keys):
                at = k * held.shape[0]
                parts[m | mask] = got[at : at + held.shape[0]]
                places[m | mask] = [(len(sources) - 1, at + j * part_rows) for j in range(n_pre - 1)]
        return [places[i << drop] for i in range(slices)]

    places = [spread(far + core, 0), spread(far[turn:] + far[:turn] + core, part_rows)]

    queries, latent_t = pl.pallas_call(
        functools.partial(query_kernel, n_row, n_slots, tokens),
        out_shape=[
            jax.ShapeDtypeStruct((slot_tokens, width), bf16),
            jax.ShapeDtypeStruct((RANK, slot_tokens), bf16),
        ],
        in_specs=[SMEM, HBM, HBM, VMEM] + [VMEM] * pairs,
        out_specs=[VMEM] * 2,
        scratch_shapes=[
            pltpu.VMEM((slot_tokens, model), bf16),
            pltpu.VMEM((slot_tokens, width), bf16),
            pltpu.SemaphoreType.DMA((2,)),
        ],
        compiler_params=params(16),
        name="queries",
    )(adapter_ids, hidden_in, frozen_query_base, up_weight_matrix, *columns)

    rows = heads * slot_tokens
    keys_bytes = local_keys * n_pre * HD * 2
    attended, sent = pl.pallas_call(
        functools.partial(attention_kernel, n_pre, n_slots, drop, part_rows, places, tokens),
        out_shape=[
            jax.ShapeDtypeStruct((slot_tokens, width), bf16),
            jax.ShapeDtypeStruct((RANK, width + slot_tokens), bf16),
        ],
        in_specs=[SMEM, SMEM, VMEM, HBM] + [VMEM] * (4 + len(sources)),
        out_specs=[VMEM] * 2,
        scratch_shapes=[
            pltpu.VMEM((local_keys * n_pre, 2 * HD), bf16),
            pltpu.VMEM((rows, HD), bf16),
            pltpu.VMEM((rows, HD), bf16),
            pltpu.VMEM((rows, HD), f32),
            pltpu.VMEM((rows, HD), f32),
            pltpu.VMEM((rows, 3 * HD), f32),
            pltpu.VMEM((slot_tokens, width), bf16),
            pltpu.VMEM((slot_tokens, width), bf16),
            pltpu.SemaphoreType.DMA((1,)),
        ],
        compiler_params=params(16 + 4 * keys_bytes // MIB),
        name="attention",
    )(
        adapter_ids,
        masks,
        queries,
        cotangent,
        latent_t,
        up_weight_matrix,
        k_prefix,
        v_prefix,
        *sources,
    )

    shared = [swap(sent, "pre", j) for j in range(n_slots)]
    attended = lax.all_gather(attended, "pre", axis=0, tiled=True)[:tokens]

    even, odd = pl.pallas_call(
        functools.partial(down_kernel, n_slots, n_row, width),
        out_shape=[jax.ShapeDtypeStruct((pairs * RANK, depth + width), bf16)] * 2,
        in_specs=[VMEM] * (n_slots + 1),
        out_specs=[VMEM] * 2,
        compiler_params=params(16),
        name="down",
    )(*shared, hidden_in)
    pieces = exchange_pieces(even, odd)

    grad_a, up_weight_gradient = pl.pallas_call(
        functools.partial(finish_kernel, n_row, tokens),
        out_shape=[
            jax.ShapeDtypeStruct((depth, rank_cols), f32),
            jax.ShapeDtypeStruct((rank_cols, width), f32),
        ],
        in_specs=[SMEM] + [VMEM] * pairs,
        out_specs=[VMEM] * 2,
        scratch_shapes=[pltpu.VMEM((rank_cols, depth), f32)],
        compiler_params=params(16),
        name="finish",
    )(adapter_ids, *pieces)
    return attended, grad_a, up_weight_gradient


def solution(mesh):
    in_specs = (
        P("row", None),
        P("row", None),
        P("pre", None),
        P("pre", None),
        P(None, "pre"),
        P(),
        P("row", None),
        P(),
        P("row", None),
    )
    out_specs = (P("row", None), P("row", None), P())
    return jax.shard_map(shards, mesh=mesh, in_specs=in_specs, out_specs=out_specs, check_vma=False)
```

```python
import functools
import math

import jax
import jax.numpy as jnp
from jax import lax
from jax.experimental import pallas as pl
from jax.experimental.pallas import tpu as pltpu
from jax.sharding import PartitionSpec as P

HD = 128
RANK = 16
CONT = 512
MB = 128
CHUNK = 512
ROW_TILE = 256
MIN_TOKENS = 16
ADAPTER_SCALE = 2.0
VERY_LOW = -1e30
LOG2E = 1.4426950408889634
MIB = 1 << 20

NT = (((1,), (1,)), ((), ()))
VMEM = pl.BlockSpec(memory_space=pltpu.VMEM)
SMEM = pl.BlockSpec(memory_space=pltpu.SMEM)
HBM = pl.BlockSpec(memory_space=pltpu.HBM)


def dot(a, b):
    return jnp.dot(a, b, preferred_element_type=jnp.float32)


def dot_nt(a, b):
    return lax.dot_general(a, b, NT, preferred_element_type=jnp.float32)


def swap(x, axis, mask):
    if mask == 0:
        return x
    return lax.ppermute(x, axis, [(s, s ^ mask) for s in range(lax.axis_size(axis))])


def params(mib):
    return pltpu.CompilerParams(vmem_limit_bytes=mib * MIB)


def adapter_of(ids, row, tokens):
    return pl.multiple_of(ids[row * tokens // CONT] * RANK, RANK)


def slot_of(slot_tokens, n_slots, offset=0):
    slot = lax.rem(lax.axis_index("pre"), n_slots) ^ offset
    return pl.ds(pl.multiple_of(slot * slot_tokens, slot_tokens), slot_tokens)


def fetch(pairs, sems):
    copies = [pltpu.make_async_copy(src, dst, sems.at[i]) for i, (src, dst) in enumerate(pairs)]
    for copy in copies:
        copy.start()
    return copies


def mask_rows(mask):
    return -(-mask.shape[0] // 16) * 16


def prep_kernel(n_row, n_slots, drop, part_rows, tokens, *refs):
    k_ref, v_ref, mask_ref, ids_ref, a_ref, hidden, base, cot, up = refs[:9]
    away_ref, slots_ref, hid_ref, base_ref, cot_ref, up_out = refs[9:15]
    mask_in, ids, a_in, at, sems = refs[15:]
    row = lax.axis_index("row")
    half = part_rows // 2
    begin = (row >> drop) * part_rows
    pairs = [(ids_ref, ids), (a_ref, a_in), (mask_ref, mask_in)]
    for a in range(2):
        span = pl.ds(pl.multiple_of(begin + a * half, half), half)
        pairs.append((k_ref.at[span, :], away_ref.at[pl.ds(2 * a * half, half), :]))
        pairs.append((v_ref.at[span, :], away_ref.at[pl.ds((2 * a + 1) * half, half), :]))
    own = slot_of(base_ref.shape[0], n_slots)
    pairs += [(base.at[own, :], base_ref), (cot.at[own, :], cot_ref), (up, up_out), (hidden.at[own, :], hid_ref)]
    copies = fetch(pairs, sems)
    copies[1].wait()
    at[...] = a_in[...].astype(jnp.float32).T
    copies[0].wait()
    for i in range(n_row):
        piece = at[pl.ds(adapter_of(ids, row ^ i, tokens), RANK), :]
        slots_ref[i * RANK : (i + 1) * RANK, :] = piece.astype(jnp.bfloat16)
    students, blocks = mask_in.shape
    copies[2].wait()
    away_ref[2 * part_rows :, :] = jnp.zeros_like(away_ref[2 * part_rows :, :])
    away_ref[2 * part_rows : 2 * part_rows + students, :blocks] = mask_in[...].astype(jnp.bfloat16)
    for copy in copies[3:]:
        copy.wait()


def query_kernel(n_row, tokens, ids, hid, base, up_ref, columns, q_ref, latt_ref):
    row = lax.axis_index("row")
    slot_tokens = q_ref.shape[0]
    depth = columns.shape[1]
    latent = jnp.zeros((slot_tokens, RANK), jnp.float32)
    latent_t = jnp.zeros((RANK, slot_tokens), jnp.float32)
    for i in range(n_row):
        piece = columns[i * RANK : (i + 1) * RANK, :]
        block = hid[:, pl.ds(pl.multiple_of((row ^ i) * depth, depth), depth)]
        latent += dot_nt(block, piece)
        latent_t += dot_nt(piece, block)
    latt_ref[...] = latent_t.astype(jnp.bfloat16)
    up = up_ref[pl.ds(adapter_of(ids, row, tokens), RANK), :]
    raised = dot(latent.astype(jnp.bfloat16), up)
    q_ref[...] = (base[...].astype(jnp.float32) + ADAPTER_SCALE * raised).astype(jnp.bfloat16)


def attention_kernel(n_pre, drop, part_rows, places, n_sources, last, tokens, *refs):
    if last:
        ids, masks, q_ref, cot_ref, latt_ref, up_ref, top_in, total_in, acc_in = refs[:9]
        sources, refs = refs[9 : 9 + n_sources], refs[9 + n_sources :]
        att_ref, sent_ref, kv, q, cot, top, total, acc, grads = refs
    else:
        masks, q_ref, cot_ref, k_own, v_own = refs[:5]
        sources, refs = refs[5 : 5 + n_sources], refs[5 + n_sources :]
        top, total, acc, kv, q, cot = refs
    row = lax.axis_index("row")
    slot_tokens, width = q_ref.shape
    heads = width // HD
    rows = heads * slot_tokens
    tile = min(ROW_TILE, rows)
    scale = 1.0 / math.sqrt(HD)
    factor = scale * LOG2E

    student = row * tokens // CONT
    half = part_rows // 2
    unit = min(MB, half)

    def keep(count, live, key_block, value_block):
        @pl.when(live)
        def _():
            at = pl.ds(pl.multiple_of(count * unit, unit), unit)
            kv[at, :HD] = value_block()
            kv[at, HD:] = key_block()

        return count + live.astype(jnp.int32)

    def own_block(b, count):
        at = pl.ds(pl.multiple_of(b * unit, unit), unit)
        live = masks[0, student, b * unit // MB] > 0
        return keep(count, live, lambda: k_own[at, :], lambda: v_own[at, :])

    def block_of(source, first):
        return lambda: sources[source][first : first + unit, :]

    count = jnp.int32(0)
    if not last:
        count = lax.fori_loop(0, k_own.shape[0] // unit, own_block, count)
    for a, i, place in places:
        piece = (row >> drop) ^ i
        for j in range(1, n_pre):
            source, first = place[j - 1]
            for u in range(half // unit):
                block = (piece * part_rows + a * half + u * unit) // MB
                count = keep(
                    count,
                    masks[j, student, block] > 0,
                    block_of(source, first + u * unit),
                    block_of(source, first + half + u * unit),
                )

    for h in range(heads):
        at = pl.ds(h * slot_tokens, slot_tokens)
        q[at, :] = q_ref[:, h * HD : (h + 1) * HD]
        cot[at, :] = cot_ref[:, h * HD : (h + 1) * HD]
    if last:
        top[...] = top_in[...]
        total[...] = total_in[...]
        acc[...] = acc_in[...]
    else:
        top[...] = jnp.full_like(top, VERY_LOW)
        total[...] = jnp.zeros_like(total)
        acc[...] = jnp.zeros_like(acc)

    def step(first, size):
        both = kv[pl.ds(pl.multiple_of(first, unit), size), :]
        values, keys = both[:, :HD], both[:, HD:]
        lane = min(size, HD)
        lanes = size // lane
        for r0 in range(0, rows, tile):
            at = pl.ds(r0, tile)
            scores = dot_nt(q[at, :], keys)
            old = top[at, :]
            new = jnp.maximum(old, jnp.max(scores, axis=1, keepdims=True))
            top[at, :] = new
            weights = jnp.exp2((scores - jnp.concatenate([new[:, :lane]] * lanes, axis=1)) * factor)
            shrink = jnp.exp2((old - new) * factor)
            partial = weights[:, :lane]
            for c in range(1, lanes):
                partial = partial + weights[:, c * lane : (c + 1) * lane]
            total[at, :] *= shrink
            total[at, :lane] += partial
            grad_weights = (weights * dot_nt(cot[at, :], values)).astype(jnp.bfloat16)
            first_two = dot(weights.astype(jnp.bfloat16), both)
            last = dot(grad_weights, keys)
            acc[at, :HD] = acc[at, :HD] * shrink + first_two[:, :HD]
            acc[at, HD : 2 * HD] = acc[at, HD : 2 * HD] * shrink + first_two[:, HD:]
            acc[at, 2 * HD :] = acc[at, 2 * HD :] * shrink + last

    per_chunk = CHUNK // unit
    full = count // per_chunk

    def full_step(c, carry):
        step(c * CHUNK, CHUNK)
        return carry

    lax.fori_loop(0, full, full_step, 0)
    size = CHUNK // 2
    while size >= unit:
        done = count // (2 * size // unit) * (2 * size)
        pl.when((count * unit - done) >= size)(functools.partial(step, done, size))
        size //= 2
    if not last:
        return

    for h in range(heads):
        at = pl.ds(h * slot_tokens, slot_tokens)
        inverse = 1.0 / jnp.sum(total[at, :], axis=1, keepdims=True)
        attended = (acc[at, :HD] * inverse).astype(jnp.bfloat16)
        att_ref[:, h * HD : (h + 1) * HD] = attended
        delta = jnp.sum(
            cot[at, :].astype(jnp.float32) * attended.astype(jnp.float32), axis=1, keepdims=True
        )
        grad = (acc[at, 2 * HD :] - delta * acc[at, HD : 2 * HD]) * (inverse * scale)
        grads[:, h * HD : (h + 1) * HD] = grad.astype(jnp.bfloat16)
    query_gradient = grads[...]
    up = up_ref[pl.ds(adapter_of(ids, row, tokens), RANK), :]
    sent_ref[:, :width] = (ADAPTER_SCALE * dot(latt_ref[...], query_gradient)).astype(jnp.bfloat16)
    sent_ref[:, width:] = (ADAPTER_SCALE * dot_nt(up, query_gradient)).astype(jnp.bfloat16)


def down_kernel(n_slots, n_row, width, *refs):
    parts, hidden, even_ref, odd_ref = refs[:n_slots], refs[n_slots], *refs[n_slots + 1 :]
    row = lax.axis_index("row")
    depth = even_ref.shape[1] - width
    slot_tokens = parts[0].shape[1] - width
    up = parts[0][:, :width].astype(jnp.float32)
    for part in parts[1:]:
        up = up + part[:, :width].astype(jnp.float32)
    up = up.astype(jnp.bfloat16)
    slots = [slot_of(slot_tokens, n_slots, j) for j in range(n_slots)]
    for i in range(n_row):
        out = odd_ref if i & 1 else even_ref
        rows = slice((i >> 1) * RANK, ((i >> 1) + 1) * RANK)
        cols = pl.ds(pl.multiple_of((row ^ i) * depth, depth), depth)
        grad = jnp.zeros((RANK, depth), jnp.float32)
        for j in range(n_slots):
            grad += dot(parts[j][:, width:], hidden[slots[j], cols])
        out[rows, :depth] = grad.astype(jnp.bfloat16)
        out[rows, depth:] = up


def finish_kernel(n_slots, n_row, tokens, ids, *refs):
    pairs, att, refs = refs[: n_row // 2], refs[n_row // 2 : n_row // 2 + n_slots], refs[n_row // 2 + n_slots :]
    att_out, down_ref, up_ref, down, sems = refs
    row = lax.axis_index("row")
    depth = down.shape[1]
    slot_tokens = att[0].shape[0]
    copies = fetch(
        [(att[j], att_out.at[slot_of(slot_tokens, n_slots, j), :]) for j in range(n_slots)], sems
    )
    down[...] = jnp.zeros_like(down)
    up_ref[...] = jnp.zeros_like(up_ref)
    for i in range(n_row):
        at = pl.ds(adapter_of(ids, row ^ i, tokens), RANK)
        part = pairs[i >> 1][(i & 1) * RANK : ((i & 1) + 1) * RANK, :]
        down[at, :] += part[:, :depth].astype(jnp.float32)
        up_ref[at, :] += part[:, depth:].astype(jnp.float32)
    down_ref[...] = down[...].T
    for copy in copies:
        copy.wait()


def shards(
    hidden_in,
    frozen_query_base,
    k_prefix,
    v_prefix,
    tree_mask,
    adapter_ids,
    a_down,
    up_weight_matrix,
    cotangent,
):
    tokens, model = hidden_in.shape
    width = frozen_query_base.shape[1]
    heads = width // HD
    depth, rank_cols = a_down.shape
    local_keys = k_prefix.shape[0]
    n_pre, n_row = lax.axis_size("pre"), lax.axis_size("row")
    n_slots = min(n_pre, tokens // MIN_TOKENS)
    slot_tokens = tokens // n_slots
    bf16, f32 = jnp.bfloat16, jnp.float32
    slices = min(n_row, local_keys // MB)
    drop = (n_row // slices).bit_length() - 1
    part_rows = local_keys // slices
    students, blocks = tree_mask.shape

    away, slots, hid, base, cot, up = pl.pallas_call(
        functools.partial(prep_kernel, n_row, n_slots, drop, part_rows, tokens),
        out_shape=[
            jax.ShapeDtypeStruct((2 * part_rows + mask_rows(tree_mask), HD), bf16),
            jax.ShapeDtypeStruct((n_row * RANK, depth), bf16),
            jax.ShapeDtypeStruct((slot_tokens, model), bf16),
            jax.ShapeDtypeStruct((slot_tokens, width), bf16),
            jax.ShapeDtypeStruct((slot_tokens, width), bf16),
            jax.ShapeDtypeStruct(up_weight_matrix.shape, bf16),
        ],
        in_specs=[HBM] * 9,
        out_specs=[VMEM] * 6,
        scratch_shapes=[
            pltpu.VMEM((students, blocks), jnp.int32),
            pltpu.SMEM(adapter_ids.shape, jnp.int32),
            pltpu.VMEM((depth, rank_cols), bf16),
            pltpu.VMEM((rank_cols, depth), f32),
            pltpu.SemaphoreType.DMA((11,)),
        ],
        compiler_params=params(56),
        name="prep",
    )(
        k_prefix,
        v_prefix,
        tree_mask,
        adapter_ids,
        a_down,
        hidden_in,
        frozen_query_base,
        cotangent,
        up_weight_matrix,
    )
    planes = [swap(away, "pre", j) for j in range(1, n_pre)]
    masks = jnp.stack(
        [tree_mask]
        + [plane[2 * part_rows : 2 * part_rows + students, :blocks].astype(jnp.int32) for plane in planes]
    )

    columns = [slots[i * RANK : (i + 1) * RANK] for i in range(n_row)]
    for bit in range(n_row.bit_length() - 1):
        moved = [i for i in range(n_row) if i >> bit & 1]
        got = swap(jnp.concatenate([columns[i] for i in moved]), "row", 1 << bit)
        for k, i in enumerate(moved):
            columns[i] = got[k * RANK : (k + 1) * RANK]
    queries, latent_t = pl.pallas_call(
        functools.partial(query_kernel, n_row, tokens),
        out_shape=[
            jax.ShapeDtypeStruct((slot_tokens, width), bf16),
            jax.ShapeDtypeStruct((RANK, slot_tokens), bf16),
        ],
        in_specs=[SMEM] + [VMEM] * 4,
        out_specs=[VMEM] * 2,
        compiler_params=params(16),
        name="queries",
    )(adapter_ids, hid, base, up, jnp.concatenate(columns))

    far = list(range(max(drop, 1), n_row.bit_length() - 1))[::-1]
    turn = len(far) // 2
    core = [0] if drop == 0 else []
    early, late = [], []

    def spread(a, order):
        offset = a * part_rows
        held = jnp.concatenate([plane[offset : offset + part_rows] for plane in planes])
        parts = {0: held}
        early.append((a, 0, [(plane, offset) for plane in planes]))
        for k, bit in enumerate(order):
            mask, keys = 1 << bit, list(parts)
            got = swap(jnp.concatenate([parts[m] for m in keys]), "row", mask)
            group = late if k == len(order) - 1 else early
            for n, m in enumerate(keys):
                at = n * held.shape[0]
                parts[m | mask] = got[at : at + held.shape[0]]
                place = [(got, at + j * part_rows) for j in range(n_pre - 1)]
                group.append((a, (m | mask) >> drop, place))

    spread(0, far + core)
    spread(1, far[turn:] + far[:turn] + core)

    rows = heads * slot_tokens
    state = [jax.ShapeDtypeStruct((rows, c), f32) for c in (HD, HD, 3 * HD)]

    def attention(group, last, operands, in_specs, out_shape, scratch):
        sources, places = [], []
        for a, i, place in group:
            for array, _ in place:
                if not any(array is other for other in sources):
                    sources.append(array)
            index = [[array is other for other in sources].index(True) for array, _ in place]
            places.append((a, i, [(n, first) for n, (_, first) in zip(index, place)]))
        keys = len(places) * (n_pre - 1) * part_rows // 2 + (0 if last else local_keys)
        return pl.pallas_call(
            functools.partial(
                attention_kernel, n_pre, drop, part_rows, places, len(sources), last, tokens
            ),
            out_shape=out_shape,
            in_specs=in_specs + [VMEM] * len(sources),
            out_specs=[VMEM] * len(out_shape),
            scratch_shapes=[
                pltpu.VMEM((keys, 2 * HD), bf16),
                pltpu.VMEM((rows, HD), bf16),
                pltpu.VMEM((rows, HD), bf16),
            ]
            + scratch,
            compiler_params=params(20 + keys * HD * 8 // MIB),
            cost_estimate=pl.CostEstimate(
                flops=4 * rows * keys * HD, bytes_accessed=keys * HD * 4, transcendentals=rows * keys // 2
            ),
            name="last_keys" if last else "first_keys",
        )(*operands, *sources)

    held_state = attention(
        early, False, (masks, queries, cot, k_prefix, v_prefix), [SMEM] + [VMEM] * 4, state, []
    )
    attended, sent = attention(
        late,
        True,
        (adapter_ids, masks, queries, cot, latent_t, up, *held_state),
        [SMEM] * 2 + [VMEM] * 7,
        [
            jax.ShapeDtypeStruct((slot_tokens, width), bf16),
            jax.ShapeDtypeStruct((RANK, width + slot_tokens), bf16),
        ],
        [pltpu.VMEM(s.shape, s.dtype) for s in state] + [pltpu.VMEM((slot_tokens, width), bf16)],
    )

    attended_parts = [swap(attended, "pre", j) for j in range(n_slots)]
    shared = [swap(sent, "pre", j) for j in range(n_slots)]

    pairs = n_row // 2
    even, odd = pl.pallas_call(
        functools.partial(down_kernel, n_slots, n_row, width),
        out_shape=[jax.ShapeDtypeStruct((pairs * RANK, depth + width), bf16)] * 2,
        in_specs=[VMEM] * (n_slots + 1),
        out_specs=[VMEM] * 2,
        compiler_params=params(16),
        name="down",
    )(*shared, hidden_in)
    odd = swap(odd, "row", 1)
    spans = [slice(m * RANK, (m + 1) * RANK) for m in range(pairs)]
    pieces = [swap(jnp.concatenate([even[at], odd[at]]), "row", 2 * m) for m, at in enumerate(spans)]

    return pl.pallas_call(
        functools.partial(finish_kernel, n_slots, n_row, tokens),
        out_shape=[
            jax.ShapeDtypeStruct((tokens, width), bf16),
            jax.ShapeDtypeStruct((depth, rank_cols), f32),
            jax.ShapeDtypeStruct((rank_cols, width), f32),
        ],
        in_specs=[SMEM] + [VMEM] * (pairs + n_slots),
        out_specs=[HBM, VMEM, VMEM],
        scratch_shapes=[pltpu.VMEM((rank_cols, depth), f32), pltpu.SemaphoreType.DMA((n_slots,))],
        compiler_params=params(16),
        name="finish",
    )(adapter_ids, *pieces, *attended_parts)


def solution(mesh):
    in_specs = (
        P("row", None),
        P("row", None),
        P("pre", None),
        P("pre", None),
        P(None, "pre"),
        P(),
        P("row", None),
        P(),
        P("row", None),
    )
    out_specs = (P("row", None), P("row", None), P())
    return jax.shard_map(shards, mesh=mesh, in_specs=in_specs, out_specs=out_specs, check_vma=False)
```

```python
import functools
import math

import jax
import jax.numpy as jnp
from jax import lax
from jax.experimental import pallas as pl
from jax.experimental.pallas import tpu as pltpu
from jax.sharding import PartitionSpec as P

HD = 128
RANK = 16
CONT = 512
MB = 128
CHUNK = 512
ROW_TILE = 512
MIN_TOKENS = 16
ADAPTER_SCALE = 2.0
VERY_LOW = -1e30
LOG2E = 1.4426950408889634
MIB = 1 << 20

NT = (((1,), (1,)), ((), ()))
VMEM = pl.BlockSpec(memory_space=pltpu.VMEM)
SMEM = pl.BlockSpec(memory_space=pltpu.SMEM)
HBM = pl.BlockSpec(memory_space=pltpu.HBM)


def dot(a, b):
    return jnp.dot(a, b, preferred_element_type=jnp.float32)


def dot_nt(a, b):
    return lax.dot_general(a, b, NT, preferred_element_type=jnp.float32)


def swap(x, axis, mask):
    if mask == 0:
        return x
    return lax.ppermute(x, axis, [(s, s ^ mask) for s in range(lax.axis_size(axis))])


def params(mib):
    return pltpu.CompilerParams(vmem_limit_bytes=mib * MIB)


def adapter_of(ids, row, tokens):
    return pl.multiple_of(ids[row * tokens // CONT] * RANK, RANK)


def slot_of(slot_tokens, n_slots, offset=0):
    slot = lax.rem(lax.axis_index("pre"), n_slots) ^ offset
    return pl.ds(pl.multiple_of(slot * slot_tokens, slot_tokens), slot_tokens)


def fetch(pairs, sems):
    copies = [pltpu.make_async_copy(src, dst, sems.at[i]) for i, (src, dst) in enumerate(pairs)]
    for copy in copies:
        copy.start()
    return copies


def mask_rows(mask):
    return -(-mask.shape[0] // 16) * 16


def prep_kernel(n_row, drop, part_rows, tokens, *refs):
    k_ref, v_ref, mask_ref, ids_ref, a_ref, away_ref, slots_ref, mask_in, ids, a_in, at, sems = refs
    row = lax.axis_index("row")
    half = part_rows // 2
    begin = (row >> drop) * part_rows
    pairs = [(ids_ref, ids), (a_ref, a_in), (mask_ref, mask_in)]
    for a in range(2):
        span = pl.ds(pl.multiple_of(begin + a * half, half), half)
        pairs.append((k_ref.at[span, :], away_ref.at[pl.ds(2 * a * half, half), :]))
        pairs.append((v_ref.at[span, :], away_ref.at[pl.ds((2 * a + 1) * half, half), :]))
    copies = fetch(pairs, sems)
    copies[1].wait()
    at[...] = a_in[...].astype(jnp.float32).T
    copies[0].wait()
    for i in range(n_row):
        piece = at[pl.ds(adapter_of(ids, row ^ i, tokens), RANK), :]
        slots_ref[i * RANK : (i + 1) * RANK, :] = piece.astype(jnp.bfloat16)
    students, blocks = mask_in.shape
    copies[2].wait()
    away_ref[2 * part_rows :, :] = jnp.zeros_like(away_ref[2 * part_rows :, :])
    away_ref[2 * part_rows : 2 * part_rows + students, :blocks] = mask_in[...].astype(jnp.bfloat16)
    for copy in copies[3:]:
        copy.wait()


def query_kernel(n_row, tokens, ids, hid, base, up_ref, columns, q_ref, latt_ref):
    row = lax.axis_index("row")
    slot_tokens = q_ref.shape[0]
    depth = columns.shape[1]
    latent = jnp.zeros((slot_tokens, RANK), jnp.float32)
    latent_t = jnp.zeros((RANK, slot_tokens), jnp.float32)
    for i in range(n_row):
        piece = columns[i * RANK : (i + 1) * RANK, :]
        block = hid[:, pl.ds(pl.multiple_of((row ^ i) * depth, depth), depth)]
        latent += dot_nt(block, piece)
        latent_t += dot_nt(piece, block)
    latt_ref[...] = latent_t.astype(jnp.bfloat16)
    up = up_ref[pl.ds(adapter_of(ids, row, tokens), RANK), :]
    raised = dot(latent.astype(jnp.bfloat16), up)
    q_ref[...] = (base[...].astype(jnp.float32) + ADAPTER_SCALE * raised).astype(jnp.bfloat16)


def attention_kernel(n_pre, drop, part_rows, places, n_sources, first, last, tokens, *refs):
    masks, q_ref, cot_ref = refs[:3]
    refs = refs[3:]
    if first:
        k_own, v_own, refs = refs[0], refs[1], refs[2:]
    else:
        held, refs = refs[:3], refs[3:]
    if last:
        ids, latt_ref, up_ref, refs = *refs[:3], refs[3:]
    sources, refs = refs[:n_sources], refs[n_sources:]
    if last:
        att_ref, sent_ref, kv, q, cot, top, total, acc, grads = refs
    else:
        top, total, acc, kv, q, cot = refs
    row = lax.axis_index("row")
    slot_tokens, width = q_ref.shape
    heads = width // HD
    rows = heads * slot_tokens
    tile = min(ROW_TILE, rows)
    scale = 1.0 / math.sqrt(HD)
    factor = scale * LOG2E

    student = row * tokens // CONT
    half = part_rows // 2
    unit = min(MB, half)

    def keep(count, live, key_block, value_block):
        @pl.when(live)
        def _():
            at = pl.ds(pl.multiple_of(count * unit, unit), unit)
            kv[at, :HD] = value_block()
            kv[at, HD:] = key_block()

        return count + live.astype(jnp.int32)

    def own_block(b, count):
        at = pl.ds(pl.multiple_of(b * unit, unit), unit)
        live = masks[0, student, b * unit // MB] > 0
        return keep(count, live, lambda: k_own[at, :], lambda: v_own[at, :])

    def block_of(source, begin):
        return lambda: sources[source][begin : begin + unit, :]

    count = jnp.int32(0)
    if first:
        count = lax.fori_loop(0, k_own.shape[0] // unit, own_block, count)
    for a, i, place in places:
        piece = (row >> drop) ^ i
        for j in range(1, n_pre):
            source, begin = place[j - 1]
            for u in range(half // unit):
                block = (piece * part_rows + a * half + u * unit) // MB
                count = keep(
                    count,
                    masks[j, student, block] > 0,
                    block_of(source, begin + u * unit),
                    block_of(source, begin + half + u * unit),
                )

    for h in range(heads):
        at = pl.ds(h * slot_tokens, slot_tokens)
        q[at, :] = q_ref[:, h * HD : (h + 1) * HD]
        cot[at, :] = cot_ref[:, h * HD : (h + 1) * HD]
    if first:
        top[...] = jnp.full_like(top, VERY_LOW)
        total[...] = jnp.zeros_like(total)
        acc[...] = jnp.zeros_like(acc)
    else:
        for ref, given in zip((top, total, acc), held):
            ref[...] = given[...]

    def step(begin, size):
        both = kv[pl.ds(pl.multiple_of(begin, unit), size), :]
        values, keys = both[:, :HD], both[:, HD:]
        lane = min(size, HD)
        lanes = size // lane
        for r0 in range(0, rows, tile):
            at = pl.ds(r0, tile)
            scores = dot_nt(q[at, :], keys)
            old = top[at, :]
            new = jnp.maximum(old, jnp.max(scores, axis=1, keepdims=True))
            top[at, :] = new
            weights = jnp.exp2((scores - jnp.concatenate([new[:, :lane]] * lanes, axis=1)) * factor)
            shrink = jnp.exp2((old - new) * factor)
            partial = weights[:, :lane]
            for c in range(1, lanes):
                partial = partial + weights[:, c * lane : (c + 1) * lane]
            total[at, :] *= shrink
            total[at, :lane] += partial
            grad_weights = (weights * dot_nt(cot[at, :], values)).astype(jnp.bfloat16)
            first_two = dot(weights.astype(jnp.bfloat16), both)
            last = dot(grad_weights, keys)
            acc[at, :HD] = acc[at, :HD] * shrink + first_two[:, :HD]
            acc[at, HD : 2 * HD] = acc[at, HD : 2 * HD] * shrink + first_two[:, HD:]
            acc[at, 2 * HD :] = acc[at, 2 * HD :] * shrink + last

    per_chunk = CHUNK // unit
    full = count // per_chunk

    def full_step(c, carry):
        step(c * CHUNK, CHUNK)
        return carry

    lax.fori_loop(0, full, full_step, 0)
    size = CHUNK // 2
    while size >= unit:
        done = count // (2 * size // unit) * (2 * size)
        pl.when((count * unit - done) >= size)(functools.partial(step, done, size))
        size //= 2
    if not last:
        return

    for h in range(heads):
        at = pl.ds(h * slot_tokens, slot_tokens)
        inverse = 1.0 / jnp.sum(total[at, :], axis=1, keepdims=True)
        attended = (acc[at, :HD] * inverse).astype(jnp.bfloat16)
        att_ref[:, h * HD : (h + 1) * HD] = attended
        delta = jnp.sum(
            cot[at, :].astype(jnp.float32) * attended.astype(jnp.float32), axis=1, keepdims=True
        )
        grad = (acc[at, 2 * HD :] - delta * acc[at, HD : 2 * HD]) * (inverse * scale)
        grads[:, h * HD : (h + 1) * HD] = grad.astype(jnp.bfloat16)
    query_gradient = grads[...]
    up = up_ref[pl.ds(adapter_of(ids, row, tokens), RANK), :]
    sent_ref[:, :width] = (ADAPTER_SCALE * dot(latt_ref[...], query_gradient)).astype(jnp.bfloat16)
    sent_ref[:, width:] = (ADAPTER_SCALE * dot_nt(up, query_gradient)).astype(jnp.bfloat16)


def down_kernel(n_slots, n_row, width, *refs):
    parts, hidden, even_ref, odd_ref = refs[:n_slots], refs[n_slots], *refs[n_slots + 1 :]
    row = lax.axis_index("row")
    depth = even_ref.shape[1] - width
    slot_tokens = parts[0].shape[1] - width
    up = parts[0][:, :width].astype(jnp.float32)
    for part in parts[1:]:
        up = up + part[:, :width].astype(jnp.float32)
    up = up.astype(jnp.bfloat16)
    slots = [slot_of(slot_tokens, n_slots, j) for j in range(n_slots)]
    for i in range(n_row):
        out = odd_ref if i & 1 else even_ref
        rows = slice((i >> 1) * RANK, ((i >> 1) + 1) * RANK)
        cols = pl.ds(pl.multiple_of((row ^ i) * depth, depth), depth)
        grad = jnp.zeros((RANK, depth), jnp.float32)
        for j in range(n_slots):
            grad += dot(parts[j][:, width:], hidden[slots[j], cols])
        out[rows, :depth] = grad.astype(jnp.bfloat16)
        out[rows, depth:] = up


def finish_kernel(n_slots, n_row, tokens, ids, *refs):
    pairs, att, refs = refs[: n_row // 2], refs[n_row // 2 : n_row // 2 + n_slots], refs[n_row // 2 + n_slots :]
    att_out, down_ref, up_ref, down, sems = refs
    row = lax.axis_index("row")
    depth = down.shape[1]
    slot_tokens = att[0].shape[0]
    copies = fetch(
        [(att[j], att_out.at[slot_of(slot_tokens, n_slots, j), :]) for j in range(n_slots)], sems
    )
    down[...] = jnp.zeros_like(down)
    up_ref[...] = jnp.zeros_like(up_ref)
    for i in range(n_row):
        at = pl.ds(adapter_of(ids, row ^ i, tokens), RANK)
        part = pairs[i >> 1][(i & 1) * RANK : ((i & 1) + 1) * RANK, :]
        down[at, :] += part[:, :depth].astype(jnp.float32)
        up_ref[at, :] += part[:, depth:].astype(jnp.float32)
    down_ref[...] = down[...].T
    for copy in copies:
        copy.wait()


def shards(
    hidden_in,
    frozen_query_base,
    k_prefix,
    v_prefix,
    tree_mask,
    adapter_ids,
    a_down,
    up_weight_matrix,
    cotangent,
):
    tokens, model = hidden_in.shape
    width = frozen_query_base.shape[1]
    heads = width // HD
    depth, rank_cols = a_down.shape
    local_keys = k_prefix.shape[0]
    n_pre, n_row = lax.axis_size("pre"), lax.axis_size("row")
    n_slots = min(n_pre, tokens // MIN_TOKENS)
    slot_tokens = tokens // n_slots
    bf16, f32 = jnp.bfloat16, jnp.float32
    slices = min(n_row, local_keys // MB)
    drop = (n_row // slices).bit_length() - 1
    part_rows = local_keys // slices
    students, blocks = tree_mask.shape

    away, slots = pl.pallas_call(
        functools.partial(prep_kernel, n_row, drop, part_rows, tokens),
        out_shape=[
            jax.ShapeDtypeStruct((2 * part_rows + mask_rows(tree_mask), HD), bf16),
            jax.ShapeDtypeStruct((n_row * RANK, depth), bf16),
        ],
        in_specs=[HBM] * 5,
        out_specs=[VMEM] * 2,
        scratch_shapes=[
            pltpu.VMEM((students, blocks), jnp.int32),
            pltpu.SMEM(adapter_ids.shape, jnp.int32),
            pltpu.VMEM((depth, rank_cols), bf16),
            pltpu.VMEM((rank_cols, depth), f32),
            pltpu.SemaphoreType.DMA((7,)),
        ],
        compiler_params=params(56),
        name="prep",
    )(k_prefix, v_prefix, tree_mask, adapter_ids, a_down)
    planes = [swap(away, "pre", j) for j in range(1, n_pre)]
    masks = jnp.stack(
        [tree_mask]
        + [plane[2 * part_rows : 2 * part_rows + students, :blocks].astype(jnp.int32) for plane in planes]
    )

    columns = [slots[i * RANK : (i + 1) * RANK] for i in range(n_row)]
    for bit in range(n_row.bit_length() - 1):
        moved = [i for i in range(n_row) if i >> bit & 1]
        got = swap(jnp.concatenate([columns[i] for i in moved]), "row", 1 << bit)
        for k, i in enumerate(moved):
            columns[i] = got[k * RANK : (k + 1) * RANK]
    planes, columns = lax.optimization_barrier((planes, jnp.concatenate(columns)))
    first = lax.axis_index("pre") % n_slots * slot_tokens
    hid, base, cot = (
        lax.dynamic_slice_in_dim(x, first, slot_tokens, 0)
        for x in (hidden_in, frozen_query_base, cotangent)
    )
    up = up_weight_matrix
    queries, latent_t = pl.pallas_call(
        functools.partial(query_kernel, n_row, tokens),
        out_shape=[
            jax.ShapeDtypeStruct((slot_tokens, width), bf16),
            jax.ShapeDtypeStruct((RANK, slot_tokens), bf16),
        ],
        in_specs=[SMEM] + [VMEM] * 4,
        out_specs=[VMEM] * 2,
        compiler_params=params(16),
        name="queries",
    )(adapter_ids, hid, base, up, columns)

    rows = heads * slot_tokens
    state = [jax.ShapeDtypeStruct((rows, c), f32) for c in (HD, HD, 3 * HD)]

    def attention(group, first, last, operands, in_specs, out_shape, scratch):
        sources, places = [], []
        for a, i, place in group:
            for array, _ in place:
                if not any(array is other for other in sources):
                    sources.append(array)
            index = [[array is other for other in sources].index(True) for array, _ in place]
            places.append((a, i, [(n, begin) for n, (_, begin) in zip(index, place)]))
        keys = len(places) * (n_pre - 1) * part_rows // 2 + (local_keys if first else 0)
        return pl.pallas_call(
            functools.partial(
                attention_kernel, n_pre, drop, part_rows, places, len(sources), first, last, tokens
            ),
            out_shape=out_shape,
            in_specs=[SMEM, VMEM, VMEM] + in_specs + [VMEM] * len(sources),
            out_specs=[VMEM] * len(out_shape),
            scratch_shapes=[
                pltpu.VMEM((keys, 2 * HD), bf16),
                pltpu.VMEM((rows, HD), bf16),
                pltpu.VMEM((rows, HD), bf16),
            ]
            + scratch,
            compiler_params=params(24 + keys * HD * 8 // MIB),
            cost_estimate=pl.CostEstimate(
                flops=4 * rows * keys * HD, bytes_accessed=keys * HD * 4, transcendentals=rows * keys // 2
            ),
            name="first_keys" if first else "last_keys" if last else "next_keys",
        )(masks, queries, cot, *operands, *sources)

    far = list(range(max(drop, 1), n_row.bit_length() - 1))[::-1]
    turn = len(far) // 2
    core = [0] if drop == 0 else []
    orders = [far + core, far[turn:] + far[:turn] + core]
    rounds = len(orders[0])
    away_rows = (n_pre - 1) * part_rows
    parts = [
        {0: jnp.concatenate([plane[a * part_rows : (a + 1) * part_rows] for plane in planes])}
        for a in range(2)
    ]
    groups = [[], [], []]
    for a in range(2):
        groups[0].append((a, 0, [(plane, a * part_rows) for plane in planes]))
    for k in range(rounds):
        got = [
            swap(jnp.concatenate(list(parts[a].values())), "row", 1 << orders[a][k]) for a in range(2)
        ]
        if k == rounds - 3:
            got, (queries, latent_t) = lax.optimization_barrier((got, (queries, latent_t)))
        if k == rounds - 2:
            held = attention(groups[0], True, False, (k_prefix, v_prefix), [VMEM] * 2, state, [])
            got, held = lax.optimization_barrier((got, held))
        for a in range(2):
            for n, m in enumerate(list(parts[a])):
                moved = m | 1 << orders[a][k]
                parts[a][moved] = got[a][n * away_rows : (n + 1) * away_rows]
                place = [(got[a], n * away_rows + j * part_rows) for j in range(n_pre - 1)]
                groups[max(0, k + 3 - rounds)].append((a, moved >> drop, place))
    held = attention(groups[1], False, False, held, [VMEM] * 3, state, [])
    attended, sent = attention(
        groups[2],
        False,
        True,
        (*held, adapter_ids, latent_t, up),
        [VMEM] * 3 + [SMEM] + [VMEM] * 2,
        [
            jax.ShapeDtypeStruct((slot_tokens, width), bf16),
            jax.ShapeDtypeStruct((RANK, width + slot_tokens), bf16),
        ],
        [pltpu.VMEM(s.shape, s.dtype) for s in state] + [pltpu.VMEM((slot_tokens, width), bf16)],
    )

    attended_parts = {0: attended}
    for bit in range(n_slots.bit_length() - 1)[::-1]:
        for m in list(attended_parts):
            attended_parts[m | 1 << bit] = swap(attended_parts[m], "pre", 1 << bit)
    shared = [swap(sent, "pre", j) for j in range(n_slots)]

    pairs = n_row // 2
    even, odd = pl.pallas_call(
        functools.partial(down_kernel, n_slots, n_row, width),
        out_shape=[jax.ShapeDtypeStruct((pairs * RANK, depth + width), bf16)] * 2,
        in_specs=[VMEM] * (n_slots + 1),
        out_specs=[VMEM] * 2,
        compiler_params=params(16),
        name="down",
    )(*shared, hidden_in)
    odd = swap(odd, "row", 1)
    spans = [slice(m * RANK, (m + 1) * RANK) for m in range(pairs)]
    pieces = [swap(jnp.concatenate([even[at], odd[at]]), "row", 2 * m) for m, at in enumerate(spans)]

    return pl.pallas_call(
        functools.partial(finish_kernel, n_slots, n_row, tokens),
        out_shape=[
            jax.ShapeDtypeStruct((tokens, width), bf16),
            jax.ShapeDtypeStruct((depth, rank_cols), f32),
            jax.ShapeDtypeStruct((rank_cols, width), f32),
        ],
        in_specs=[SMEM] + [VMEM] * (pairs + n_slots),
        out_specs=[HBM, VMEM, VMEM],
        scratch_shapes=[pltpu.VMEM((rank_cols, depth), f32), pltpu.SemaphoreType.DMA((n_slots,))],
        compiler_params=params(16),
        name="finish",
    )(adapter_ids, *pieces, *(attended_parts[j] for j in range(n_slots)))


def solution(mesh):
    in_specs = (
        P("row", None),
        P("row", None),
        P("pre", None),
        P("pre", None),
        P(None, "pre"),
        P(),
        P("row", None),
        P(),
        P("row", None),
    )
    out_specs = (P("row", None), P("row", None), P())
    return jax.shard_map(shards, mesh=mesh, in_specs=in_specs, out_specs=out_specs, check_vma=False)
```

```python
import functools
import math

import jax
import jax.numpy as jnp
from jax import lax
from jax.experimental import pallas as pl
from jax.experimental.pallas import tpu as pltpu
from jax.sharding import PartitionSpec as P

HD = 128
RANK = 16
CONT = 512
MB = 128
CHUNK = 512
ROW_TILE = 1024
MIN_TOKENS = 16
ADAPTER_SCALE = 2.0
VERY_LOW = -1e30
LOG2E = 1.4426950408889634
MIB = 1 << 20

NT = (((1,), (1,)), ((), ()))
VMEM = pl.BlockSpec(memory_space=pltpu.VMEM)
SMEM = pl.BlockSpec(memory_space=pltpu.SMEM)
HBM = pl.BlockSpec(memory_space=pltpu.HBM)


def dot(a, b):
    return jnp.dot(a, b, preferred_element_type=jnp.float32)


def dot_nt(a, b):
    return lax.dot_general(a, b, NT, preferred_element_type=jnp.float32)


def swap(x, axis, mask):
    if mask == 0:
        return x
    return lax.ppermute(x, axis, [(s, s ^ mask) for s in range(lax.axis_size(axis))])


def params(mib):
    return pltpu.CompilerParams(vmem_limit_bytes=mib * MIB)


def adapter_of(ids, row, tokens):
    return pl.multiple_of(ids[row * tokens // CONT] * RANK, RANK)


def slot_of(slot_tokens, n_slots, offset=0):
    slot = lax.rem(lax.axis_index("pre"), n_slots) ^ offset
    return pl.ds(pl.multiple_of(slot * slot_tokens, slot_tokens), slot_tokens)


def fetch(pairs, sems):
    copies = [pltpu.make_async_copy(src, dst, sems.at[i]) for i, (src, dst) in enumerate(pairs)]
    for copy in copies:
        copy.start()
    return copies


def mask_rows(mask):
    return -(-mask.shape[0] // 16) * 16


def away_kernel(drop, part_rows, k_ref, v_ref, mask_ref, away_ref, mask_in, sems):
    half = part_rows // 2
    begin = (lax.axis_index("row") >> drop) * part_rows
    pairs = [(mask_ref, mask_in)]
    for a in range(2):
        span = pl.ds(pl.multiple_of(begin + a * half, half), half)
        pairs.append((k_ref.at[span, :], away_ref.at[pl.ds(2 * a * half, half), :]))
        pairs.append((v_ref.at[span, :], away_ref.at[pl.ds((2 * a + 1) * half, half), :]))
    copies = fetch(pairs, sems)
    students, blocks = mask_in.shape
    copies[0].wait()
    away_ref[2 * part_rows :, :] = jnp.zeros_like(away_ref[2 * part_rows :, :])
    away_ref[2 * part_rows : 2 * part_rows + students, :blocks] = mask_in[...].astype(jnp.bfloat16)
    for copy in copies[1:]:
        copy.wait()


def pick_kernel(n_row, tokens, ids_ref, a_ref, slots_ref, ids, a_in, at, sems):
    row = lax.axis_index("row")
    copies = fetch([(ids_ref, ids), (a_ref, a_in)], sems)
    copies[1].wait()
    at[...] = a_in[...].astype(jnp.float32).T
    copies[0].wait()
    for i in range(n_row):
        piece = at[pl.ds(adapter_of(ids, row ^ i, tokens), RANK), :]
        slots_ref[i * RANK : (i + 1) * RANK, :] = piece.astype(jnp.bfloat16)


def query_kernel(n_row, tokens, ids, hid, base, up_ref, columns, q_ref, latt_ref):
    row = lax.axis_index("row")
    slot_tokens = q_ref.shape[0]
    depth = columns.shape[1]
    latent = jnp.zeros((slot_tokens, RANK), jnp.float32)
    latent_t = jnp.zeros((RANK, slot_tokens), jnp.float32)
    for i in range(n_row):
        piece = columns[i * RANK : (i + 1) * RANK, :]
        block = hid[:, pl.ds(pl.multiple_of((row ^ i) * depth, depth), depth)]
        latent += dot_nt(block, piece)
        latent_t += dot_nt(piece, block)
    latt_ref[...] = latent_t.astype(jnp.bfloat16)
    up = up_ref[pl.ds(adapter_of(ids, row, tokens), RANK), :]
    raised = dot(latent.astype(jnp.bfloat16), up)
    q_ref[...] = (base[...].astype(jnp.float32) + ADAPTER_SCALE * raised).astype(jnp.bfloat16)


def attention_kernel(n_pre, drop, part_rows, places, n_sources, first, last, tokens, *refs):
    masks, q_ref, cot_ref = refs[:3]
    refs = refs[3:]
    if first:
        k_own, v_own, refs = refs[0], refs[1], refs[2:]
    else:
        held, refs = refs[:3], refs[3:]
    if last:
        ids, latt_ref, up_ref, refs = *refs[:3], refs[3:]
    sources, refs = refs[:n_sources], refs[n_sources:]
    if last:
        att_ref, sent_ref, kv, q, cot, top, total, acc, grads = refs
    else:
        top, total, acc, kv, q, cot = refs
    row = lax.axis_index("row")
    slot_tokens, width = q_ref.shape
    heads = width // HD
    rows = heads * slot_tokens
    tile = min(ROW_TILE, rows)
    scale = 1.0 / math.sqrt(HD)
    factor = scale * LOG2E

    student = row * tokens // CONT
    half = part_rows // 2
    unit = min(MB, half)

    def keep(count, live, key_block, value_block):
        @pl.when(live)
        def _():
            at = pl.ds(pl.multiple_of(count * unit, unit), unit)
            kv[at, :HD] = value_block()
            kv[at, HD:] = key_block()

        return count + live.astype(jnp.int32)

    def own_block(b, count):
        at = pl.ds(pl.multiple_of(b * unit, unit), unit)
        live = masks[0, student, b * unit // MB] > 0
        return keep(count, live, lambda: k_own[at, :], lambda: v_own[at, :])

    def block_of(source, begin):
        return lambda: sources[source][begin : begin + unit, :]

    count = jnp.int32(0)
    if first:
        count = lax.fori_loop(0, k_own.shape[0] // unit, own_block, count)
    for a, i, place in places:
        piece = (row >> drop) ^ i
        for j in range(1, n_pre):
            source, begin = place[j - 1]
            for u in range(half // unit):
                block = (piece * part_rows + a * half + u * unit) // MB
                count = keep(
                    count,
                    masks[j, student, block] > 0,
                    block_of(source, begin + u * unit),
                    block_of(source, begin + half + u * unit),
                )

    for h in range(heads):
        at = pl.ds(h * slot_tokens, slot_tokens)
        q[at, :] = q_ref[:, h * HD : (h + 1) * HD]
        cot[at, :] = cot_ref[:, h * HD : (h + 1) * HD]
    if first:
        top[...] = jnp.full_like(top, VERY_LOW)
        total[...] = jnp.zeros_like(total)
        acc[...] = jnp.zeros_like(acc)
    else:
        for ref, given in zip((top, total, acc), held):
            ref[...] = given[...]

    def step(begin, size):
        both = kv[pl.ds(pl.multiple_of(begin, unit), size), :]
        values, keys = both[:, :HD], both[:, HD:]
        lane = min(size, HD)
        lanes = size // lane
        for r0 in range(0, rows, tile):
            at = pl.ds(r0, tile)
            scores = dot_nt(q[at, :], keys)
            old = top[at, :]
            new = jnp.maximum(old, jnp.max(scores, axis=1, keepdims=True))
            top[at, :] = new
            weights = jnp.exp2((scores - jnp.concatenate([new[:, :lane]] * lanes, axis=1)) * factor)
            shrink = jnp.exp2((old - new) * factor)
            partial = weights[:, :lane]
            for c in range(1, lanes):
                partial = partial + weights[:, c * lane : (c + 1) * lane]
            total[at, :] *= shrink
            total[at, :lane] += partial
            grad_weights = (weights * dot_nt(cot[at, :], values)).astype(jnp.bfloat16)
            first_two = dot(weights.astype(jnp.bfloat16), both)
            last = dot(grad_weights, keys)
            acc[at, :HD] = acc[at, :HD] * shrink + first_two[:, :HD]
            acc[at, HD : 2 * HD] = acc[at, HD : 2 * HD] * shrink + first_two[:, HD:]
            acc[at, 2 * HD :] = acc[at, 2 * HD :] * shrink + last

    per_chunk = CHUNK // unit
    full = count // per_chunk

    def full_step(c, carry):
        step(c * CHUNK, CHUNK)
        return carry

    lax.fori_loop(0, full, full_step, 0)
    rest = count * unit - full * CHUNK
    for blocks in range(1, CHUNK // MB):
        pl.when(rest // MB == blocks)(functools.partial(step, full * CHUNK, blocks * MB))
    if unit < MB:
        pl.when(rest % MB > 0)(functools.partial(step, (count - 1) * unit, unit))
    if not last:
        return

    for h in range(heads):
        at = pl.ds(h * slot_tokens, slot_tokens)
        inverse = 1.0 / jnp.sum(total[at, :], axis=1, keepdims=True)
        attended = (acc[at, :HD] * inverse).astype(jnp.bfloat16)
        att_ref[:, h * HD : (h + 1) * HD] = attended
        delta = jnp.sum(
            cot[at, :].astype(jnp.float32) * attended.astype(jnp.float32), axis=1, keepdims=True
        )
        grad = (acc[at, 2 * HD :] - delta * acc[at, HD : 2 * HD]) * (inverse * scale)
        grads[:, h * HD : (h + 1) * HD] = grad.astype(jnp.bfloat16)
    query_gradient = grads[...]
    up = up_ref[pl.ds(adapter_of(ids, row, tokens), RANK), :]
    sent_ref[:, :width] = (ADAPTER_SCALE * dot(latt_ref[...], query_gradient)).astype(jnp.bfloat16)
    sent_ref[:, width:] = (ADAPTER_SCALE * dot_nt(up, query_gradient)).astype(jnp.bfloat16)


def down_kernel(n_slots, n_row, width, *refs):
    parts, hidden, even_ref, odd_ref = refs[:n_slots], refs[n_slots], *refs[n_slots + 1 :]
    row = lax.axis_index("row")
    depth = even_ref.shape[1] - width
    slot_tokens = parts[0].shape[1] - width
    up = parts[0][:, :width].astype(jnp.float32)
    for part in parts[1:]:
        up = up + part[:, :width].astype(jnp.float32)
    up = up.astype(jnp.bfloat16)
    slots = [slot_of(slot_tokens, n_slots, j) for j in range(n_slots)]
    for i in range(n_row):
        out = odd_ref if i & 1 else even_ref
        rows = slice((i >> 1) * RANK, ((i >> 1) + 1) * RANK)
        cols = pl.ds(pl.multiple_of((row ^ i) * depth, depth), depth)
        grad = jnp.zeros((RANK, depth), jnp.float32)
        for j in range(n_slots):
            grad += dot(parts[j][:, width:], hidden[slots[j], cols])
        out[rows, :depth] = grad.astype(jnp.bfloat16)
        out[rows, depth:] = up


def finish_kernel(n_slots, n_row, tokens, ids, *refs):
    pairs, att, refs = refs[: n_row // 2], refs[n_row // 2 : n_row // 2 + n_slots], refs[n_row // 2 + n_slots :]
    att_out, down_ref, up_ref, down, sems = refs
    row = lax.axis_index("row")
    depth = down.shape[1]
    slot_tokens = att[0].shape[0]
    copies = fetch(
        [(att[j], att_out.at[slot_of(slot_tokens, n_slots, j), :]) for j in range(n_slots)], sems
    )
    down[...] = jnp.zeros_like(down)
    up_ref[...] = jnp.zeros_like(up_ref)
    for i in range(n_row):
        at = pl.ds(adapter_of(ids, row ^ i, tokens), RANK)
        part = pairs[i >> 1][(i & 1) * RANK : ((i & 1) + 1) * RANK, :]
        down[at, :] += part[:, :depth].astype(jnp.float32)
        up_ref[at, :] += part[:, depth:].astype(jnp.float32)
    down_ref[...] = down[...].T
    for copy in copies:
        copy.wait()


def shards(
    hidden_in,
    frozen_query_base,
    k_prefix,
    v_prefix,
    tree_mask,
    adapter_ids,
    a_down,
    up_weight_matrix,
    cotangent,
):
    tokens, model = hidden_in.shape
    width = frozen_query_base.shape[1]
    heads = width // HD
    depth, rank_cols = a_down.shape
    local_keys = k_prefix.shape[0]
    n_pre, n_row = lax.axis_size("pre"), lax.axis_size("row")
    n_slots = min(n_pre, tokens // MIN_TOKENS)
    slot_tokens = tokens // n_slots
    bf16, f32 = jnp.bfloat16, jnp.float32
    slices = min(n_row, local_keys // MB)
    drop = (n_row // slices).bit_length() - 1
    part_rows = local_keys // slices
    students, blocks = tree_mask.shape

    away = pl.pallas_call(
        functools.partial(away_kernel, drop, part_rows),
        out_shape=jax.ShapeDtypeStruct((2 * part_rows + mask_rows(tree_mask), HD), bf16),
        in_specs=[HBM] * 3,
        out_specs=VMEM,
        scratch_shapes=[pltpu.VMEM((students, blocks), jnp.int32), pltpu.SemaphoreType.DMA((5,))],
        compiler_params=params(56),
        name="away",
    )(k_prefix, v_prefix, tree_mask)

    away, a_down = lax.optimization_barrier((away, a_down))
    slots = pl.pallas_call(
        functools.partial(pick_kernel, n_row, tokens),
        out_shape=jax.ShapeDtypeStruct((n_row * RANK, depth), bf16),
        in_specs=[HBM] * 2,
        out_specs=VMEM,
        scratch_shapes=[
            pltpu.SMEM(adapter_ids.shape, jnp.int32),
            pltpu.VMEM((depth, rank_cols), bf16),
            pltpu.VMEM((rank_cols, depth), f32),
            pltpu.SemaphoreType.DMA((2,)),
        ],
        compiler_params=params(56),
        name="pick",
    )(adapter_ids, a_down)
    planes = {0: away}
    for bit in range(n_pre.bit_length() - 1)[::-1]:
        for m in list(planes):
            planes[m | 1 << bit] = swap(planes[m], "pre", 1 << bit)
    columns = [slots[i * RANK : (i + 1) * RANK] for i in range(n_row)]
    own = (hidden_in, frozen_query_base, cotangent)
    for bit in range(n_row.bit_length() - 1):
        moved = [i for i in range(n_row) if i >> bit & 1]
        got = swap(jnp.concatenate([columns[i] for i in moved]), "row", 1 << bit)
        if bit == 0:
            got, planes[1] = lax.optimization_barrier((got, planes[1]))
        if bit == 1:
            got, own = lax.optimization_barrier((got, own))
        for k, i in enumerate(moved):
            columns[i] = got[k * RANK : (k + 1) * RANK]
    planes = [planes[j] for j in range(1, n_pre)]
    planes, columns = lax.optimization_barrier((planes, jnp.concatenate(columns)))
    masks = jnp.stack(
        [tree_mask]
        + [plane[2 * part_rows : 2 * part_rows + students, :blocks].astype(jnp.int32) for plane in planes]
    )
    first = lax.axis_index("pre") % n_slots * slot_tokens
    hid, base, cot = (lax.dynamic_slice_in_dim(x, first, slot_tokens, 0) for x in own)
    up = up_weight_matrix
    queries, latent_t = pl.pallas_call(
        functools.partial(query_kernel, n_row, tokens),
        out_shape=[
            jax.ShapeDtypeStruct((slot_tokens, width), bf16),
            jax.ShapeDtypeStruct((RANK, slot_tokens), bf16),
        ],
        in_specs=[SMEM] + [VMEM] * 4,
        out_specs=[VMEM] * 2,
        compiler_params=params(16),
        name="queries",
    )(adapter_ids, hid, base, up, columns)

    rows = heads * slot_tokens
    state = [jax.ShapeDtypeStruct((rows, c), f32) for c in (HD, HD, 3 * HD)]

    def attention(group, first, last, operands, in_specs, out_shape, scratch):
        sources, places = [], []
        for a, i, place in group:
            for array, _ in place:
                if not any(array is other for other in sources):
                    sources.append(array)
            index = [[array is other for other in sources].index(True) for array, _ in place]
            places.append((a, i, [(n, begin) for n, (_, begin) in zip(index, place)]))
        keys = len(places) * (n_pre - 1) * part_rows // 2 + (local_keys if first else 0)
        return pl.pallas_call(
            functools.partial(
                attention_kernel, n_pre, drop, part_rows, places, len(sources), first, last, tokens
            ),
            out_shape=out_shape,
            in_specs=[SMEM, VMEM, VMEM] + in_specs + [VMEM] * len(sources),
            out_specs=[VMEM] * len(out_shape),
            scratch_shapes=[
                pltpu.VMEM((keys, 2 * HD), bf16),
                pltpu.VMEM((rows, HD), bf16),
                pltpu.VMEM((rows, HD), bf16),
            ]
            + scratch,
            compiler_params=params(24 + keys * HD * 8 // MIB),
            cost_estimate=pl.CostEstimate(
                flops=4 * rows * keys * HD, bytes_accessed=keys * HD * 4, transcendentals=rows * keys // 2
            ),
            name="first_keys" if first else "last_keys" if last else "next_keys",
        )(masks, queries, cot, *operands, *sources)

    far = list(range(max(drop, 1), n_row.bit_length() - 1))[::-1]
    turn = len(far) // 2
    core = [0] if drop == 0 else []
    orders = [far + core, far[turn:] + far[:turn] + core]
    rounds = len(orders[0])
    away_rows = (n_pre - 1) * part_rows
    parts = [
        {0: jnp.concatenate([plane[a * part_rows : (a + 1) * part_rows] for plane in planes])}
        for a in range(2)
    ]
    groups = [[], [], []]
    for a in range(2):
        groups[0].append((a, 0, [(plane, a * part_rows) for plane in planes]))
    for k in range(rounds):
        got = [
            swap(jnp.concatenate(list(parts[a].values())), "row", 1 << orders[a][k]) for a in range(2)
        ]
        if k == rounds - 3:
            got, (queries, latent_t) = lax.optimization_barrier((got, (queries, latent_t)))
        if k == rounds - 2:
            held = attention(groups[0], True, False, (k_prefix, v_prefix), [VMEM] * 2, state, [])
            got, held = lax.optimization_barrier((got, held))
        for a in range(2):
            for n, m in enumerate(list(parts[a])):
                moved = m | 1 << orders[a][k]
                parts[a][moved] = got[a][n * away_rows : (n + 1) * away_rows]
                place = [(got[a], n * away_rows + j * part_rows) for j in range(n_pre - 1)]
                groups[max(0, k + 3 - rounds)].append((a, moved >> drop, place))
    held = attention(groups[1], False, False, held, [VMEM] * 3, state, [])
    attended, sent = attention(
        groups[2],
        False,
        True,
        (*held, adapter_ids, latent_t, up),
        [VMEM] * 3 + [SMEM] + [VMEM] * 2,
        [
            jax.ShapeDtypeStruct((slot_tokens, width), bf16),
            jax.ShapeDtypeStruct((RANK, width + slot_tokens), bf16),
        ],
        [pltpu.VMEM(s.shape, s.dtype) for s in state] + [pltpu.VMEM((slot_tokens, width), bf16)],
    )

    slot_bits = range(n_slots.bit_length() - 1)
    attended_parts, shared = {0: attended}, [sent]
    if n_slots > 1:
        attended_parts[n_slots >> 1] = swap(attended, "pre", n_slots >> 1)
    for bit in slot_bits:
        got = swap(jnp.concatenate(shared), "pre", 1 << bit)
        shared += [got[n * RANK : (n + 1) * RANK] for n in range(len(shared))]

    pairs = n_row // 2
    even, odd = pl.pallas_call(
        functools.partial(down_kernel, n_slots, n_row, width),
        out_shape=[jax.ShapeDtypeStruct((pairs * RANK, depth + width), bf16)] * 2,
        in_specs=[VMEM] * (n_slots + 1),
        out_specs=[VMEM] * 2,
        compiler_params=params(16),
        name="down",
    )(*shared, hidden_in)
    odd = swap(odd, "row", 1)
    spans = [slice(m * RANK, (m + 1) * RANK) for m in range(pairs)]
    pieces = [swap(jnp.concatenate([even[at], odd[at]]), "row", 2 * m) for m, at in enumerate(spans)]

    if n_slots > 1:
        pieces, far_part = lax.optimization_barrier((pieces, attended_parts[n_slots >> 1]))
        attended_parts[n_slots >> 1] = far_part
    for bit in slot_bits[:-1][::-1]:
        for m in list(attended_parts):
            attended_parts[m | 1 << bit] = swap(attended_parts[m], "pre", 1 << bit)

    return pl.pallas_call(
        functools.partial(finish_kernel, n_slots, n_row, tokens),
        out_shape=[
            jax.ShapeDtypeStruct((tokens, width), bf16),
            jax.ShapeDtypeStruct((depth, rank_cols), f32),
            jax.ShapeDtypeStruct((rank_cols, width), f32),
        ],
        in_specs=[SMEM] + [VMEM] * (pairs + n_slots),
        out_specs=[HBM, VMEM, VMEM],
        scratch_shapes=[pltpu.VMEM((rank_cols, depth), f32), pltpu.SemaphoreType.DMA((n_slots,))],
        compiler_params=params(16),
        name="finish",
    )(adapter_ids, *pieces, *(attended_parts[j] for j in range(n_slots)))


def solution(mesh):
    in_specs = (
        P("row", None),
        P("row", None),
        P("pre", None),
        P("pre", None),
        P(None, "pre"),
        P(),
        P("row", None),
        P(),
        P("row", None),
    )
    out_specs = (P("row", None), P("row", None), P())
    return jax.shard_map(shards, mesh=mesh, in_specs=in_specs, out_specs=out_specs, check_vma=False)
```

```python
import functools
import math

import jax
import jax.numpy as jnp
from jax import lax
from jax.experimental import pallas as pl
from jax.experimental.pallas import tpu as pltpu
from jax.sharding import PartitionSpec as P

HD = 128
RANK = 16
CONT = 512
MB = 128
CHUNK = 512
ROW_TILE = 512
MIN_TOKENS = 16
ADAPTER_SCALE = 2.0
VERY_LOW = -1e30
LOG2E = 1.4426950408889634
MIB = 1 << 20

NT = (((1,), (1,)), ((), ()))
VMEM = pl.BlockSpec(memory_space=pltpu.VMEM)
SMEM = pl.BlockSpec(memory_space=pltpu.SMEM)
HBM = pl.BlockSpec(memory_space=pltpu.HBM)


def dot(a, b):
    return jnp.dot(a, b, preferred_element_type=jnp.float32)


def dot_nt(a, b):
    return lax.dot_general(a, b, NT, preferred_element_type=jnp.float32)


def swap(x, axis, mask):
    if mask == 0:
        return x
    return lax.ppermute(x, axis, [(s, s ^ mask) for s in range(lax.axis_size(axis))])


def params(mib):
    return pltpu.CompilerParams(vmem_limit_bytes=mib * MIB)


def adapter_of(ids, row, tokens):
    return pl.multiple_of(ids[row * tokens // CONT] * RANK, RANK)


def slot_of(slot_tokens, n_slots, offset=0):
    slot = lax.rem(lax.axis_index("pre"), n_slots) ^ offset
    return pl.ds(pl.multiple_of(slot * slot_tokens, slot_tokens), slot_tokens)


def fetch(pairs, sems):
    copies = [pltpu.make_async_copy(src, dst, sems.at[i]) for i, (src, dst) in enumerate(pairs)]
    for copy in copies:
        copy.start()
    return copies


def mask_rows(mask):
    return -(-mask.shape[0] // 16) * 16


def away_kernel(drop, part_rows, k_ref, v_ref, mask_ref, away_ref, mask_in, sems):
    half = part_rows // 2
    begin = (lax.axis_index("row") >> drop) * part_rows
    pairs = [(mask_ref, mask_in)]
    for a in range(2):
        span = pl.ds(pl.multiple_of(begin + a * half, half), half)
        pairs.append((k_ref.at[span, :], away_ref.at[pl.ds(2 * a * half, half), :]))
        pairs.append((v_ref.at[span, :], away_ref.at[pl.ds((2 * a + 1) * half, half), :]))
    copies = fetch(pairs, sems)
    students, blocks = mask_in.shape
    copies[0].wait()
    away_ref[2 * part_rows :, :] = jnp.zeros_like(away_ref[2 * part_rows :, :])
    away_ref[2 * part_rows : 2 * part_rows + students, :blocks] = mask_in[...].astype(jnp.bfloat16)
    for copy in copies[1:]:
        copy.wait()


def pick_kernel(n_row, tokens, ids_ref, a_ref, slots_ref, ids, a_in, at, sems):
    row = lax.axis_index("row")
    copies = fetch([(ids_ref, ids), (a_ref, a_in)], sems)
    copies[1].wait()
    at[...] = a_in[...].astype(jnp.float32).T
    copies[0].wait()
    for i in range(n_row):
        piece = at[pl.ds(adapter_of(ids, row ^ i, tokens), RANK), :]
        slots_ref[i * RANK : (i + 1) * RANK, :] = piece.astype(jnp.bfloat16)


def query_kernel(n_row, tokens, ids, hid, base, up_ref, columns, q_ref, latt_ref):
    row = lax.axis_index("row")
    slot_tokens = q_ref.shape[0]
    depth = columns.shape[1]
    latent = jnp.zeros((slot_tokens, RANK), jnp.float32)
    latent_t = jnp.zeros((RANK, slot_tokens), jnp.float32)
    for i in range(n_row):
        piece = columns[i * RANK : (i + 1) * RANK, :]
        block = hid[:, pl.ds(pl.multiple_of((row ^ i) * depth, depth), depth)]
        latent += dot_nt(block, piece)
        latent_t += dot_nt(piece, block)
    latt_ref[...] = latent_t.astype(jnp.bfloat16)
    up = up_ref[pl.ds(adapter_of(ids, row, tokens), RANK), :]
    raised = dot(latent.astype(jnp.bfloat16), up)
    q_ref[...] = (base[...].astype(jnp.float32) + ADAPTER_SCALE * raised).astype(jnp.bfloat16)


def attention_kernel(n_pre, drop, part_rows, places, n_sources, first, last, tokens, *refs):
    masks, q_ref, cot_ref = refs[:3]
    refs = refs[3:]
    if first:
        k_own, v_own, refs = refs[0], refs[1], refs[2:]
    else:
        held, refs = refs[:3], refs[3:]
    if last:
        ids, latt_ref, up_ref, refs = *refs[:3], refs[3:]
    sources, refs = refs[:n_sources], refs[n_sources:]
    if last:
        att_ref, sent_ref, kv, q, cot, top, total, acc, grads = refs
    else:
        top, total, acc, kv, q, cot = refs
    row = lax.axis_index("row")
    slot_tokens, width = q_ref.shape
    heads = width // HD
    rows = heads * slot_tokens
    tile = min(ROW_TILE, rows)
    scale = 1.0 / math.sqrt(HD)
    factor = scale * LOG2E

    student = row * tokens // CONT
    half = part_rows // 2
    unit = min(MB, half)

    def keep(count, live, key_block, value_block):
        @pl.when(live)
        def _():
            at = pl.ds(pl.multiple_of(count * unit, unit), unit)
            kv[at, :HD] = value_block()
            kv[at, HD:] = key_block()

        return count + live.astype(jnp.int32)

    def own_block(b, count):
        at = pl.ds(pl.multiple_of(b * unit, unit), unit)
        live = masks[0, student, b * unit // MB] > 0
        return keep(count, live, lambda: k_own[at, :], lambda: v_own[at, :])

    def block_of(source, begin):
        return lambda: sources[source][begin : begin + unit, :]

    count = jnp.int32(0)
    if first:
        count = lax.fori_loop(0, k_own.shape[0] // unit, own_block, count)
    for a, i, place in places:
        piece = (row >> drop) ^ i
        for j in range(1, n_pre):
            source, begin = place[j - 1]
            for u in range(half // unit):
                block = (piece * part_rows + a * half + u * unit) // MB
                count = keep(
                    count,
                    masks[j, student, block] > 0,
                    block_of(source, begin + u * unit),
                    block_of(source, begin + half + u * unit),
                )

    for h in range(heads):
        at = pl.ds(h * slot_tokens, slot_tokens)
        q[at, :] = q_ref[:, h * HD : (h + 1) * HD]
        cot[at, :] = cot_ref[:, h * HD : (h + 1) * HD]
    def over_keys(step):
        per_chunk = CHUNK // unit
        full = count // per_chunk

        def full_step(c, carry):
            step(c * CHUNK, CHUNK)
            return carry

        lax.fori_loop(0, full, full_step, 0)
        rest = count * unit - full * CHUNK
        for blocks in range(1, CHUNK // MB):
            pl.when(rest // MB == blocks)(functools.partial(step, full * CHUNK, blocks * MB))
        if unit < MB:
            pl.when(rest % MB > 0)(functools.partial(step, (count - 1) * unit, unit))

    def lanes(x):
        lane = min(x.shape[1], HD)
        return [x[:, c : c + lane] for c in range(0, x.shape[1], lane)]

    top[...] = jnp.full_like(top, VERY_LOW)

    def largest(begin, size):
        keys = kv[pl.ds(pl.multiple_of(begin, unit), size), HD:]
        for r0 in range(0, rows, tile):
            at = pl.ds(r0, tile)
            found = functools.reduce(jnp.maximum, lanes(dot_nt(q[at, :], keys)))
            top[at, : found.shape[1]] = jnp.maximum(top[at, : found.shape[1]], found)

    over_keys(largest)
    for h in range(heads):
        at = pl.ds(h * slot_tokens, slot_tokens)
        new = jnp.max(top[at, :], axis=1, keepdims=True)
        if first:
            top[at, :] = jnp.broadcast_to(new, (slot_tokens, HD))
            total[at, :] = jnp.zeros((slot_tokens, HD), jnp.float32)
            acc[at, :] = jnp.zeros((slot_tokens, 3 * HD), jnp.float32)
        else:
            old = held[0][at, :]
            new = jnp.maximum(old, new)
            shrink = jnp.exp2((old - new) * factor)
            top[at, :] = new
            total[at, :] = held[1][at, :] * shrink
            acc[at, :] = held[2][at, :] * jnp.concatenate([shrink] * 3, axis=1)

    def add(begin, size):
        both = kv[pl.ds(pl.multiple_of(begin, unit), size), :]
        values, keys = both[:, :HD], both[:, HD:]
        for r0 in range(0, rows, tile):
            at = pl.ds(r0, tile)
            scores = dot_nt(q[at, :], keys)
            shift = top[at, : min(size, HD)]
            weights = jnp.concatenate([jnp.exp2((x - shift) * factor) for x in lanes(scores)], axis=1)
            partial = functools.reduce(jnp.add, lanes(weights))
            total[at, : partial.shape[1]] += partial
            grad_weights = (weights * dot_nt(cot[at, :], values)).astype(jnp.bfloat16)
            acc[at, : 2 * HD] += dot(weights.astype(jnp.bfloat16), both)
            acc[at, 2 * HD :] += dot(grad_weights, keys)

    over_keys(add)
    if not last:
        return

    for h in range(heads):
        at = pl.ds(h * slot_tokens, slot_tokens)
        inverse = 1.0 / jnp.sum(total[at, :], axis=1, keepdims=True)
        attended = (acc[at, :HD] * inverse).astype(jnp.bfloat16)
        att_ref[:, h * HD : (h + 1) * HD] = attended
        delta = jnp.sum(
            cot[at, :].astype(jnp.float32) * attended.astype(jnp.float32), axis=1, keepdims=True
        )
        grad = (acc[at, 2 * HD :] - delta * acc[at, HD : 2 * HD]) * (inverse * scale)
        grads[:, h * HD : (h + 1) * HD] = grad.astype(jnp.bfloat16)
    query_gradient = grads[...]
    up = up_ref[pl.ds(adapter_of(ids, row, tokens), RANK), :]
    sent_ref[:, :width] = (ADAPTER_SCALE * dot(latt_ref[...], query_gradient)).astype(jnp.bfloat16)
    sent_ref[:, width:] = (ADAPTER_SCALE * dot_nt(up, query_gradient)).astype(jnp.bfloat16)


def down_kernel(n_slots, n_row, width, *refs):
    parts, hidden, even_ref, odd_ref = refs[:n_slots], refs[n_slots], *refs[n_slots + 1 :]
    row = lax.axis_index("row")
    depth = even_ref.shape[1] - width
    slot_tokens = parts[0].shape[1] - width
    up = parts[0][:, :width].astype(jnp.float32)
    for part in parts[1:]:
        up = up + part[:, :width].astype(jnp.float32)
    up = up.astype(jnp.bfloat16)
    slots = [slot_of(slot_tokens, n_slots, j) for j in range(n_slots)]
    for i in range(n_row):
        out = odd_ref if i & 1 else even_ref
        rows = slice((i >> 1) * RANK, ((i >> 1) + 1) * RANK)
        cols = pl.ds(pl.multiple_of((row ^ i) * depth, depth), depth)
        grad = jnp.zeros((RANK, depth), jnp.float32)
        for j in range(n_slots):
            grad += dot(parts[j][:, width:], hidden[slots[j], cols])
        out[rows, :depth] = grad.astype(jnp.bfloat16)
        out[rows, depth:] = up


def finish_kernel(n_row, tokens, ids, *refs):
    pairs, (down_ref, up_ref, down) = refs[: n_row // 2], refs[n_row // 2 :]
    row = lax.axis_index("row")
    depth = down.shape[1]
    down[...] = jnp.zeros_like(down)
    up_ref[...] = jnp.zeros_like(up_ref)
    for i in range(n_row):
        at = pl.ds(adapter_of(ids, row ^ i, tokens), RANK)
        part = pairs[i >> 1][(i & 1) * RANK : ((i & 1) + 1) * RANK, :]
        down[at, :] += part[:, :depth].astype(jnp.float32)
        up_ref[at, :] += part[:, depth:].astype(jnp.float32)
    down_ref[...] = down[...].T


def place_kernel(n_slots, *refs):
    parts, out, sems = refs[:n_slots], *refs[n_slots:]
    slot_tokens = parts[0].shape[0]
    for copy in fetch(
        [(parts[j], out.at[slot_of(slot_tokens, n_slots, j), :]) for j in range(n_slots)], sems
    ):
        copy.wait()


def shards(
    hidden_in,
    frozen_query_base,
    k_prefix,
    v_prefix,
    tree_mask,
    adapter_ids,
    a_down,
    up_weight_matrix,
    cotangent,
):
    tokens, model = hidden_in.shape
    width = frozen_query_base.shape[1]
    heads = width // HD
    depth, rank_cols = a_down.shape
    local_keys = k_prefix.shape[0]
    n_pre, n_row = lax.axis_size("pre"), lax.axis_size("row")
    n_slots = min(n_pre, tokens // MIN_TOKENS)
    slot_tokens = tokens // n_slots
    bf16, f32 = jnp.bfloat16, jnp.float32
    slices = min(n_row, local_keys // MB)
    drop = (n_row // slices).bit_length() - 1
    part_rows = local_keys // slices
    students, blocks = tree_mask.shape

    away = pl.pallas_call(
        functools.partial(away_kernel, drop, part_rows),
        out_shape=jax.ShapeDtypeStruct((2 * part_rows + mask_rows(tree_mask), HD), bf16),
        in_specs=[HBM] * 3,
        out_specs=VMEM,
        scratch_shapes=[pltpu.VMEM((students, blocks), jnp.int32), pltpu.SemaphoreType.DMA((5,))],
        compiler_params=params(56),
        name="away",
    )(k_prefix, v_prefix, tree_mask)

    away, a_down = lax.optimization_barrier((away, a_down))
    slots = pl.pallas_call(
        functools.partial(pick_kernel, n_row, tokens),
        out_shape=jax.ShapeDtypeStruct((n_row * RANK, depth), bf16),
        in_specs=[HBM] * 2,
        out_specs=VMEM,
        scratch_shapes=[
            pltpu.SMEM(adapter_ids.shape, jnp.int32),
            pltpu.VMEM((depth, rank_cols), bf16),
            pltpu.VMEM((rank_cols, depth), f32),
            pltpu.SemaphoreType.DMA((2,)),
        ],
        compiler_params=params(56),
        name="pick",
    )(adapter_ids, a_down)
    far_plane = n_pre >> 1
    planes = {far_plane: swap(away, "pre", far_plane)}
    planes[0], slots = lax.optimization_barrier((away, slots))
    for bit in range(n_pre.bit_length() - 2)[::-1]:
        for m in list(planes):
            planes[m | 1 << bit] = swap(planes[m], "pre", 1 << bit)
    columns = [slots[i * RANK : (i + 1) * RANK] for i in range(n_row)]
    own = (hidden_in, frozen_query_base, cotangent)
    for bit in range(n_row.bit_length() - 1):
        moved = [i for i in range(n_row) if i >> bit & 1]
        got = swap(jnp.concatenate([columns[i] for i in moved]), "row", 1 << bit)
        if bit == 0:
            got, planes[far_plane] = lax.optimization_barrier((got, planes[far_plane]))
        if bit == 1:
            got, own = lax.optimization_barrier((got, own))
        for k, i in enumerate(moved):
            columns[i] = got[k * RANK : (k + 1) * RANK]
    planes = [planes[j] for j in range(1, n_pre)]
    planes, columns = lax.optimization_barrier((planes, jnp.concatenate(columns)))
    masks = jnp.stack(
        [tree_mask]
        + [plane[2 * part_rows : 2 * part_rows + students, :blocks].astype(jnp.int32) for plane in planes]
    )
    first = lax.axis_index("pre") % n_slots * slot_tokens
    hid, base, cot = (lax.dynamic_slice_in_dim(x, first, slot_tokens, 0) for x in own)
    up = up_weight_matrix
    queries, latent_t = pl.pallas_call(
        functools.partial(query_kernel, n_row, tokens),
        out_shape=[
            jax.ShapeDtypeStruct((slot_tokens, width), bf16),
            jax.ShapeDtypeStruct((RANK, slot_tokens), bf16),
        ],
        in_specs=[SMEM] + [VMEM] * 4,
        out_specs=[VMEM] * 2,
        compiler_params=params(16),
        name="queries",
    )(adapter_ids, hid, base, up, columns)

    rows = heads * slot_tokens
    state = [jax.ShapeDtypeStruct((rows, c), f32) for c in (HD, HD, 3 * HD)]

    def attention(group, first, last, operands, in_specs, out_shape, scratch):
        sources, places = [], []
        for a, i, place in group:
            for array, _ in place:
                if not any(array is other for other in sources):
                    sources.append(array)
            index = [[array is other for other in sources].index(True) for array, _ in place]
            places.append((a, i, [(n, begin) for n, (_, begin) in zip(index, place)]))
        keys = len(places) * (n_pre - 1) * part_rows // 2 + (local_keys if first else 0)
        return pl.pallas_call(
            functools.partial(
                attention_kernel, n_pre, drop, part_rows, places, len(sources), first, last, tokens
            ),
            out_shape=out_shape,
            in_specs=[SMEM, VMEM, VMEM] + in_specs + [VMEM] * len(sources),
            out_specs=[VMEM] * len(out_shape),
            scratch_shapes=[
                pltpu.VMEM((keys, 2 * HD), bf16),
                pltpu.VMEM((rows, HD), bf16),
                pltpu.VMEM((rows, HD), bf16),
            ]
            + scratch,
            compiler_params=params(24 + keys * HD * 8 // MIB),
            cost_estimate=pl.CostEstimate(
                flops=4 * rows * keys * HD, bytes_accessed=keys * HD * 4, transcendentals=rows * keys // 2
            ),
            name="first_keys" if first else "last_keys" if last else "next_keys",
        )(masks, queries, cot, *operands, *sources)

    far = list(range(max(drop, 1), n_row.bit_length() - 1))[::-1]
    turn = len(far) // 2
    core = [0] if drop == 0 else []
    orders = [far + core, far[turn:] + far[:turn] + core]
    rounds = len(orders[0])
    away_rows = (n_pre - 1) * part_rows
    parts = [
        {0: jnp.concatenate([plane[a * part_rows : (a + 1) * part_rows] for plane in planes])}
        for a in range(2)
    ]
    groups = [[], [], []]
    for a in range(2):
        groups[0].append((a, 0, [(plane, a * part_rows) for plane in planes]))
    for k in range(rounds):
        got = [
            swap(jnp.concatenate(list(parts[a].values())), "row", 1 << orders[a][k]) for a in range(2)
        ]
        if k == rounds - 3:
            got, (queries, latent_t) = lax.optimization_barrier((got, (queries, latent_t)))
        if k == rounds - 2:
            held = attention(groups[0], True, False, (k_prefix, v_prefix), [VMEM] * 2, state, [])
            got, held = lax.optimization_barrier((got, held))
        for a in range(2):
            for n, m in enumerate(list(parts[a])):
                moved = m | 1 << orders[a][k]
                parts[a][moved] = got[a][n * away_rows : (n + 1) * away_rows]
                place = [(got[a], n * away_rows + j * part_rows) for j in range(n_pre - 1)]
                groups[max(0, k + 3 - rounds)].append((a, moved >> drop, place))
    held = attention(groups[1], False, False, held, [VMEM] * 3, state, [])
    attended, sent = attention(
        groups[2],
        False,
        True,
        (*held, adapter_ids, latent_t, up),
        [VMEM] * 3 + [SMEM] + [VMEM] * 2,
        [
            jax.ShapeDtypeStruct((slot_tokens, width), bf16),
            jax.ShapeDtypeStruct((RANK, width + slot_tokens), bf16),
        ],
        [pltpu.VMEM(s.shape, s.dtype) for s in state] + [pltpu.VMEM((slot_tokens, width), bf16)],
    )

    far_slot = n_slots >> 1
    attended_parts = {far_slot: swap(attended, "pre", far_slot)}
    shared = [swap(sent, "pre", j) for j in range(n_slots)]

    pairs = n_row // 2
    even, odd = pl.pallas_call(
        functools.partial(down_kernel, n_slots, n_row, width),
        out_shape=[jax.ShapeDtypeStruct((pairs * RANK, depth + width), bf16)] * 2,
        in_specs=[VMEM] * (n_slots + 1),
        out_specs=[VMEM] * 2,
        compiler_params=params(16),
        name="down",
    )(*shared, hidden_in)
    odd = swap(odd, "row", 1)
    spans = [slice(m * RANK, (m + 1) * RANK) for m in range(pairs)]
    pieces = [swap(jnp.concatenate([even[at], odd[at]]), "row", 2 * m) for m, at in enumerate(spans)]

    attended_parts[0] = attended
    pieces, attended_parts[far_slot] = lax.optimization_barrier((pieces, attended_parts[far_slot]))
    for bit in range(n_slots.bit_length() - 2)[::-1]:
        for m in list(attended_parts):
            attended_parts[m | 1 << bit] = swap(attended_parts[m], "pre", 1 << bit)

    grad_a, up_weight_gradient = pl.pallas_call(
        functools.partial(finish_kernel, n_row, tokens),
        out_shape=[
            jax.ShapeDtypeStruct((depth, rank_cols), f32),
            jax.ShapeDtypeStruct((rank_cols, width), f32),
        ],
        in_specs=[SMEM] + [VMEM] * pairs,
        out_specs=[VMEM] * 2,
        scratch_shapes=[pltpu.VMEM((rank_cols, depth), f32)],
        compiler_params=params(16),
        name="finish",
    )(adapter_ids, *pieces)

    attended = pl.pallas_call(
        functools.partial(place_kernel, n_slots),
        out_shape=jax.ShapeDtypeStruct((tokens, width), bf16),
        in_specs=[VMEM] * n_slots,
        out_specs=HBM,
        scratch_shapes=[pltpu.SemaphoreType.DMA((n_slots,))],
        compiler_params=params(16),
        cost_estimate=pl.CostEstimate(
            flops=100 * tokens * width * HD, bytes_accessed=100 * tokens * width, transcendentals=0
        ),
        name="place",
    )(*(attended_parts[j] for j in range(n_slots)))
    return attended, grad_a, up_weight_gradient


def solution(mesh):
    in_specs = (
        P("row", None),
        P("row", None),
        P("pre", None),
        P("pre", None),
        P(None, "pre"),
        P(),
        P("row", None),
        P(),
        P("row", None),
    )
    out_specs = (P("row", None), P("row", None), P())
    return jax.shard_map(shards, mesh=mesh, in_specs=in_specs, out_specs=out_specs, check_vma=False)
```

```python
import functools
import math

import jax
import jax.numpy as jnp
from jax import lax
from jax.experimental import pallas as pl
from jax.experimental.pallas import tpu as pltpu
from jax.sharding import PartitionSpec as P

HD = 128
RANK = 16
CONT = 512
MB = 128
CHUNK = 512
ROW_TILE = 128
MIN_TOKENS = 16
ADAPTER_SCALE = 2.0
VERY_LOW = -1e30
LOG2E = 1.4426950408889634
MIB = 1 << 20

NT = (((1,), (1,)), ((), ()))
VMEM = pl.BlockSpec(memory_space=pltpu.VMEM)
SMEM = pl.BlockSpec(memory_space=pltpu.SMEM)
HBM = pl.BlockSpec(memory_space=pltpu.HBM)


def dot(a, b):
    return jnp.dot(a, b, preferred_element_type=jnp.float32)


def dot_nt(a, b):
    return lax.dot_general(a, b, NT, preferred_element_type=jnp.float32)


def swap(x, axis, mask):
    if mask == 0:
        return x
    return lax.ppermute(x, axis, [(s, s ^ mask) for s in range(lax.axis_size(axis))])


def params(mib):
    return pltpu.CompilerParams(vmem_limit_bytes=mib * MIB)


def adapter_of(ids, row, tokens):
    return pl.multiple_of(ids[row * tokens // CONT] * RANK, RANK)


def slot_of(slot_tokens, n_slots, offset=0):
    slot = lax.rem(lax.axis_index("pre"), n_slots) ^ offset
    return pl.ds(pl.multiple_of(slot * slot_tokens, slot_tokens), slot_tokens)


def fetch(pairs, sems):
    copies = [pltpu.make_async_copy(src, dst, sems.at[i]) for i, (src, dst) in enumerate(pairs)]
    for copy in copies:
        copy.start()
    return copies


def mask_rows(mask):
    return -(-mask.shape[0] // 16) * 16


def away_kernel(drop, part_rows, k_ref, v_ref, mask_ref, away_ref, mask_in, sems):
    half = part_rows // 2
    begin = (lax.axis_index("row") >> drop) * part_rows
    pairs = [(mask_ref, mask_in)]
    for a in range(2):
        span = pl.ds(pl.multiple_of(begin + a * half, half), half)
        pairs.append((k_ref.at[span, :], away_ref.at[pl.ds(2 * a * half, half), :]))
        pairs.append((v_ref.at[span, :], away_ref.at[pl.ds((2 * a + 1) * half, half), :]))
    copies = fetch(pairs, sems)
    students, blocks = mask_in.shape
    copies[0].wait()
    away_ref[2 * part_rows :, :] = jnp.zeros_like(away_ref[2 * part_rows :, :])
    away_ref[2 * part_rows : 2 * part_rows + students, :blocks] = mask_in[...].astype(jnp.bfloat16)
    for copy in copies[1:]:
        copy.wait()


def pick_kernel(n_row, tokens, ids_ref, a_ref, slots_ref, ids, a_in, at, sems):
    row = lax.axis_index("row")
    cols = a_ref.shape[0] // (2 * HD)
    copies = fetch([(ids_ref, ids), (a_ref, a_in)], sems)
    copies[1].wait()
    at[...] = a_in[...].astype(jnp.float32).T
    copies[0].wait()
    for i in range(n_row):
        piece = at[pl.ds(adapter_of(ids, row ^ i, tokens), RANK), :].astype(jnp.bfloat16)
        for half in range(2):
            for c in range(cols):
                first = ((half * n_row + i) * cols + c) * RANK
                lane = (half * cols + c) * HD
                slots_ref[first : first + RANK, :] = piece[:, lane : lane + HD]


def query_kernel(n_row, tokens, ids, hid, base, up_ref, low, high, q_ref, latt_ref):
    row = lax.axis_index("row")
    slot_tokens = q_ref.shape[0]
    cols = low.shape[0] // (n_row * RANK)
    span = cols * HD
    latent = jnp.zeros((slot_tokens, RANK), jnp.float32)
    latent_t = jnp.zeros((RANK, slot_tokens), jnp.float32)
    for i in range(n_row):
        for half, ref in enumerate((low, high)):
            firsts = [(i * cols + c) * RANK for c in range(cols)]
            piece = jnp.concatenate([ref[first : first + RANK, :] for first in firsts], axis=1)
            block = hid[:, pl.ds(pl.multiple_of(((row ^ i) * 2 + half) * span, span), span)]
            latent += dot_nt(block, piece)
            latent_t += dot_nt(piece, block)
    latt_ref[...] = latent_t.astype(jnp.bfloat16)
    up = up_ref[pl.ds(adapter_of(ids, row, tokens), RANK), :]
    raised = dot(latent.astype(jnp.bfloat16), up)
    q_ref[...] = (base[...].astype(jnp.float32) + ADAPTER_SCALE * raised).astype(jnp.bfloat16)


def attention_kernel(n_pre, drop, part_rows, places, n_sources, first, last, tokens, *refs):
    masks, q_ref, cot_ref = refs[:3]
    refs = refs[3:]
    if first:
        k_own, v_own, refs = refs[0], refs[1], refs[2:]
    else:
        held, refs = refs[:3], refs[3:]
    if last:
        ids, latt_ref, up_ref, refs = *refs[:3], refs[3:]
    sources, refs = refs[:n_sources], refs[n_sources:]
    if last:
        att_ref, sent_ref, kv, q, cot, top, total, acc, grads = refs
    else:
        top, total, acc, kv, q, cot = refs
    row = lax.axis_index("row")
    slot_tokens, width = q_ref.shape
    heads = width // HD
    rows = heads * slot_tokens
    tile = min(ROW_TILE, rows)
    scale = 1.0 / math.sqrt(HD)
    factor = scale * LOG2E

    student = row * tokens // CONT
    half = part_rows // 2
    unit = min(MB, half)

    def keep(count, live, key_block, value_block):
        @pl.when(live)
        def _():
            at = pl.ds(pl.multiple_of(count * unit, unit), unit)
            kv[at, :HD] = value_block()
            kv[at, HD:] = key_block()

        return count + live.astype(jnp.int32)

    def own_block(b, count):
        at = pl.ds(pl.multiple_of(b * unit, unit), unit)
        live = masks[0, student, b * unit // MB] > 0
        return keep(count, live, lambda: k_own[at, :], lambda: v_own[at, :])

    def block_of(source, begin):
        return lambda: sources[source][begin : begin + unit, :]

    count = jnp.int32(0)
    if first:
        count = lax.fori_loop(0, k_own.shape[0] // unit, own_block, count)
    for a, i, place in places:
        piece = (row >> drop) ^ i
        for j in range(1, n_pre):
            source, begin = place[j - 1]
            for u in range(half // unit):
                block = (piece * part_rows + a * half + u * unit) // MB
                count = keep(
                    count,
                    masks[j, student, block] > 0,
                    block_of(source, begin + u * unit),
                    block_of(source, begin + half + u * unit),
                )

    for h in range(heads):
        at = pl.ds(h * slot_tokens, slot_tokens)
        q[at, :] = q_ref[:, h * HD : (h + 1) * HD]
        cot[at, :] = cot_ref[:, h * HD : (h + 1) * HD]
    if first:
        top[...] = jnp.full_like(top, VERY_LOW)
        total[...] = jnp.zeros_like(total)
        acc[...] = jnp.zeros_like(acc)
    else:
        for ref, given in zip((top, total, acc), held):
            ref[...] = given[...]

    def step(begin, size):
        both = kv[pl.ds(pl.multiple_of(begin, unit), size), :]
        values, keys = both[:, :HD], both[:, HD:]
        lane = min(size, HD)
        lanes = size // lane
        for r0 in range(0, rows, tile):
            at = pl.ds(r0, tile)
            scores = dot_nt(q[at, :], keys)
            old = top[at, :]
            new = jnp.maximum(old, jnp.max(scores, axis=1, keepdims=True))
            top[at, :] = new
            weights = jnp.exp2((scores - jnp.concatenate([new[:, :lane]] * lanes, axis=1)) * factor)
            shrink = jnp.exp2((old - new) * factor)
            partial = weights[:, :lane]
            for c in range(1, lanes):
                partial = partial + weights[:, c * lane : (c + 1) * lane]
            total[at, :] *= shrink
            total[at, :lane] += partial
            grad_weights = (weights * dot_nt(cot[at, :], values)).astype(jnp.bfloat16)
            first_two = dot(weights.astype(jnp.bfloat16), both)
            last = dot(grad_weights, keys)
            acc[at, :HD] = acc[at, :HD] * shrink + first_two[:, :HD]
            acc[at, HD : 2 * HD] = acc[at, HD : 2 * HD] * shrink + first_two[:, HD:]
            acc[at, 2 * HD :] = acc[at, 2 * HD :] * shrink + last

    per_chunk = CHUNK // unit
    full = count // per_chunk

    def full_step(c, carry):
        step(c * CHUNK, CHUNK)
        return carry

    lax.fori_loop(0, full, full_step, 0)
    rest = count * unit - full * CHUNK
    for blocks in range(1, CHUNK // MB):
        pl.when(rest // MB == blocks)(functools.partial(step, full * CHUNK, blocks * MB))
    if unit < MB:
        pl.when(rest % MB > 0)(functools.partial(step, (count - 1) * unit, unit))
    if not last:
        return

    for h in range(heads):
        at = pl.ds(h * slot_tokens, slot_tokens)
        inverse = 1.0 / jnp.sum(total[at, :], axis=1, keepdims=True)
        attended = (acc[at, :HD] * inverse).astype(jnp.bfloat16)
        att_ref[:, h * HD : (h + 1) * HD] = attended
        delta = jnp.sum(
            cot[at, :].astype(jnp.float32) * attended.astype(jnp.float32), axis=1, keepdims=True
        )
        grad = (acc[at, 2 * HD :] - delta * acc[at, HD : 2 * HD]) * (inverse * scale)
        grads[:, h * HD : (h + 1) * HD] = grad.astype(jnp.bfloat16)
    query_gradient = grads[...]
    up = up_ref[pl.ds(adapter_of(ids, row, tokens), RANK), :]
    sent_ref[:, :width] = (ADAPTER_SCALE * dot(latt_ref[...], query_gradient)).astype(jnp.bfloat16)
    sent_ref[:, width:] = (ADAPTER_SCALE * dot_nt(up, query_gradient)).astype(jnp.bfloat16)


def down_kernel(n_slots, n_row, width, *refs):
    parts, hidden, even_ref, odd_ref = refs[:n_slots], refs[n_slots], *refs[n_slots + 1 :]
    row = lax.axis_index("row")
    depth = even_ref.shape[1] - width
    slot_tokens = parts[0].shape[1] - width
    up = parts[0][:, :width].astype(jnp.float32)
    for part in parts[1:]:
        up = up + part[:, :width].astype(jnp.float32)
    up = up.astype(jnp.bfloat16)
    slots = [slot_of(slot_tokens, n_slots, j) for j in range(n_slots)]
    for i in range(n_row):
        out = odd_ref if i & 1 else even_ref
        rows = slice((i >> 1) * RANK, ((i >> 1) + 1) * RANK)
        cols = pl.ds(pl.multiple_of((row ^ i) * depth, depth), depth)
        grad = jnp.zeros((RANK, depth), jnp.float32)
        for j in range(n_slots):
            grad += dot(parts[j][:, width:], hidden[slots[j], cols])
        out[rows, :depth] = grad.astype(jnp.bfloat16)
        out[rows, depth:] = up


def finish_kernel(n_row, tokens, ids, *refs):
    pairs, (down_ref, up_ref, down) = refs[: n_row // 2], refs[n_row // 2 :]
    row = lax.axis_index("row")
    depth = down.shape[1]
    down[...] = jnp.zeros_like(down)
    up_ref[...] = jnp.zeros_like(up_ref)
    for i in range(n_row):
        at = pl.ds(adapter_of(ids, row ^ i, tokens), RANK)
        part = pairs[i >> 1][(i & 1) * RANK : ((i & 1) + 1) * RANK, :]
        down[at, :] += part[:, :depth].astype(jnp.float32)
        up_ref[at, :] += part[:, depth:].astype(jnp.float32)
    down_ref[...] = down[...].T


def place_kernel(n_slots, *refs):
    parts, out, sems = refs[:n_slots], *refs[n_slots:]
    slot_tokens = parts[0].shape[0]
    for copy in fetch(
        [(parts[j], out.at[slot_of(slot_tokens, n_slots, j), :]) for j in range(n_slots)], sems
    ):
        copy.wait()


def shards(
    hidden_in,
    frozen_query_base,
    k_prefix,
    v_prefix,
    tree_mask,
    adapter_ids,
    a_down,
    up_weight_matrix,
    cotangent,
):
    tokens, model = hidden_in.shape
    width = frozen_query_base.shape[1]
    heads = width // HD
    depth, rank_cols = a_down.shape
    local_keys = k_prefix.shape[0]
    n_pre, n_row = lax.axis_size("pre"), lax.axis_size("row")
    n_slots = min(n_pre, tokens // MIN_TOKENS)
    slot_tokens = tokens // n_slots
    bf16, f32 = jnp.bfloat16, jnp.float32
    slices = min(n_row, local_keys // MB)
    drop = (n_row // slices).bit_length() - 1
    part_rows = local_keys // slices
    students, blocks = tree_mask.shape

    away = pl.pallas_call(
        functools.partial(away_kernel, drop, part_rows),
        out_shape=jax.ShapeDtypeStruct((2 * part_rows + mask_rows(tree_mask), HD), bf16),
        in_specs=[HBM] * 3,
        out_specs=VMEM,
        scratch_shapes=[pltpu.VMEM((students, blocks), jnp.int32), pltpu.SemaphoreType.DMA((5,))],
        compiler_params=params(56),
        name="away",
    )(k_prefix, v_prefix, tree_mask)

    away, a_down = lax.optimization_barrier((away, a_down))
    slots = pl.pallas_call(
        functools.partial(pick_kernel, n_row, tokens),
        out_shape=jax.ShapeDtypeStruct((n_row * RANK * depth // HD, HD), bf16),
        in_specs=[HBM] * 2,
        out_specs=VMEM,
        scratch_shapes=[
            pltpu.SMEM(adapter_ids.shape, jnp.int32),
            pltpu.VMEM((depth, rank_cols), bf16),
            pltpu.VMEM((rank_cols, depth), f32),
            pltpu.SemaphoreType.DMA((2,)),
        ],
        compiler_params=params(56),
        name="pick",
    )(adapter_ids, a_down)
    far_plane = n_pre >> 1
    planes = {far_plane: swap(away, "pre", far_plane)}
    planes[0], slots = lax.optimization_barrier((away, slots))
    for bit in range(n_pre.bit_length() - 2)[::-1]:
        for m in list(planes):
            planes[m | 1 << bit] = swap(planes[m], "pre", 1 << bit)
    far = list(range(max(drop, 1), n_row.bit_length() - 1))[::-1]
    turn = len(far) // 2
    orders = [order + ([0] if drop == 0 else []) for order in (far, far[turn:] + far[:turn])]

    piece_rows = depth // (2 * HD) * RANK
    columns = [
        [slots[(a * n_row + i) * piece_rows : (a * n_row + i + 1) * piece_rows] for i in range(n_row)]
        for a in range(2)
    ]

    def moved(bit):
        return [i for i in range(n_row) if i >> bit & 1]

    def put(a, bit, got):
        for n, i in enumerate(moved(bit)):
            columns[a][i] = got[n * piece_rows : (n + 1) * piece_rows]

    core = moved(0)
    got = swap(jnp.concatenate([columns[a][i] for a in range(2) for i in core]), "row", 1)
    got, planes[far_plane] = lax.optimization_barrier((got, planes[far_plane]))
    put(0, 0, got[: len(core) * piece_rows])
    put(1, 0, got[len(core) * piece_rows :])
    for a in range(2):
        for bit in range(1, n_row.bit_length() - 1):
            if bit != orders[a][0]:
                put(a, bit, swap(jnp.concatenate([columns[a][i] for i in moved(bit)]), "row", 1 << bit))
    planes = [planes[j] for j in range(1, n_pre)]
    planes, columns = lax.optimization_barrier((planes, columns))
    masks = jnp.stack(
        [tree_mask]
        + [plane[2 * part_rows : 2 * part_rows + students, :blocks].astype(jnp.int32) for plane in planes]
    )

    first = lax.axis_index("pre") % n_slots * slot_tokens
    hid, base, cot = (lax.dynamic_slice_in_dim(x, first, slot_tokens, 0) for x in (hidden_in, frozen_query_base, cotangent))
    up = up_weight_matrix
    rows = heads * slot_tokens
    state = [jax.ShapeDtypeStruct((rows, c), f32) for c in (HD, HD, 3 * HD)]

    def attention(group, first, last, operands, in_specs, out_shape, scratch):
        sources, places = [], []
        for a, i, place in group:
            for array, _ in place:
                if not any(array is other for other in sources):
                    sources.append(array)
            index = [[array is other for other in sources].index(True) for array, _ in place]
            places.append((a, i, [(n, begin) for n, (_, begin) in zip(index, place)]))
        keys = len(places) * (n_pre - 1) * part_rows // 2 + (local_keys if first else 0)
        return pl.pallas_call(
            functools.partial(
                attention_kernel, n_pre, drop, part_rows, places, len(sources), first, last, tokens
            ),
            out_shape=out_shape,
            in_specs=[SMEM, VMEM, VMEM] + in_specs + [VMEM] * len(sources),
            out_specs=[VMEM] * len(out_shape),
            scratch_shapes=[
                pltpu.VMEM((keys, 2 * HD), bf16),
                pltpu.VMEM((rows, HD), bf16),
                pltpu.VMEM((rows, HD), bf16),
            ]
            + scratch,
            compiler_params=params(24 + keys * HD * 8 // MIB),
            cost_estimate=pl.CostEstimate(
                flops=4 * rows * keys * HD, bytes_accessed=keys * HD * 4, transcendentals=rows * keys // 2
            ),
            name="first_keys" if first else "last_keys" if last else "next_keys",
        )(masks, queries, cot, *operands, *sources)

    rounds = len(orders[0])
    away_rows = (n_pre - 1) * part_rows
    parts = [
        {0: jnp.concatenate([plane[a * part_rows : (a + 1) * part_rows] for plane in planes])}
        for a in range(2)
    ]
    groups = [[], [], []]
    for a in range(2):
        groups[0].append((a, 0, [(plane, a * part_rows) for plane in planes]))
    for k in range(rounds):
        got = []
        for a in range(2):
            bit = orders[a][k]
            payload = list(parts[a].values())
            if k == 0:
                payload += [columns[a][i] for i in moved(bit)]
            got.append(swap(jnp.concatenate(payload), "row", 1 << bit))
            if k == 0:
                put(a, bit, got[a][away_rows:])
        if k == 0:
            queries, latent_t = pl.pallas_call(
                functools.partial(query_kernel, n_row, tokens),
                out_shape=[
                    jax.ShapeDtypeStruct((slot_tokens, width), bf16),
                    jax.ShapeDtypeStruct((RANK, slot_tokens), bf16),
                ],
                in_specs=[SMEM] + [VMEM] * 5,
                out_specs=[VMEM] * 2,
                compiler_params=params(16),
                name="queries",
            )(adapter_ids, hid, base, up, *(jnp.concatenate(c) for c in columns))
        if k == rounds - 2:
            held = attention(groups[0], True, False, (k_prefix, v_prefix), [VMEM] * 2, state, [])
            got, held = lax.optimization_barrier((got, held))
        for a in range(2):
            for n, m in enumerate(list(parts[a])):
                there = m | 1 << orders[a][k]
                parts[a][there] = got[a][n * away_rows : (n + 1) * away_rows]
                place = [(got[a], n * away_rows + j * part_rows) for j in range(n_pre - 1)]
                groups[max(0, k + 3 - rounds)].append((a, there >> drop, place))
    held = attention(groups[1], False, False, held, [VMEM] * 3, state, [])
    attended, sent = attention(
        groups[2],
        False,
        True,
        (*held, adapter_ids, latent_t, up),
        [VMEM] * 3 + [SMEM] + [VMEM] * 2,
        [
            jax.ShapeDtypeStruct((slot_tokens, width), bf16),
            jax.ShapeDtypeStruct((RANK, width + slot_tokens), bf16),
        ],
        [pltpu.VMEM(s.shape, s.dtype) for s in state] + [pltpu.VMEM((slot_tokens, width), bf16)],
    )

    far_slot = n_slots >> 1
    attended_parts = {far_slot: swap(attended, "pre", far_slot)}
    shared = [swap(sent, "pre", j) for j in range(n_slots)]

    pairs = n_row // 2
    even, odd = pl.pallas_call(
        functools.partial(down_kernel, n_slots, n_row, width),
        out_shape=[jax.ShapeDtypeStruct((pairs * RANK, depth + width), bf16)] * 2,
        in_specs=[VMEM] * (n_slots + 1),
        out_specs=[VMEM] * 2,
        compiler_params=params(16),
        name="down",
    )(*shared, hidden_in)
    odd = swap(odd, "row", 1)
    spans = [slice(m * RANK, (m + 1) * RANK) for m in range(pairs)]
    pieces = [swap(jnp.concatenate([even[at], odd[at]]), "row", 2 * m) for m, at in enumerate(spans)]

    attended_parts[0] = attended
    pieces, attended_parts[far_slot] = lax.optimization_barrier((pieces, attended_parts[far_slot]))
    for bit in range(n_slots.bit_length() - 2)[::-1]:
        for m in list(attended_parts):
            attended_parts[m | 1 << bit] = swap(attended_parts[m], "pre", 1 << bit)

    grad_a, up_weight_gradient = pl.pallas_call(
        functools.partial(finish_kernel, n_row, tokens),
        out_shape=[
            jax.ShapeDtypeStruct((depth, rank_cols), f32),
            jax.ShapeDtypeStruct((rank_cols, width), f32),
        ],
        in_specs=[SMEM] + [VMEM] * pairs,
        out_specs=[VMEM] * 2,
        scratch_shapes=[pltpu.VMEM((rank_cols, depth), f32)],
        compiler_params=params(16),
        name="finish",
    )(adapter_ids, *pieces)

    attended = pl.pallas_call(
        functools.partial(place_kernel, n_slots),
        out_shape=jax.ShapeDtypeStruct((tokens, width), bf16),
        in_specs=[VMEM] * n_slots,
        out_specs=HBM,
        scratch_shapes=[pltpu.SemaphoreType.DMA((n_slots,))],
        compiler_params=params(16),
        cost_estimate=pl.CostEstimate(
            flops=100 * tokens * width * HD, bytes_accessed=100 * tokens * width, transcendentals=0
        ),
        name="place",
    )(*(attended_parts[j] for j in range(n_slots)))
    return attended, grad_a, up_weight_gradient


def solution(mesh):
    in_specs = (
        P("row", None),
        P("row", None),
        P("pre", None),
        P("pre", None),
        P(None, "pre"),
        P(),
        P("row", None),
        P(),
        P("row", None),
    )
    out_specs = (P("row", None), P("row", None), P())
    return jax.shard_map(shards, mesh=mesh, in_specs=in_specs, out_specs=out_specs, check_vma=False)
```

```python
import functools
import math

import jax
import jax.numpy as jnp
from jax import lax
from jax.experimental import pallas as pl
from jax.experimental.pallas import tpu as pltpu
from jax.sharding import PartitionSpec as P

HD = 128
RANK = 16
CONT = 512
MB = 128
CHUNK = 1024
ROW_TILE = 1024
MIN_TOKENS = 16
ADAPTER_SCALE = 2.0
VERY_LOW = -1e30
LOG2E = 1.4426950408889634
MIB = 1 << 20

NT = (((1,), (1,)), ((), ()))
VMEM = pl.BlockSpec(memory_space=pltpu.VMEM)
SMEM = pl.BlockSpec(memory_space=pltpu.SMEM)
HBM = pl.BlockSpec(memory_space=pltpu.HBM)


def dot(a, b):
    return jnp.dot(a, b, preferred_element_type=jnp.float32)


def dot_nt(a, b):
    return lax.dot_general(a, b, NT, preferred_element_type=jnp.float32)


def swap(x, axis, mask):
    if mask == 0:
        return x
    return lax.ppermute(x, axis, [(s, s ^ mask) for s in range(lax.axis_size(axis))])


def params(mib):
    return pltpu.CompilerParams(vmem_limit_bytes=mib * MIB)


def adapter_of(ids, row, tokens):
    return pl.multiple_of(ids[row * tokens // CONT] * RANK, RANK)


def slot_of(slot_tokens, n_slots, offset=0):
    slot = lax.rem(lax.axis_index("pre"), n_slots) ^ offset
    return pl.ds(pl.multiple_of(slot * slot_tokens, slot_tokens), slot_tokens)


def fetch(pairs, sems):
    copies = [pltpu.make_async_copy(src, dst, sems.at[i]) for i, (src, dst) in enumerate(pairs)]
    for copy in copies:
        copy.start()
    return copies


def mask_rows(mask):
    return -(-mask.shape[0] // 16) * 16


def away_kernel(drop, part_rows, k_ref, v_ref, mask_ref, away_ref, mask_in, sems):
    half = part_rows // 2
    begin = (lax.axis_index("row") >> drop) * part_rows
    pairs = [(mask_ref, mask_in)]
    for a in range(2):
        span = pl.ds(pl.multiple_of(begin + a * half, half), half)
        pairs.append((k_ref.at[span, :], away_ref.at[pl.ds(2 * a * half, half), :]))
        pairs.append((v_ref.at[span, :], away_ref.at[pl.ds((2 * a + 1) * half, half), :]))
    copies = fetch(pairs, sems)
    students, blocks = mask_in.shape
    copies[0].wait()
    away_ref[2 * part_rows :, :] = jnp.zeros_like(away_ref[2 * part_rows :, :])
    away_ref[2 * part_rows : 2 * part_rows + students, :blocks] = mask_in[...].astype(jnp.bfloat16)
    for copy in copies[1:]:
        copy.wait()


def pick_kernel(n_row, tokens, ids, a_ref, slots_ref, at):
    row = lax.axis_index("row")
    cols = a_ref.shape[0] // (2 * HD)
    at[...] = a_ref[...].astype(jnp.float32).T
    for i in range(n_row):
        piece = at[pl.ds(adapter_of(ids, row ^ i, tokens), RANK), :].astype(jnp.bfloat16)
        for half in range(2):
            for c in range(cols):
                first = ((half * n_row + i) * cols + c) * RANK
                lane = (half * cols + c) * HD
                slots_ref[first : first + RANK, :] = piece[:, lane : lane + HD]


def query_kernel(n_row, tokens, ids, hid, base, up_ref, low, high, q_ref, latt_ref):
    row = lax.axis_index("row")
    slot_tokens = q_ref.shape[0]
    cols = low.shape[0] // (n_row * RANK)
    span = cols * HD
    latent = jnp.zeros((slot_tokens, RANK), jnp.float32)
    latent_t = jnp.zeros((RANK, slot_tokens), jnp.float32)
    for i in range(n_row):
        for half, ref in enumerate((low, high)):
            firsts = [(i * cols + c) * RANK for c in range(cols)]
            piece = jnp.concatenate([ref[first : first + RANK, :] for first in firsts], axis=1)
            block = hid[:, pl.ds(pl.multiple_of(((row ^ i) * 2 + half) * span, span), span)]
            latent += dot_nt(block, piece)
            latent_t += dot_nt(piece, block)
    latt_ref[...] = latent_t.astype(jnp.bfloat16)
    up = up_ref[pl.ds(adapter_of(ids, row, tokens), RANK), :]
    raised = dot(latent.astype(jnp.bfloat16), up)
    q_ref[...] = (base[...].astype(jnp.float32) + ADAPTER_SCALE * raised).astype(jnp.bfloat16)


def attention_kernel(n_pre, drop, part_rows, places, n_sources, first, last, tokens, *refs):
    masks, q_ref, cot_ref = refs[:3]
    refs = refs[3:]
    if first:
        k_own, v_own, refs = refs[0], refs[1], refs[2:]
    else:
        held, refs = refs[:3], refs[3:]
    if last:
        ids, latt_ref, up_ref, refs = *refs[:3], refs[3:]
    sources, refs = refs[:n_sources], refs[n_sources:]
    if last:
        att_ref, sent_ref, kv, q, cot, top, total, acc, grads = refs
    else:
        top, total, acc, kv, q, cot = refs
    row = lax.axis_index("row")
    slot_tokens, width = q_ref.shape
    heads = width // HD
    rows = heads * slot_tokens
    tile = min(ROW_TILE, rows)
    scale = 1.0 / math.sqrt(HD)
    factor = scale * LOG2E

    student = row * tokens // CONT
    half = part_rows // 2
    unit = min(MB, half)

    def keep(count, live, key_block, value_block):
        @pl.when(live)
        def _():
            at = pl.ds(pl.multiple_of(count * unit, unit), unit)
            kv[at, :HD] = value_block()
            kv[at, HD:] = key_block()

        return count + live.astype(jnp.int32)

    def own_block(b, count):
        at = pl.ds(pl.multiple_of(b * unit, unit), unit)
        live = masks[0, student, b * unit // MB] > 0
        return keep(count, live, lambda: k_own[at, :], lambda: v_own[at, :])

    def block_of(source, begin):
        return lambda: sources[source][begin : begin + unit, :]

    count = jnp.int32(0)
    if first:
        count = lax.fori_loop(0, k_own.shape[0] // unit, own_block, count)
    for a, i, place in places:
        piece = (row >> drop) ^ i
        for j in range(1, n_pre):
            source, begin = place[j - 1]
            for u in range(half // unit):
                block = (piece * part_rows + a * half + u * unit) // MB
                count = keep(
                    count,
                    masks[j, student, block] > 0,
                    block_of(source, begin + u * unit),
                    block_of(source, begin + half + u * unit),
                )

    for h in range(heads):
        at = pl.ds(h * slot_tokens, slot_tokens)
        q[at, :] = q_ref[:, h * HD : (h + 1) * HD]
        cot[at, :] = cot_ref[:, h * HD : (h + 1) * HD]
    if first:
        top[...] = jnp.full_like(top, VERY_LOW)
        total[...] = jnp.zeros_like(total)
        acc[...] = jnp.zeros_like(acc)
    else:
        for ref, given in zip((top, total, acc), held):
            ref[...] = given[...]

    def step(begin, size):
        both = kv[pl.ds(pl.multiple_of(begin, unit), size), :]
        values, keys = both[:, :HD], both[:, HD:]
        lane = min(size, HD)
        lanes = size // lane
        for r0 in range(0, rows, tile):
            at = pl.ds(r0, tile)
            scores = dot_nt(q[at, :], keys)
            old = top[at, :]
            new = jnp.maximum(old, jnp.max(scores, axis=1, keepdims=True))
            top[at, :] = new
            weights = jnp.exp2((scores - jnp.concatenate([new[:, :lane]] * lanes, axis=1)) * factor)
            shrink = jnp.exp2((old - new) * factor)
            partial = weights[:, :lane]
            for c in range(1, lanes):
                partial = partial + weights[:, c * lane : (c + 1) * lane]
            total[at, :] *= shrink
            total[at, :lane] += partial
            grad_weights = (weights * dot_nt(cot[at, :], values)).astype(jnp.bfloat16)
            first_two = dot(weights.astype(jnp.bfloat16), both)
            last = dot(grad_weights, keys)
            acc[at, :HD] = acc[at, :HD] * shrink + first_two[:, :HD]
            acc[at, HD : 2 * HD] = acc[at, HD : 2 * HD] * shrink + first_two[:, HD:]
            acc[at, 2 * HD :] = acc[at, 2 * HD :] * shrink + last

    per_chunk = CHUNK // unit
    full = count // per_chunk

    def full_step(c, carry):
        step(c * CHUNK, CHUNK)
        return carry

    lax.fori_loop(0, full, full_step, 0)
    size = CHUNK // 2
    while size >= unit:
        done = count // (2 * size // unit) * (2 * size)
        pl.when(count * unit - done >= size)(functools.partial(step, done, size))
        size //= 2
    if not last:
        return

    for h in range(heads):
        at = pl.ds(h * slot_tokens, slot_tokens)
        inverse = 1.0 / jnp.sum(total[at, :], axis=1, keepdims=True)
        attended = (acc[at, :HD] * inverse).astype(jnp.bfloat16)
        att_ref[:, h * HD : (h + 1) * HD] = attended
        delta = jnp.sum(
            cot[at, :].astype(jnp.float32) * attended.astype(jnp.float32), axis=1, keepdims=True
        )
        grad = (acc[at, 2 * HD :] - delta * acc[at, HD : 2 * HD]) * (inverse * scale)
        grads[:, h * HD : (h + 1) * HD] = grad.astype(jnp.bfloat16)
    query_gradient = grads[...]
    up = up_ref[pl.ds(adapter_of(ids, row, tokens), RANK), :]
    sent_ref[:, :width] = (ADAPTER_SCALE * dot(latt_ref[...], query_gradient)).astype(jnp.bfloat16)
    sent_ref[:, width:] = (ADAPTER_SCALE * dot_nt(up, query_gradient)).astype(jnp.bfloat16)


def down_kernel(n_slots, n_row, width, *refs):
    parts, hidden, even_ref, odd_ref = refs[:n_slots], refs[n_slots], *refs[n_slots + 1 :]
    row = lax.axis_index("row")
    depth = even_ref.shape[1] - width
    slot_tokens = parts[0].shape[1] - width
    up = parts[0][:, :width].astype(jnp.float32)
    for part in parts[1:]:
        up = up + part[:, :width].astype(jnp.float32)
    up = up.astype(jnp.bfloat16)
    slots = [slot_of(slot_tokens, n_slots, j) for j in range(n_slots)]
    for i in range(n_row):
        out = odd_ref if i & 1 else even_ref
        rows = slice((i >> 1) * RANK, ((i >> 1) + 1) * RANK)
        cols = pl.ds(pl.multiple_of((row ^ i) * depth, depth), depth)
        grad = jnp.zeros((RANK, depth), jnp.float32)
        for j in range(n_slots):
            grad += dot(parts[j][:, width:], hidden[slots[j], cols])
        out[rows, :depth] = grad.astype(jnp.bfloat16)
        out[rows, depth:] = up


def finish_kernel(n_row, tokens, ids, *refs):
    pairs, (down_ref, up_ref, down) = refs[: n_row // 2], refs[n_row // 2 :]
    row = lax.axis_index("row")
    depth = down.shape[1]
    down[...] = jnp.zeros_like(down)
    up_ref[...] = jnp.zeros_like(up_ref)
    for i in range(n_row):
        at = pl.ds(adapter_of(ids, row ^ i, tokens), RANK)
        part = pairs[i >> 1][(i & 1) * RANK : ((i & 1) + 1) * RANK, :]
        down[at, :] += part[:, :depth].astype(jnp.float32)
        up_ref[at, :] += part[:, depth:].astype(jnp.float32)
    down_ref[...] = down[...].T


def place_kernel(n_slots, *refs):
    parts, out, sems = refs[:n_slots], *refs[n_slots:]
    slot_tokens = parts[0].shape[0]
    for copy in fetch(
        [(parts[j], out.at[slot_of(slot_tokens, n_slots, j), :]) for j in range(n_slots)], sems
    ):
        copy.wait()


def shards(
    hidden_in,
    frozen_query_base,
    k_prefix,
    v_prefix,
    tree_mask,
    adapter_ids,
    a_down,
    up_weight_matrix,
    cotangent,
):
    tokens, model = hidden_in.shape
    width = frozen_query_base.shape[1]
    heads = width // HD
    depth, rank_cols = a_down.shape
    local_keys = k_prefix.shape[0]
    n_pre, n_row = lax.axis_size("pre"), lax.axis_size("row")
    n_slots = min(n_pre, tokens // MIN_TOKENS)
    slot_tokens = tokens // n_slots
    bf16, f32 = jnp.bfloat16, jnp.float32
    slices = min(n_row, local_keys // MB)
    drop = (n_row // slices).bit_length() - 1
    part_rows = local_keys // slices
    students, blocks = tree_mask.shape

    away = pl.pallas_call(
        functools.partial(away_kernel, drop, part_rows),
        out_shape=jax.ShapeDtypeStruct((2 * part_rows + mask_rows(tree_mask), HD), bf16),
        in_specs=[HBM] * 3,
        out_specs=VMEM,
        scratch_shapes=[pltpu.VMEM((students, blocks), jnp.int32), pltpu.SemaphoreType.DMA((5,))],
        compiler_params=params(56),
        name="away",
    )(k_prefix, v_prefix, tree_mask)

    away, a_down = lax.optimization_barrier((away, a_down))
    slots = pl.pallas_call(
        functools.partial(pick_kernel, n_row, tokens),
        out_shape=jax.ShapeDtypeStruct((n_row * RANK * depth // HD, HD), bf16),
        in_specs=[SMEM, VMEM],
        out_specs=VMEM,
        scratch_shapes=[pltpu.VMEM((rank_cols, depth), f32)],
        compiler_params=params(16),
        name="pick",
    )(adapter_ids, a_down)
    far_plane = n_pre >> 1
    planes = {0: away, far_plane: swap(away, "pre", far_plane)}
    for bit in range(n_pre.bit_length() - 2)[::-1]:
        for m in sorted(planes):
            planes[m | 1 << bit] = swap(planes[m], "pre", 1 << bit)
    far = list(range(max(drop, 1), n_row.bit_length() - 1))[::-1]
    turn = len(far) // 2
    orders = [order + ([0] if drop == 0 else []) for order in (far, far[turn:] + far[:turn])]

    piece_rows = depth // (2 * HD) * RANK
    columns = [
        [slots[(a * n_row + i) * piece_rows : (a * n_row + i + 1) * piece_rows] for i in range(n_row)]
        for a in range(2)
    ]

    def moved(bit):
        return [i for i in range(n_row) if i >> bit & 1]

    def put(a, bit, got):
        for n, i in enumerate(moved(bit)):
            columns[a][i] = got[n * piece_rows : (n + 1) * piece_rows]

    core = moved(0)
    got = swap(jnp.concatenate([columns[a][i] for a in range(2) for i in core]), "row", 1)
    got, planes[far_plane] = lax.optimization_barrier((got, planes[far_plane]))
    put(0, 0, got[: len(core) * piece_rows])
    put(1, 0, got[len(core) * piece_rows :])
    for a in range(2):
        for bit in range(1, n_row.bit_length() - 1):
            if bit != orders[a][0]:
                put(a, bit, swap(jnp.concatenate([columns[a][i] for i in moved(bit)]), "row", 1 << bit))
    planes = [planes[j] for j in range(1, n_pre)]
    planes, columns = lax.optimization_barrier((planes, columns))
    masks = jnp.stack(
        [tree_mask]
        + [plane[2 * part_rows : 2 * part_rows + students, :blocks].astype(jnp.int32) for plane in planes]
    )

    first = lax.axis_index("pre") % n_slots * slot_tokens
    hid, base, cot = (lax.dynamic_slice_in_dim(x, first, slot_tokens, 0) for x in (hidden_in, frozen_query_base, cotangent))
    up = up_weight_matrix
    rows = heads * slot_tokens
    state = [jax.ShapeDtypeStruct((rows, c), f32) for c in (HD, HD, 3 * HD)]

    def attention(group, first, last, operands, in_specs, out_shape, scratch):
        sources, places = [], []
        for a, i, place in group:
            for array, _ in place:
                if not any(array is other for other in sources):
                    sources.append(array)
            index = [[array is other for other in sources].index(True) for array, _ in place]
            places.append((a, i, [(n, begin) for n, (_, begin) in zip(index, place)]))
        keys = len(places) * (n_pre - 1) * part_rows // 2 + (local_keys if first else 0)
        return pl.pallas_call(
            functools.partial(
                attention_kernel, n_pre, drop, part_rows, places, len(sources), first, last, tokens
            ),
            out_shape=out_shape,
            in_specs=[SMEM, VMEM, VMEM] + in_specs + [VMEM] * len(sources),
            out_specs=[VMEM] * len(out_shape),
            scratch_shapes=[
                pltpu.VMEM((keys, 2 * HD), bf16),
                pltpu.VMEM((rows, HD), bf16),
                pltpu.VMEM((rows, HD), bf16),
            ]
            + scratch,
            compiler_params=params(24 + keys * HD * 8 // MIB),
            cost_estimate=pl.CostEstimate(
                flops=4 * rows * keys * HD, bytes_accessed=keys * HD * 4, transcendentals=rows * keys // 2
            ),
            name="first_keys" if first else "last_keys" if last else "next_keys",
        )(masks, queries, cot, *operands, *sources)

    rounds = len(orders[0])
    away_rows = (n_pre - 1) * part_rows
    parts = [
        {0: jnp.concatenate([plane[a * part_rows : (a + 1) * part_rows] for plane in planes])}
        for a in range(2)
    ]
    groups = [[], [], []]
    for a in range(2):
        groups[0].append((a, 0, [(plane, a * part_rows) for plane in planes]))
    for k in range(rounds):
        got = []
        for a in range(2):
            bit = orders[a][k]
            payload = list(parts[a].values())
            if k == 0:
                payload += [columns[a][i] for i in moved(bit)]
            got.append(swap(jnp.concatenate(payload), "row", 1 << bit))
            if k == 0:
                put(a, bit, got[a][away_rows:])
        if k == 0:
            queries, latent_t = pl.pallas_call(
                functools.partial(query_kernel, n_row, tokens),
                out_shape=[
                    jax.ShapeDtypeStruct((slot_tokens, width), bf16),
                    jax.ShapeDtypeStruct((RANK, slot_tokens), bf16),
                ],
                in_specs=[SMEM] + [VMEM] * 5,
                out_specs=[VMEM] * 2,
                compiler_params=params(16),
                name="queries",
            )(adapter_ids, hid, base, up, *(jnp.concatenate(c) for c in columns))
        if k == rounds - 2:
            held = attention(groups[0], True, False, (k_prefix, v_prefix), [VMEM] * 2, state, [])
            got, held = lax.optimization_barrier((got, held))
        for a in range(2):
            for n, m in enumerate(list(parts[a])):
                there = m | 1 << orders[a][k]
                parts[a][there] = got[a][n * away_rows : (n + 1) * away_rows]
                place = [(got[a], n * away_rows + j * part_rows) for j in range(n_pre - 1)]
                groups[max(0, k + 3 - rounds)].append((a, there >> drop, place))
    held = attention(groups[1], False, False, held, [VMEM] * 3, state, [])
    attended, sent = attention(
        groups[2],
        False,
        True,
        (*held, adapter_ids, latent_t, up),
        [VMEM] * 3 + [SMEM] + [VMEM] * 2,
        [
            jax.ShapeDtypeStruct((slot_tokens, width), bf16),
            jax.ShapeDtypeStruct((RANK, width + slot_tokens), bf16),
        ],
        [pltpu.VMEM(s.shape, s.dtype) for s in state] + [pltpu.VMEM((slot_tokens, width), bf16)],
    )

    far_slot = n_slots >> 1
    attended_parts = {far_slot: swap(attended, "pre", far_slot)}
    shared = [swap(sent, "pre", j) for j in range(n_slots)]

    pairs = n_row // 2
    even, odd = pl.pallas_call(
        functools.partial(down_kernel, n_slots, n_row, width),
        out_shape=[jax.ShapeDtypeStruct((pairs * RANK, depth + width), bf16)] * 2,
        in_specs=[VMEM] * (n_slots + 1),
        out_specs=[VMEM] * 2,
        compiler_params=params(16),
        name="down",
    )(*shared, hidden_in)
    odd = swap(odd, "row", 1)
    spans = [slice(m * RANK, (m + 1) * RANK) for m in range(pairs)]
    pieces = [swap(jnp.concatenate([even[at], odd[at]]), "row", 2 * m) for m, at in enumerate(spans)]

    attended_parts[0] = attended
    pieces, attended_parts[far_slot] = lax.optimization_barrier((pieces, attended_parts[far_slot]))
    for bit in range(n_slots.bit_length() - 2)[::-1]:
        for m in list(attended_parts):
            attended_parts[m | 1 << bit] = swap(attended_parts[m], "pre", 1 << bit)

    grad_a, up_weight_gradient = pl.pallas_call(
        functools.partial(finish_kernel, n_row, tokens),
        out_shape=[
            jax.ShapeDtypeStruct((depth, rank_cols), f32),
            jax.ShapeDtypeStruct((rank_cols, width), f32),
        ],
        in_specs=[SMEM] + [VMEM] * pairs,
        out_specs=[VMEM] * 2,
        scratch_shapes=[pltpu.VMEM((rank_cols, depth), f32)],
        compiler_params=params(16),
        name="finish",
    )(adapter_ids, *pieces)

    attended = pl.pallas_call(
        functools.partial(place_kernel, n_slots),
        out_shape=jax.ShapeDtypeStruct((tokens, width), bf16),
        in_specs=[VMEM] * n_slots,
        out_specs=HBM,
        scratch_shapes=[pltpu.SemaphoreType.DMA((n_slots,))],
        compiler_params=params(16),
        cost_estimate=pl.CostEstimate(
            flops=100 * tokens * width * HD, bytes_accessed=100 * tokens * width, transcendentals=0
        ),
        name="place",
    )(*(attended_parts[j] for j in range(n_slots)))
    return attended, grad_a, up_weight_gradient


def solution(mesh):
    in_specs = (
        P("row", None),
        P("row", None),
        P("pre", None),
        P("pre", None),
        P(None, "pre"),
        P(),
        P("row", None),
        P(),
        P("row", None),
    )
    out_specs = (P("row", None), P("row", None), P())
    return jax.shard_map(shards, mesh=mesh, in_specs=in_specs, out_specs=out_specs, check_vma=False)
```

```python
import functools
import math

import jax
import jax.numpy as jnp
from jax import lax
from jax.experimental import pallas as pl
from jax.experimental.pallas import tpu as pltpu
from jax.sharding import PartitionSpec as P

HD = 128
RANK = 16
CONT = 512
MB = 128
CHUNK = 512
SUB_ROWS = 64
MIN_TOKENS = 16
ADAPTER_SCALE = 2.0
VERY_LOW = -1e30
LOG2E = 1.4426950408889634
MIB = 1 << 20

NT = (((1,), (1,)), ((), ()))
VMEM = pl.BlockSpec(memory_space=pltpu.VMEM)
SMEM = pl.BlockSpec(memory_space=pltpu.SMEM)
HBM = pl.BlockSpec(memory_space=pltpu.HBM)


def dot(a, b):
    return jnp.dot(a, b, preferred_element_type=jnp.float32)


def dot_nt(a, b):
    return lax.dot_general(a, b, NT, preferred_element_type=jnp.float32)


def swap(x, axis, mask):
    if mask == 0:
        return x
    return lax.ppermute(x, axis, [(s, s ^ mask) for s in range(lax.axis_size(axis))])


def params(mib):
    return pltpu.CompilerParams(vmem_limit_bytes=mib * MIB)


def adapter_of(ids, row, tokens):
    return pl.multiple_of(ids[row * tokens // CONT] * RANK, RANK)


def slot_of(slot_tokens, n_slots, offset=0):
    slot = lax.rem(lax.axis_index("pre"), n_slots) ^ offset
    return pl.ds(pl.multiple_of(slot * slot_tokens, slot_tokens), slot_tokens)


def fetch(pairs, sems):
    copies = [pltpu.make_async_copy(src, dst, sems.at[i]) for i, (src, dst) in enumerate(pairs)]
    for copy in copies:
        copy.start()
    return copies


def mask_rows(mask):
    return -(-mask.shape[0] // 16) * 16


def away_kernel(drop, part_rows, k_ref, v_ref, mask_ref, away_ref, mask_in, sems):
    half = part_rows // 2
    begin = (lax.axis_index("row") >> drop) * part_rows
    pairs = [(mask_ref, mask_in)]
    for a in range(2):
        span = pl.ds(pl.multiple_of(begin + a * half, half), half)
        pairs.append((k_ref.at[span, :], away_ref.at[pl.ds(2 * a * half, half), :]))
        pairs.append((v_ref.at[span, :], away_ref.at[pl.ds((2 * a + 1) * half, half), :]))
    copies = fetch(pairs, sems)
    students, blocks = mask_in.shape
    copies[0].wait()
    away_ref[2 * part_rows :, :] = jnp.zeros_like(away_ref[2 * part_rows :, :])
    away_ref[2 * part_rows : 2 * part_rows + students, :blocks] = mask_in[...].astype(jnp.bfloat16)
    for copy in copies[1:]:
        copy.wait()


def pick_kernel(n_row, tokens, ids, a_ref, slots_ref, at):
    row = lax.axis_index("row")
    cols = a_ref.shape[0] // (2 * HD)
    at[...] = a_ref[...].astype(jnp.float32).T
    for i in range(n_row):
        piece = at[pl.ds(adapter_of(ids, row ^ i, tokens), RANK), :].astype(jnp.bfloat16)
        for half in range(2):
            for c in range(cols):
                first = ((half * n_row + i) * cols + c) * RANK
                lane = (half * cols + c) * HD
                slots_ref[first : first + RANK, :] = piece[:, lane : lane + HD]


def query_kernel(n_row, tokens, ids, hid, base, up_ref, low, high, q_ref, latt_ref):
    row = lax.axis_index("row")
    slot_tokens = q_ref.shape[0]
    cols = low.shape[0] // (n_row * RANK)
    span = cols * HD
    latent = jnp.zeros((slot_tokens, RANK), jnp.float32)
    latent_t = jnp.zeros((RANK, slot_tokens), jnp.float32)
    for i in range(n_row):
        for half, ref in enumerate((low, high)):
            firsts = [(i * cols + c) * RANK for c in range(cols)]
            piece = jnp.concatenate([ref[first : first + RANK, :] for first in firsts], axis=1)
            block = hid[:, pl.ds(pl.multiple_of(((row ^ i) * 2 + half) * span, span), span)]
            latent += dot_nt(block, piece)
            latent_t += dot_nt(piece, block)
    latt_ref[...] = latent_t.astype(jnp.bfloat16)
    up = up_ref[pl.ds(adapter_of(ids, row, tokens), RANK), :]
    raised = dot(latent.astype(jnp.bfloat16), up)
    q_ref[...] = (base[...].astype(jnp.float32) + ADAPTER_SCALE * raised).astype(jnp.bfloat16)


def attention_kernel(n_pre, drop, part_rows, places, n_sources, first, last, tokens, *refs):
    masks, q_ref, cot_ref = refs[:3]
    refs = refs[3:]
    if first:
        k_own, v_own, refs = refs[0], refs[1], refs[2:]
    else:
        held, refs = refs[:3], refs[3:]
    if last:
        ids, latt_ref, up_ref, refs = *refs[:3], refs[3:]
    sources, refs = refs[:n_sources], refs[n_sources:]
    if last:
        att_ref, sent_ref, kv, q, cot, *slots, top, total, acc, grads = refs
    else:
        top, total, acc, kv, q, cot, *slots = refs
    slots = slots[:5], slots[5:]
    row = lax.axis_index("row")
    slot_tokens, width = q_ref.shape
    heads = width // HD
    rows = heads * slot_tokens
    scale = 1.0 / math.sqrt(HD)
    factor = scale * LOG2E

    student = row * tokens // CONT
    half = part_rows // 2
    unit = min(MB, half)

    def keep(count, live, key_block, value_block):
        @pl.when(live)
        def _():
            at = pl.ds(pl.multiple_of(count * unit, unit), unit)
            kv[at, :HD] = value_block()
            kv[at, HD:] = key_block()

        return count + live.astype(jnp.int32)

    def own_block(b, count):
        at = pl.ds(pl.multiple_of(b * unit, unit), unit)
        live = masks[0, student, b * unit // MB] > 0
        return keep(count, live, lambda: k_own[at, :], lambda: v_own[at, :])

    def block_of(source, begin):
        return lambda: sources[source][begin : begin + unit, :]

    count = jnp.int32(0)
    if first:
        count = lax.fori_loop(0, k_own.shape[0] // unit, own_block, count)
    for a, i, place in places:
        piece = (row >> drop) ^ i
        for j in range(1, n_pre):
            source, begin = place[j - 1]
            for u in range(half // unit):
                block = (piece * part_rows + a * half + u * unit) // MB
                count = keep(
                    count,
                    masks[j, student, block] > 0,
                    block_of(source, begin + u * unit),
                    block_of(source, begin + half + u * unit),
                )

    for h in range(heads):
        at = pl.ds(h * slot_tokens, slot_tokens)
        q[at, :] = q_ref[:, h * HD : (h + 1) * HD]
        cot[at, :] = cot_ref[:, h * HD : (h + 1) * HD]
    if first:
        top[...] = jnp.full_like(top, VERY_LOW)
        total[...] = jnp.zeros_like(total)
        acc[...] = jnp.zeros_like(acc)
    else:
        for ref, given in zip((top, total, acc), held):
            ref[...] = given[...]

    def products(begin, size, scores, others):
        both = kv[pl.ds(pl.multiple_of(begin, unit), size), :]
        scores[:, :size] = dot_nt(q[...], both[:, HD:])
        others[:, :size] = dot_nt(cot[...], both[:, :HD])

    def weigh(size, scores, others, weights, grad_weights, shrink):
        lane = min(size, HD)
        for r0 in range(0, rows, SUB_ROWS):
            at = slice(r0, min(r0 + SUB_ROWS, rows))
            blocks = [scores[at, c : c + lane] for c in range(0, size, lane)]
            old = top[at, :]
            new = jnp.maximum(old, jnp.max(functools.reduce(jnp.maximum, blocks), axis=1, keepdims=True))
            top[at, :] = new
            less = jnp.exp2((old - new) * factor)
            shrink[at, :] = less
            partial = None
            for n, block in enumerate(blocks):
                weight = jnp.exp2((block - new[:, :lane]) * factor)
                partial = weight if partial is None else partial + weight
                place = slice(n * lane, (n + 1) * lane)
                weights[at, place] = weight.astype(jnp.bfloat16)
                grad_weights[at, place] = (weight * others[at, place]).astype(jnp.bfloat16)
            total[at, :] *= less
            total[at, :lane] += partial

    def add(begin, size, weights, grad_weights, shrink):
        both = kv[pl.ds(pl.multiple_of(begin, unit), size), :]
        less = shrink[...]
        first_two = dot(weights[:, :size], both)
        last_one = dot(grad_weights[:, :size], both[:, HD:])
        acc[:, :HD] = acc[:, :HD] * less + first_two[:, :HD]
        acc[:, HD : 2 * HD] = acc[:, HD : 2 * HD] * less + first_two[:, HD:]
        acc[:, 2 * HD :] = acc[:, 2 * HD :] * less + last_one

    full = count // (CHUNK // unit)

    def two_chunks(c, carry):
        begin = 2 * c * CHUNK
        products(begin + CHUNK, CHUNK, *slots[1][:2])
        weigh(CHUNK, *slots[0])
        add(begin, CHUNK, *slots[0][2:])
        products(jnp.minimum(begin + 2 * CHUNK, (full - 1) * CHUNK), CHUNK, *slots[0][:2])
        weigh(CHUNK, *slots[1])
        add(begin + CHUNK, CHUNK, *slots[1][2:])
        return carry

    @pl.when(full > 0)
    def _():
        products(0, CHUNK, *slots[0][:2])

    lax.fori_loop(0, full // 2, two_chunks, 0)

    @pl.when(full % 2 > 0)
    def _():
        weigh(CHUNK, *slots[0])
        add((full - 1) * CHUNK, CHUNK, *slots[0][2:])

    def step(begin, size):
        products(begin, size, *slots[0][:2])
        weigh(size, *slots[0])
        add(begin, size, *slots[0][2:])

    size = CHUNK // 2
    while size >= unit:
        done = count // (2 * size // unit) * (2 * size)
        pl.when(count * unit - done >= size)(functools.partial(step, done, size))
        size //= 2
    if not last:
        return

    for h in range(heads):
        at = pl.ds(h * slot_tokens, slot_tokens)
        inverse = 1.0 / jnp.sum(total[at, :], axis=1, keepdims=True)
        attended = (acc[at, :HD] * inverse).astype(jnp.bfloat16)
        att_ref[:, h * HD : (h + 1) * HD] = attended
        delta = jnp.sum(
            cot[at, :].astype(jnp.float32) * attended.astype(jnp.float32), axis=1, keepdims=True
        )
        grad = (acc[at, 2 * HD :] - delta * acc[at, HD : 2 * HD]) * (inverse * scale)
        grads[:, h * HD : (h + 1) * HD] = grad.astype(jnp.bfloat16)
    query_gradient = grads[...]
    up = up_ref[pl.ds(adapter_of(ids, row, tokens), RANK), :]
    sent_ref[:, :width] = (ADAPTER_SCALE * dot(latt_ref[...], query_gradient)).astype(jnp.bfloat16)
    sent_ref[:, width:] = (ADAPTER_SCALE * dot_nt(up, query_gradient)).astype(jnp.bfloat16)


def down_kernel(n_slots, n_row, width, *refs):
    parts, hidden, even_ref, odd_ref = refs[:n_slots], refs[n_slots], *refs[n_slots + 1 :]
    row = lax.axis_index("row")
    depth = even_ref.shape[1] - width
    slot_tokens = parts[0].shape[1] - width
    up = parts[0][:, :width].astype(jnp.float32)
    for part in parts[1:]:
        up = up + part[:, :width].astype(jnp.float32)
    up = up.astype(jnp.bfloat16)
    slots = [slot_of(slot_tokens, n_slots, j) for j in range(n_slots)]
    for i in range(n_row):
        out = odd_ref if i & 1 else even_ref
        rows = slice((i >> 1) * RANK, ((i >> 1) + 1) * RANK)
        cols = pl.ds(pl.multiple_of((row ^ i) * depth, depth), depth)
        grad = jnp.zeros((RANK, depth), jnp.float32)
        for j in range(n_slots):
            grad += dot(parts[j][:, width:], hidden[slots[j], cols])
        out[rows, :depth] = grad.astype(jnp.bfloat16)
        out[rows, depth:] = up


def finish_kernel(n_row, tokens, ids, *refs):
    pairs, (down_ref, up_ref, down) = refs[: n_row // 2], refs[n_row // 2 :]
    row = lax.axis_index("row")
    depth = down.shape[1]
    down[...] = jnp.zeros_like(down)
    up_ref[...] = jnp.zeros_like(up_ref)
    for i in range(n_row):
        at = pl.ds(adapter_of(ids, row ^ i, tokens), RANK)
        part = pairs[i >> 1][(i & 1) * RANK : ((i & 1) + 1) * RANK, :]
        down[at, :] += part[:, :depth].astype(jnp.float32)
        up_ref[at, :] += part[:, depth:].astype(jnp.float32)
    down_ref[...] = down[...].T


def place_kernel(n_slots, *refs):
    parts, out, sems = refs[:n_slots], *refs[n_slots:]
    slot_tokens = parts[0].shape[0]
    for copy in fetch(
        [(parts[j], out.at[slot_of(slot_tokens, n_slots, j), :]) for j in range(n_slots)], sems
    ):
        copy.wait()


def shards(
    hidden_in,
    frozen_query_base,
    k_prefix,
    v_prefix,
    tree_mask,
    adapter_ids,
    a_down,
    up_weight_matrix,
    cotangent,
):
    tokens, model = hidden_in.shape
    width = frozen_query_base.shape[1]
    heads = width // HD
    depth, rank_cols = a_down.shape
    local_keys = k_prefix.shape[0]
    n_pre, n_row = lax.axis_size("pre"), lax.axis_size("row")
    n_slots = min(n_pre, tokens // MIN_TOKENS)
    slot_tokens = tokens // n_slots
    bf16, f32 = jnp.bfloat16, jnp.float32
    slices = min(n_row, local_keys // MB)
    drop = (n_row // slices).bit_length() - 1
    part_rows = local_keys // slices
    students, blocks = tree_mask.shape

    away = pl.pallas_call(
        functools.partial(away_kernel, drop, part_rows),
        out_shape=jax.ShapeDtypeStruct((2 * part_rows + mask_rows(tree_mask), HD), bf16),
        in_specs=[HBM] * 3,
        out_specs=VMEM,
        scratch_shapes=[pltpu.VMEM((students, blocks), jnp.int32), pltpu.SemaphoreType.DMA((5,))],
        compiler_params=params(56),
        name="away",
    )(k_prefix, v_prefix, tree_mask)

    away, a_down = lax.optimization_barrier((away, a_down))
    slots = pl.pallas_call(
        functools.partial(pick_kernel, n_row, tokens),
        out_shape=jax.ShapeDtypeStruct((n_row * RANK * depth // HD, HD), bf16),
        in_specs=[SMEM, VMEM],
        out_specs=VMEM,
        scratch_shapes=[pltpu.VMEM((rank_cols, depth), f32)],
        compiler_params=params(16),
        name="pick",
    )(adapter_ids, a_down)
    far_plane = n_pre >> 1
    planes = {0: away, far_plane: swap(away, "pre", far_plane)}
    for bit in range(n_pre.bit_length() - 2)[::-1]:
        for m in sorted(planes):
            planes[m | 1 << bit] = swap(planes[m], "pre", 1 << bit)
    far = list(range(max(drop, 1), n_row.bit_length() - 1))[::-1]
    turn = len(far) // 2
    orders = [order + ([0] if drop == 0 else []) for order in (far, far[turn:] + far[:turn])]

    piece_rows = depth // (2 * HD) * RANK
    columns = [
        [slots[(a * n_row + i) * piece_rows : (a * n_row + i + 1) * piece_rows] for i in range(n_row)]
        for a in range(2)
    ]

    def moved(bit):
        return [i for i in range(n_row) if i >> bit & 1]

    def put(a, bit, got):
        for n, i in enumerate(moved(bit)):
            columns[a][i] = got[n * piece_rows : (n + 1) * piece_rows]

    core = moved(0)
    got = swap(jnp.concatenate([columns[a][i] for a in range(2) for i in core]), "row", 1)
    got, planes[far_plane] = lax.optimization_barrier((got, planes[far_plane]))
    put(0, 0, got[: len(core) * piece_rows])
    put(1, 0, got[len(core) * piece_rows :])
    for a in range(2):
        for bit in range(1, n_row.bit_length() - 1):
            if bit != orders[a][0]:
                put(a, bit, swap(jnp.concatenate([columns[a][i] for i in moved(bit)]), "row", 1 << bit))
    planes = [planes[j] for j in range(1, n_pre)]
    planes, columns = lax.optimization_barrier((planes, columns))
    masks = jnp.stack(
        [tree_mask]
        + [plane[2 * part_rows : 2 * part_rows + students, :blocks].astype(jnp.int32) for plane in planes]
    )

    first = lax.axis_index("pre") % n_slots * slot_tokens
    hid, base, cot = (lax.dynamic_slice_in_dim(x, first, slot_tokens, 0) for x in (hidden_in, frozen_query_base, cotangent))
    up = up_weight_matrix
    rows = heads * slot_tokens
    state = [jax.ShapeDtypeStruct((rows, c), f32) for c in (HD, HD, 3 * HD)]

    def attention(group, first, last, operands, in_specs, out_shape, scratch):
        sources, places = [], []
        for a, i, place in group:
            for array, _ in place:
                if not any(array is other for other in sources):
                    sources.append(array)
            index = [[array is other for other in sources].index(True) for array, _ in place]
            places.append((a, i, [(n, begin) for n, (_, begin) in zip(index, place)]))
        keys = len(places) * (n_pre - 1) * part_rows // 2 + (local_keys if first else 0)
        return pl.pallas_call(
            functools.partial(
                attention_kernel, n_pre, drop, part_rows, places, len(sources), first, last, tokens
            ),
            out_shape=out_shape,
            in_specs=[SMEM, VMEM, VMEM] + in_specs + [VMEM] * len(sources),
            out_specs=[VMEM] * len(out_shape),
            scratch_shapes=[
                pltpu.VMEM((keys, 2 * HD), bf16),
                pltpu.VMEM((rows, HD), bf16),
                pltpu.VMEM((rows, HD), bf16),
            ]
            + [
                pltpu.VMEM((rows, c), dtype)
                for c, dtype in ((CHUNK, f32), (CHUNK, f32), (CHUNK, bf16), (CHUNK, bf16), (HD, f32))
            ]
            * 2
            + scratch,
            compiler_params=params(32 + keys * HD * 8 // MIB),
            cost_estimate=pl.CostEstimate(
                flops=4 * rows * keys * HD, bytes_accessed=keys * HD * 4, transcendentals=rows * keys // 2
            ),
            name="first_keys" if first else "last_keys" if last else "next_keys",
        )(masks, queries, cot, *operands, *sources)

    rounds = len(orders[0])
    away_rows = (n_pre - 1) * part_rows
    parts = [
        {0: jnp.concatenate([plane[a * part_rows : (a + 1) * part_rows] for plane in planes])}
        for a in range(2)
    ]
    groups = [[], [], []]
    for a in range(2):
        groups[0].append((a, 0, [(plane, a * part_rows) for plane in planes]))
    for k in range(rounds):
        got = []
        for a in range(2):
            bit = orders[a][k]
            payload = list(parts[a].values())
            if k == 0:
                payload += [columns[a][i] for i in moved(bit)]
            got.append(swap(jnp.concatenate(payload), "row", 1 << bit))
            if k == 0:
                put(a, bit, got[a][away_rows:])
        if k == 0:
            queries, latent_t = pl.pallas_call(
                functools.partial(query_kernel, n_row, tokens),
                out_shape=[
                    jax.ShapeDtypeStruct((slot_tokens, width), bf16),
                    jax.ShapeDtypeStruct((RANK, slot_tokens), bf16),
                ],
                in_specs=[SMEM] + [VMEM] * 5,
                out_specs=[VMEM] * 2,
                compiler_params=params(16),
                name="queries",
            )(adapter_ids, hid, base, up, *(jnp.concatenate(c) for c in columns))
        if k == rounds - 2:
            held = attention(groups[0], True, False, (k_prefix, v_prefix), [VMEM] * 2, state, [])
            got, held = lax.optimization_barrier((got, held))
        for a in range(2):
            for n, m in enumerate(list(parts[a])):
                there = m | 1 << orders[a][k]
                parts[a][there] = got[a][n * away_rows : (n + 1) * away_rows]
                place = [(got[a], n * away_rows + j * part_rows) for j in range(n_pre - 1)]
                groups[max(0, k + 3 - rounds)].append((a, there >> drop, place))
    held = attention(groups[1], False, False, held, [VMEM] * 3, state, [])
    attended, sent = attention(
        groups[2],
        False,
        True,
        (*held, adapter_ids, latent_t, up),
        [VMEM] * 3 + [SMEM] + [VMEM] * 2,
        [
            jax.ShapeDtypeStruct((slot_tokens, width), bf16),
            jax.ShapeDtypeStruct((RANK, width + slot_tokens), bf16),
        ],
        [pltpu.VMEM(s.shape, s.dtype) for s in state] + [pltpu.VMEM((slot_tokens, width), bf16)],
    )

    far_slot = n_slots >> 1
    attended_parts = {far_slot: swap(attended, "pre", far_slot)}
    shared = [swap(sent, "pre", j) for j in range(n_slots)]

    pairs = n_row // 2
    even, odd = pl.pallas_call(
        functools.partial(down_kernel, n_slots, n_row, width),
        out_shape=[jax.ShapeDtypeStruct((pairs * RANK, depth + width), bf16)] * 2,
        in_specs=[VMEM] * (n_slots + 1),
        out_specs=[VMEM] * 2,
        compiler_params=params(16),
        name="down",
    )(*shared, hidden_in)
    odd = swap(odd, "row", 1)
    spans = [slice(m * RANK, (m + 1) * RANK) for m in range(pairs)]
    pieces = [swap(jnp.concatenate([even[at], odd[at]]), "row", 2 * m) for m, at in enumerate(spans)]

    attended_parts[0] = attended
    pieces[1], attended_parts[far_slot] = lax.optimization_barrier((pieces[1], attended_parts[far_slot]))
    for bit in range(n_slots.bit_length() - 2)[::-1]:
        for m in list(attended_parts):
            attended_parts[m | 1 << bit] = swap(attended_parts[m], "pre", 1 << bit)

    grad_a, up_weight_gradient = pl.pallas_call(
        functools.partial(finish_kernel, n_row, tokens),
        out_shape=[
            jax.ShapeDtypeStruct((depth, rank_cols), f32),
            jax.ShapeDtypeStruct((rank_cols, width), f32),
        ],
        in_specs=[SMEM] + [VMEM] * pairs,
        out_specs=[VMEM] * 2,
        scratch_shapes=[pltpu.VMEM((rank_cols, depth), f32)],
        compiler_params=params(16),
        name="finish",
    )(adapter_ids, *pieces)

    attended = pl.pallas_call(
        functools.partial(place_kernel, n_slots),
        out_shape=jax.ShapeDtypeStruct((tokens, width), bf16),
        in_specs=[VMEM] * n_slots,
        out_specs=HBM,
        scratch_shapes=[pltpu.SemaphoreType.DMA((n_slots,))],
        compiler_params=params(16),
        cost_estimate=pl.CostEstimate(
            flops=100 * tokens * width * HD, bytes_accessed=100 * tokens * width, transcendentals=0
        ),
        name="place",
    )(*(attended_parts[j] for j in range(n_slots)))
    return attended, grad_a, up_weight_gradient


def solution(mesh):
    in_specs = (
        P("row", None),
        P("row", None),
        P("pre", None),
        P("pre", None),
        P(None, "pre"),
        P(),
        P("row", None),
        P(),
        P("row", None),
    )
    out_specs = (P("row", None), P("row", None), P())
    return jax.shard_map(shards, mesh=mesh, in_specs=in_specs, out_specs=out_specs, check_vma=False)
```

```python
import functools
import math

import jax
import jax.numpy as jnp
from jax import lax
from jax.experimental import pallas as pl
from jax.experimental.pallas import tpu as pltpu
from jax.sharding import PartitionSpec as P

HD = 128
RANK = 16
CONT = 512
MB = 128
CHUNK = 1024
ROW_TILE = 1024
MIN_TOKENS = 16
ADAPTER_SCALE = 2.0
VERY_LOW = -1e30
LOG2E = 1.4426950408889634
MIB = 1 << 20

NT = (((1,), (1,)), ((), ()))
VMEM = pl.BlockSpec(memory_space=pltpu.VMEM)
SMEM = pl.BlockSpec(memory_space=pltpu.SMEM)
HBM = pl.BlockSpec(memory_space=pltpu.HBM)


def dot(a, b):
    return jnp.dot(a, b, preferred_element_type=jnp.float32)


def dot_nt(a, b):
    return lax.dot_general(a, b, NT, preferred_element_type=jnp.float32)


def swap(x, axis, mask):
    if mask == 0:
        return x
    return lax.ppermute(x, axis, [(s, s ^ mask) for s in range(lax.axis_size(axis))])


def params(mib):
    return pltpu.CompilerParams(vmem_limit_bytes=mib * MIB)


def adapter_of(ids, row, tokens):
    return pl.multiple_of(ids[row * tokens // CONT] * RANK, RANK)


def slot_of(slot_tokens, n_slots, offset=0):
    slot = lax.rem(lax.axis_index("pre"), n_slots) ^ offset
    return pl.ds(pl.multiple_of(slot * slot_tokens, slot_tokens), slot_tokens)


def fetch(pairs, sems):
    copies = [pltpu.make_async_copy(src, dst, sems.at[i]) for i, (src, dst) in enumerate(pairs)]
    for copy in copies:
        copy.start()
    return copies


def mask_rows(mask):
    return -(-mask.shape[0] // 16) * 16


def away_kernel(drop, part_rows, k_ref, v_ref, mask_ref, away_ref, mask_in, sems):
    half = part_rows // 2
    begin = (lax.axis_index("row") >> drop) * part_rows
    pairs = [(mask_ref, mask_in)]
    for a in range(2):
        span = pl.ds(pl.multiple_of(begin + a * half, half), half)
        pairs.append((k_ref.at[span, :], away_ref.at[pl.ds(2 * a * half, half), :]))
        pairs.append((v_ref.at[span, :], away_ref.at[pl.ds((2 * a + 1) * half, half), :]))
    copies = fetch(pairs, sems)
    students, blocks = mask_in.shape
    copies[0].wait()
    away_ref[2 * part_rows :, :] = jnp.zeros_like(away_ref[2 * part_rows :, :])
    away_ref[2 * part_rows : 2 * part_rows + students, :blocks] = mask_in[...].astype(jnp.bfloat16)
    for copy in copies[1:]:
        copy.wait()


def pick_kernel(n_row, tokens, ids, a_ref, slots_ref, at):
    row = lax.axis_index("row")
    cols = a_ref.shape[0] // (2 * HD)
    at[...] = a_ref[...].astype(jnp.float32).T
    for i in range(n_row):
        piece = at[pl.ds(adapter_of(ids, row ^ i, tokens), RANK), :].astype(jnp.bfloat16)
        for half in range(2):
            for c in range(cols):
                first = ((half * n_row + i) * cols + c) * RANK
                lane = (half * cols + c) * HD
                slots_ref[first : first + RANK, :] = piece[:, lane : lane + HD]


def query_kernel(n_row, tokens, ids, hid, base, up_ref, low, high, q_ref, latt_ref):
    row = lax.axis_index("row")
    slot_tokens = q_ref.shape[0]
    cols = low.shape[0] // (n_row * RANK)
    span = cols * HD
    latent = jnp.zeros((slot_tokens, RANK), jnp.float32)
    latent_t = jnp.zeros((RANK, slot_tokens), jnp.float32)
    for i in range(n_row):
        for half, ref in enumerate((low, high)):
            firsts = [(i * cols + c) * RANK for c in range(cols)]
            piece = jnp.concatenate([ref[first : first + RANK, :] for first in firsts], axis=1)
            block = hid[:, pl.ds(pl.multiple_of(((row ^ i) * 2 + half) * span, span), span)]
            latent += dot_nt(block, piece)
            latent_t += dot_nt(piece, block)
    latt_ref[...] = latent_t.astype(jnp.bfloat16)
    up = up_ref[pl.ds(adapter_of(ids, row, tokens), RANK), :]
    raised = dot(latent.astype(jnp.bfloat16), up)
    q_ref[...] = (base[...].astype(jnp.float32) + ADAPTER_SCALE * raised).astype(jnp.bfloat16)


def attention_kernel(n_pre, drop, part_rows, places, n_sources, first, last, tokens, *refs):
    masks, q_ref, cot_ref = refs[:3]
    refs = refs[3:]
    if first:
        k_own, v_own, refs = refs[0], refs[1], refs[2:]
    else:
        held, refs = refs[:3], refs[3:]
    if last:
        ids, latt_ref, up_ref, refs = *refs[:3], refs[3:]
    sources, refs = refs[:n_sources], refs[n_sources:]
    if last:
        out_ref, kv, q, cot, top, total, acc, grads = refs
    else:
        top, total, acc, kv, q, cot = refs
    row = lax.axis_index("row")
    slot_tokens, width = q_ref.shape
    heads = width // HD
    rows = heads * slot_tokens
    tile = min(ROW_TILE, rows)
    scale = 1.0 / math.sqrt(HD)
    factor = scale * LOG2E

    student = row * tokens // CONT
    half = part_rows // 2
    unit = min(MB, half)

    def keep(count, live, key_block, value_block):
        @pl.when(live)
        def _():
            at = pl.ds(pl.multiple_of(count * unit, unit), unit)
            kv[at, :HD] = value_block()
            kv[at, HD:] = key_block()

        return count + live.astype(jnp.int32)

    def own_block(b, count):
        at = pl.ds(pl.multiple_of(b * unit, unit), unit)
        live = masks[0, student, b * unit // MB] > 0
        return keep(count, live, lambda: k_own[at, :], lambda: v_own[at, :])

    def block_of(source, begin):
        return lambda: sources[source][begin : begin + unit, :]

    count = jnp.int32(0)
    if first:
        count = lax.fori_loop(0, k_own.shape[0] // unit, own_block, count)
    for a, i, place in places:
        piece = (row >> drop) ^ i
        for j in range(1, n_pre):
            source, begin = place[j - 1]
            for u in range(half // unit):
                block = (piece * part_rows + a * half + u * unit) // MB
                count = keep(
                    count,
                    masks[j, student, block] > 0,
                    block_of(source, begin + u * unit),
                    block_of(source, begin + half + u * unit),
                )

    for h in range(heads):
        at = pl.ds(h * slot_tokens, slot_tokens)
        q[at, :] = q_ref[:, h * HD : (h + 1) * HD]
        cot[at, :] = cot_ref[:, h * HD : (h + 1) * HD]
    if first:
        top[...] = jnp.full_like(top, VERY_LOW)
        total[...] = jnp.zeros_like(total)
        acc[...] = jnp.zeros_like(acc)
    else:
        for ref, given in zip((top, total, acc), held):
            ref[...] = given[...]

    def step(begin, size):
        both = kv[pl.ds(pl.multiple_of(begin, unit), size), :]
        values, keys = both[:, :HD], both[:, HD:]
        lane = min(size, HD)
        lanes = size // lane
        for r0 in range(0, rows, tile):
            at = pl.ds(r0, tile)
            scores = dot_nt(q[at, :], keys)
            old = top[at, :]
            new = jnp.maximum(old, jnp.max(scores, axis=1, keepdims=True))
            top[at, :] = new
            weights = jnp.exp2((scores - jnp.concatenate([new[:, :lane]] * lanes, axis=1)) * factor)
            shrink = jnp.exp2((old - new) * factor)
            partial = weights[:, :lane]
            for c in range(1, lanes):
                partial = partial + weights[:, c * lane : (c + 1) * lane]
            total[at, :] *= shrink
            total[at, :lane] += partial
            grad_weights = (weights * dot_nt(cot[at, :], values)).astype(jnp.bfloat16)
            first_two = dot(weights.astype(jnp.bfloat16), both)
            last = dot(grad_weights, keys)
            acc[at, :HD] = acc[at, :HD] * shrink + first_two[:, :HD]
            acc[at, HD : 2 * HD] = acc[at, HD : 2 * HD] * shrink + first_two[:, HD:]
            acc[at, 2 * HD :] = acc[at, 2 * HD :] * shrink + last

    per_chunk = CHUNK // unit
    full = count // per_chunk

    def full_step(c, carry):
        step(c * CHUNK, CHUNK)
        return carry

    lax.fori_loop(0, full, full_step, 0)
    size = CHUNK // 2
    while size >= unit:
        done = count // (2 * size // unit) * (2 * size)
        pl.when(count * unit - done >= size)(functools.partial(step, done, size))
        size //= 2
    if not last:
        return

    for h in range(heads):
        at = pl.ds(h * slot_tokens, slot_tokens)
        inverse = 1.0 / jnp.sum(total[at, :], axis=1, keepdims=True)
        attended = (acc[at, :HD] * inverse).astype(jnp.bfloat16)
        out_ref[at, :] = attended
        delta = jnp.sum(
            cot[at, :].astype(jnp.float32) * attended.astype(jnp.float32), axis=1, keepdims=True
        )
        grad = (acc[at, 2 * HD :] - delta * acc[at, HD : 2 * HD]) * (inverse * scale)
        grads[:, h * HD : (h + 1) * HD] = grad.astype(jnp.bfloat16)
    query_gradient = grads[...]
    up = up_ref[pl.ds(adapter_of(ids, row, tokens), RANK), :]
    up_grad = (ADAPTER_SCALE * dot(latt_ref[...], query_gradient)).astype(jnp.bfloat16)
    for h in range(heads):
        first = rows + h * RANK
        out_ref[first : first + RANK, :] = up_grad[:, h * HD : (h + 1) * HD]
    grad_latent = (ADAPTER_SCALE * dot_nt(up, query_gradient)).astype(jnp.bfloat16)
    out_ref[rows + heads * RANK :, :] = jnp.zeros((RANK, HD), jnp.bfloat16)
    out_ref[rows + heads * RANK :, :slot_tokens] = grad_latent


def down_kernel(n_slots, n_row, slot_tokens, width, firsts, *refs):
    parts, hidden, even_ref, odd_ref = refs[:n_slots], refs[n_slots], *refs[n_slots + 1 :]
    row = lax.axis_index("row")
    depth = even_ref.shape[1] - width
    heads = width // HD
    ups, latents = [], []
    for part, first in zip(parts, firsts):
        ups.append([part[first + h * RANK : first + (h + 1) * RANK, :] for h in range(heads)])
        latents.append(part[first + heads * RANK : first + (heads + 1) * RANK, :slot_tokens])
    up = [sum(x.astype(jnp.float32) for x in terms).astype(jnp.bfloat16) for terms in zip(*ups)]
    up = jnp.concatenate(up, axis=1)
    slots = [slot_of(slot_tokens, n_slots, j) for j in range(n_slots)]
    for i in range(n_row):
        out = odd_ref if i & 1 else even_ref
        rows = slice((i >> 1) * RANK, ((i >> 1) + 1) * RANK)
        cols = pl.ds(pl.multiple_of((row ^ i) * depth, depth), depth)
        grad = jnp.zeros((RANK, depth), jnp.float32)
        for j in range(n_slots):
            grad += dot(latents[j], hidden[slots[j], cols])
        out[rows, :depth] = grad.astype(jnp.bfloat16)
        out[rows, depth:] = up


def finish_kernel(n_row, tokens, ids, *refs):
    pairs, (down_ref, up_ref, down) = refs[: n_row // 2], refs[n_row // 2 :]
    row = lax.axis_index("row")
    depth = down.shape[1]
    down[...] = jnp.zeros_like(down)
    up_ref[...] = jnp.zeros_like(up_ref)
    for i in range(n_row):
        at = pl.ds(adapter_of(ids, row ^ i, tokens), RANK)
        part = pairs[i >> 1][(i & 1) * RANK : ((i & 1) + 1) * RANK, :]
        down[at, :] += part[:, :depth].astype(jnp.float32)
        up_ref[at, :] += part[:, depth:].astype(jnp.float32)
    down_ref[...] = down[...].T


def place_kernel(n_slots, slot_tokens, *refs):
    parts, out, sems = refs[:n_slots], *refs[n_slots:]
    pairs = []
    for j in range(n_slots):
        slot = slot_of(slot_tokens, n_slots, j)
        for h in range(out.shape[1] // HD):
            at = pl.ds(h * slot_tokens, slot_tokens)
            pairs.append((parts[j].at[at, :], out.at[slot, pl.ds(h * HD, HD)]))
    for copy in fetch(pairs, sems):
        copy.wait()


def shards(
    hidden_in,
    frozen_query_base,
    k_prefix,
    v_prefix,
    tree_mask,
    adapter_ids,
    a_down,
    up_weight_matrix,
    cotangent,
):
    tokens, model = hidden_in.shape
    width = frozen_query_base.shape[1]
    heads = width // HD
    depth, rank_cols = a_down.shape
    local_keys = k_prefix.shape[0]
    n_pre, n_row = lax.axis_size("pre"), lax.axis_size("row")
    n_slots = min(n_pre, tokens // MIN_TOKENS)
    slot_tokens = tokens // n_slots
    bf16, f32 = jnp.bfloat16, jnp.float32
    slices = min(n_row, local_keys // MB)
    drop = (n_row // slices).bit_length() - 1
    part_rows = local_keys // slices
    students, blocks = tree_mask.shape

    away = pl.pallas_call(
        functools.partial(away_kernel, drop, part_rows),
        out_shape=jax.ShapeDtypeStruct((2 * part_rows + mask_rows(tree_mask), HD), bf16),
        in_specs=[HBM] * 3,
        out_specs=VMEM,
        scratch_shapes=[pltpu.VMEM((students, blocks), jnp.int32), pltpu.SemaphoreType.DMA((5,))],
        compiler_params=params(56),
        name="away",
    )(k_prefix, v_prefix, tree_mask)

    away, a_down = lax.optimization_barrier((away, a_down))
    slots = pl.pallas_call(
        functools.partial(pick_kernel, n_row, tokens),
        out_shape=jax.ShapeDtypeStruct((n_row * RANK * depth // HD, HD), bf16),
        in_specs=[SMEM, VMEM],
        out_specs=VMEM,
        scratch_shapes=[pltpu.VMEM((rank_cols, depth), f32)],
        compiler_params=params(16),
        name="pick",
    )(adapter_ids, a_down)
    far_plane = n_pre >> 1
    planes = {0: away, far_plane: swap(away, "pre", far_plane)}
    for bit in range(n_pre.bit_length() - 2)[::-1]:
        for m in sorted(planes):
            planes[m | 1 << bit] = swap(planes[m], "pre", 1 << bit)
    far = list(range(max(drop, 1), n_row.bit_length() - 1))[::-1]
    turn = len(far) // 2
    orders = [order + ([0] if drop == 0 else []) for order in (far, far[turn:] + far[:turn])]

    piece_rows = depth // (2 * HD) * RANK
    columns = [
        [slots[(a * n_row + i) * piece_rows : (a * n_row + i + 1) * piece_rows] for i in range(n_row)]
        for a in range(2)
    ]

    def moved(bit):
        return [i for i in range(n_row) if i >> bit & 1]

    def put(a, bit, got):
        for n, i in enumerate(moved(bit)):
            columns[a][i] = got[n * piece_rows : (n + 1) * piece_rows]

    core = moved(0)
    got = swap(jnp.concatenate([columns[a][i] for a in range(2) for i in core]), "row", 1)
    got, planes[far_plane] = lax.optimization_barrier((got, planes[far_plane]))
    put(0, 0, got[: len(core) * piece_rows])
    put(1, 0, got[len(core) * piece_rows :])
    for a in range(2):
        for bit in range(1, n_row.bit_length() - 1):
            if bit != orders[a][0]:
                put(a, bit, swap(jnp.concatenate([columns[a][i] for i in moved(bit)]), "row", 1 << bit))
    planes = [planes[j] for j in range(1, n_pre)]
    masks = jnp.stack(
        [tree_mask]
        + [plane[2 * part_rows : 2 * part_rows + students, :blocks].astype(jnp.int32) for plane in planes]
    )
    planes, columns, masks = lax.optimization_barrier((planes, columns, masks))

    first = lax.axis_index("pre") % n_slots * slot_tokens
    hid, base, cot = (lax.dynamic_slice_in_dim(x, first, slot_tokens, 0) for x in (hidden_in, frozen_query_base, cotangent))
    up = up_weight_matrix
    rows = heads * slot_tokens
    state = [jax.ShapeDtypeStruct((rows, c), f32) for c in (HD, HD, 3 * HD)]

    def attention(group, first, last, operands, in_specs, out_shape, scratch):
        sources, places = [], []
        for a, i, place in group:
            for array, _ in place:
                if not any(array is other for other in sources):
                    sources.append(array)
            index = [[array is other for other in sources].index(True) for array, _ in place]
            places.append((a, i, [(n, begin) for n, (_, begin) in zip(index, place)]))
        keys = len(places) * (n_pre - 1) * part_rows // 2 + (local_keys if first else 0)
        return pl.pallas_call(
            functools.partial(
                attention_kernel, n_pre, drop, part_rows, places, len(sources), first, last, tokens
            ),
            out_shape=out_shape,
            in_specs=[SMEM, VMEM, VMEM] + in_specs + [VMEM] * len(sources),
            out_specs=[VMEM] * len(out_shape),
            scratch_shapes=[
                pltpu.VMEM((keys, 2 * HD), bf16),
                pltpu.VMEM((rows, HD), bf16),
                pltpu.VMEM((rows, HD), bf16),
            ]
            + scratch,
            compiler_params=params(24 + keys * HD * 8 // MIB),
            cost_estimate=pl.CostEstimate(
                flops=4 * rows * keys * HD, bytes_accessed=keys * HD * 4, transcendentals=rows * keys // 2
            ),
            name="first_keys" if first else "last_keys" if last else "next_keys",
        )(masks, queries, cot, *operands, *sources)

    rounds = len(orders[0])
    away_rows = (n_pre - 1) * part_rows
    parts = [
        {0: jnp.concatenate([plane[a * part_rows : (a + 1) * part_rows] for plane in planes])}
        for a in range(2)
    ]
    groups = [[], [], []]
    for a in range(2):
        groups[0].append((a, 0, [(plane, a * part_rows) for plane in planes]))
    for k in range(rounds):
        got = []
        for a in range(2):
            bit = orders[a][k]
            payload = list(parts[a].values())
            if k == 0:
                payload += [columns[a][i] for i in moved(bit)]
            got.append(swap(jnp.concatenate(payload), "row", 1 << bit))
            if k == 0:
                put(a, bit, got[a][away_rows:])
        if k == 0:
            queries, latent_t = pl.pallas_call(
                functools.partial(query_kernel, n_row, tokens),
                out_shape=[
                    jax.ShapeDtypeStruct((slot_tokens, width), bf16),
                    jax.ShapeDtypeStruct((RANK, slot_tokens), bf16),
                ],
                in_specs=[SMEM] + [VMEM] * 5,
                out_specs=[VMEM] * 2,
                compiler_params=params(16),
                name="queries",
            )(adapter_ids, hid, base, up, *(jnp.concatenate(c) for c in columns))
        if k == rounds - 2:
            held = attention(groups[0], True, False, (k_prefix, v_prefix), [VMEM] * 2, state, [])
            got, held = lax.optimization_barrier((got, held))
        for a in range(2):
            for n, m in enumerate(list(parts[a])):
                there = m | 1 << orders[a][k]
                parts[a][there] = got[a][n * away_rows : (n + 1) * away_rows]
                place = [(got[a], n * away_rows + j * part_rows) for j in range(n_pre - 1)]
                groups[max(0, k + 3 - rounds)].append((a, there >> drop, place))
    held = attention(groups[1], False, False, held, [VMEM] * 3, state, [])
    small_rows = (heads + 1) * RANK
    (done,) = attention(
        groups[2],
        False,
        True,
        (*held, adapter_ids, latent_t, up),
        [VMEM] * 3 + [SMEM] + [VMEM] * 2,
        [jax.ShapeDtypeStruct((rows + small_rows, HD), bf16)],
        [pltpu.VMEM(s.shape, s.dtype) for s in state] + [pltpu.VMEM((slot_tokens, width), bf16)],
    )

    finished, small, small_firsts = {0: done}, {0: done}, {0: rows}
    for j in range(1, n_slots):
        if j & (j - 1) == 0:
            finished[j] = small[j] = swap(done, "pre", j)
            small_firsts[j] = rows
        else:
            small[j] = swap(done[rows:], "pre", j)
            small_firsts[j] = 0

    pairs = n_row // 2
    even, odd = pl.pallas_call(
        functools.partial(
            down_kernel, n_slots, n_row, slot_tokens, width, [small_firsts[j] for j in range(n_slots)]
        ),
        out_shape=[jax.ShapeDtypeStruct((pairs * RANK, depth + width), bf16)] * 2,
        in_specs=[VMEM] * (n_slots + 1),
        out_specs=[VMEM] * 2,
        compiler_params=params(16),
        name="down",
    )(*(small[j] for j in range(n_slots)), hidden_in)
    odd = swap(odd, "row", 1)
    spans = [slice(m * RANK, (m + 1) * RANK) for m in range(pairs)]
    pieces = [swap(jnp.concatenate([even[at], odd[at]]), "row", 2 * m) for m, at in enumerate(spans)]

    for j in range(1, n_slots):
        if j not in finished:
            finished[j] = swap(finished[j & (j - 1)][:rows], "pre", j & -j)

    grad_a, up_weight_gradient = pl.pallas_call(
        functools.partial(finish_kernel, n_row, tokens),
        out_shape=[
            jax.ShapeDtypeStruct((depth, rank_cols), f32),
            jax.ShapeDtypeStruct((rank_cols, width), f32),
        ],
        in_specs=[SMEM] + [VMEM] * pairs,
        out_specs=[VMEM] * 2,
        scratch_shapes=[pltpu.VMEM((rank_cols, depth), f32)],
        compiler_params=params(16),
        name="finish",
    )(adapter_ids, *pieces)

    attended = pl.pallas_call(
        functools.partial(place_kernel, n_slots, slot_tokens),
        out_shape=jax.ShapeDtypeStruct((tokens, width), bf16),
        in_specs=[VMEM] * n_slots,
        out_specs=HBM,
        scratch_shapes=[pltpu.SemaphoreType.DMA((n_slots * heads,))],
        compiler_params=params(16),
        cost_estimate=pl.CostEstimate(
            flops=100 * tokens * width * HD, bytes_accessed=100 * tokens * width, transcendentals=0
        ),
        name="place",
    )(*(finished[j] for j in range(n_slots)))
    return attended, grad_a, up_weight_gradient


def solution(mesh):
    in_specs = (
        P("row", None),
        P("row", None),
        P("pre", None),
        P("pre", None),
        P(None, "pre"),
        P(),
        P("row", None),
        P(),
        P("row", None),
    )
    out_specs = (P("row", None), P("row", None), P())
    return jax.shard_map(shards, mesh=mesh, in_specs=in_specs, out_specs=out_specs, check_vma=False)
```

```python
import functools
import math

import jax
import jax.numpy as jnp
from jax import lax
from jax.experimental import pallas as pl
from jax.experimental.pallas import tpu as pltpu
from jax.sharding import PartitionSpec as P

HD = 128
RANK = 16
CONT = 512
MB = 128
CHUNK = 1024
ROW_TILE = 1024
MIN_TOKENS = 16
ADAPTER_SCALE = 2.0
VERY_LOW = -1e30
LOG2E = 1.4426950408889634
MIB = 1 << 20

NT = (((1,), (1,)), ((), ()))
VMEM = pl.BlockSpec(memory_space=pltpu.VMEM)
SMEM = pl.BlockSpec(memory_space=pltpu.SMEM)
HBM = pl.BlockSpec(memory_space=pltpu.HBM)


def dot(a, b):
    return jnp.dot(a, b, preferred_element_type=jnp.float32)


def dot_nt(a, b):
    return lax.dot_general(a, b, NT, preferred_element_type=jnp.float32)


def swap(x, axis, mask):
    if mask == 0:
        return x
    return lax.ppermute(x, axis, [(s, s ^ mask) for s in range(lax.axis_size(axis))])


def params(mib):
    return pltpu.CompilerParams(vmem_limit_bytes=mib * MIB)


def adapter_of(ids, row, tokens):
    return pl.multiple_of(ids[row * tokens // CONT] * RANK, RANK)


def slot_of(slot_tokens, n_slots, offset=0):
    slot = lax.rem(lax.axis_index("pre"), n_slots) ^ offset
    return pl.ds(pl.multiple_of(slot * slot_tokens, slot_tokens), slot_tokens)


def fetch(pairs, sems):
    copies = [pltpu.make_async_copy(src, dst, sems.at[i]) for i, (src, dst) in enumerate(pairs)]
    for copy in copies:
        copy.start()
    return copies


def mask_rows(mask):
    return -(-mask.shape[0] // 16) * 16


def away_kernel(drop, part_rows, k_ref, v_ref, mask_ref, away_ref, mask_in, sems):
    half = part_rows // 2
    begin = (lax.axis_index("row") >> drop) * part_rows
    pairs = [(mask_ref, mask_in)]
    for a in range(2):
        span = pl.ds(pl.multiple_of(begin + a * half, half), half)
        pairs.append((k_ref.at[span, :], away_ref.at[pl.ds(2 * a * half, half), :]))
        pairs.append((v_ref.at[span, :], away_ref.at[pl.ds((2 * a + 1) * half, half), :]))
    copies = fetch(pairs, sems)
    students, blocks = mask_in.shape
    copies[0].wait()
    away_ref[2 * part_rows :, :] = jnp.zeros_like(away_ref[2 * part_rows :, :])
    away_ref[2 * part_rows : 2 * part_rows + students, :blocks] = mask_in[...].astype(jnp.bfloat16)
    for copy in copies[1:]:
        copy.wait()


def pick_kernel(n_row, tokens, ids, a_ref, slots_ref, at):
    row = lax.axis_index("row")
    cols = a_ref.shape[0] // (2 * HD)
    at[...] = a_ref[...].astype(jnp.float32).T
    for i in range(n_row):
        piece = at[pl.ds(adapter_of(ids, row ^ i, tokens), RANK), :].astype(jnp.bfloat16)
        for half in range(2):
            for c in range(cols):
                first = ((half * n_row + i) * cols + c) * RANK
                lane = (half * cols + c) * HD
                slots_ref[first : first + RANK, :] = piece[:, lane : lane + HD]


def query_kernel(n_row, tokens, ids, hid, base, up_ref, low, high, q_ref, latt_ref):
    row = lax.axis_index("row")
    slot_tokens = q_ref.shape[0]
    cols = low.shape[0] // (n_row * RANK)
    span = cols * HD
    latent = jnp.zeros((slot_tokens, RANK), jnp.float32)
    for i in range(n_row):
        for half, ref in enumerate((low, high)):
            firsts = [(i * cols + c) * RANK for c in range(cols)]
            piece = jnp.concatenate([ref[first : first + RANK, :] for first in firsts], axis=1)
            block = hid[:, pl.ds(pl.multiple_of(((row ^ i) * 2 + half) * span, span), span)]
            latent += dot_nt(block, piece)
    latent = latent.astype(jnp.bfloat16)
    square = (RANK, RANK)
    same = lax.broadcasted_iota(jnp.int32, square, 0) == lax.broadcasted_iota(jnp.int32, square, 1)
    eye = jnp.where(same, 1.0, 0.0).astype(jnp.bfloat16)
    latt_ref[...] = dot_nt(eye, latent).astype(jnp.bfloat16)
    up = up_ref[pl.ds(adapter_of(ids, row, tokens), RANK), :]
    raised = dot(latent, up)
    q_ref[...] = (base[...].astype(jnp.float32) + ADAPTER_SCALE * raised).astype(jnp.bfloat16)


def attention_kernel(n_pre, drop, part_rows, places, n_sources, first, last, tokens, *refs):
    masks, q_ref, cot_ref = refs[:3]
    refs = refs[3:]
    if first:
        k_own, v_own, refs = refs[0], refs[1], refs[2:]
    else:
        held, refs = refs[:3], refs[3:]
    if last:
        ids, latt_ref, up_ref, refs = *refs[:3], refs[3:]
    sources, refs = refs[:n_sources], refs[n_sources:]
    if last:
        att_ref, sent_ref, kv, q, cot, top, total, acc, grads = refs
    else:
        top, total, acc, kv, q, cot = refs
    row = lax.axis_index("row")
    slot_tokens, width = q_ref.shape
    heads = width // HD
    rows = heads * slot_tokens
    tile = min(ROW_TILE, rows)
    scale = 1.0 / math.sqrt(HD)
    factor = scale * LOG2E

    student = row * tokens // CONT
    half = part_rows // 2
    unit = min(MB, half)

    def keep(count, live, key_block, value_block):
        at = pl.ds(pl.multiple_of(count * unit, unit), unit)
        kv[at, :HD] = value_block()
        kv[at, HD:] = key_block()
        return count + live.astype(jnp.int32)

    def own_block(b, count):
        at = pl.ds(pl.multiple_of(b * unit, unit), unit)
        live = masks[0, student, b * unit // MB] > 0
        return keep(count, live, lambda: k_own[at, :], lambda: v_own[at, :])

    def block_of(source, begin):
        return lambda: sources[source][begin : begin + unit, :]

    count = jnp.int32(0)
    if first:
        count = lax.fori_loop(0, k_own.shape[0] // unit, own_block, count)
    for a, i, place in places:
        piece = (row >> drop) ^ i
        for j in range(1, n_pre):
            source, begin = place[j - 1]
            for u in range(half // unit):
                block = (piece * part_rows + a * half + u * unit) // MB
                count = keep(
                    count,
                    masks[j, student, block] > 0,
                    block_of(source, begin + u * unit),
                    block_of(source, begin + half + u * unit),
                )

    for h in range(heads):
        at = pl.ds(h * slot_tokens, slot_tokens)
        q[at, :] = q_ref[:, h * HD : (h + 1) * HD]
        cot[at, :] = cot_ref[:, h * HD : (h + 1) * HD]
    if first:
        top[...] = jnp.full_like(top, VERY_LOW)
        total[...] = jnp.zeros_like(total)
        acc[...] = jnp.zeros_like(acc)
    else:
        for ref, given in zip((top, total, acc), held):
            ref[...] = given[...]

    def step(begin, size):
        both = kv[pl.ds(pl.multiple_of(begin, unit), size), :]
        values, keys = both[:, :HD], both[:, HD:]
        lane = min(size, HD)
        lanes = size // lane
        for r0 in range(0, rows, tile):
            at = pl.ds(r0, tile)
            scores = dot_nt(q[at, :], keys)
            old = top[at, :]
            new = jnp.maximum(old, jnp.max(scores, axis=1, keepdims=True))
            top[at, :] = new
            weights = jnp.exp2((scores - jnp.concatenate([new[:, :lane]] * lanes, axis=1)) * factor)
            shrink = jnp.exp2((old - new) * factor)
            partial = weights[:, :lane]
            for c in range(1, lanes):
                partial = partial + weights[:, c * lane : (c + 1) * lane]
            total[at, :] *= shrink
            total[at, :lane] += partial
            grad_weights = (weights * dot_nt(cot[at, :], values)).astype(jnp.bfloat16)
            first_two = dot(weights.astype(jnp.bfloat16), both)
            last = dot(grad_weights, keys)
            acc[at, :HD] = acc[at, :HD] * shrink + first_two[:, :HD]
            acc[at, HD : 2 * HD] = acc[at, HD : 2 * HD] * shrink + first_two[:, HD:]
            acc[at, 2 * HD :] = acc[at, 2 * HD :] * shrink + last

    per_chunk = CHUNK // unit
    full = count // per_chunk

    def full_step(c, carry):
        step(c * CHUNK, CHUNK)
        return carry

    lax.fori_loop(0, full, full_step, 0)
    size = CHUNK // 2
    while size >= unit:
        done = count // (2 * size // unit) * (2 * size)
        pl.when(count * unit - done >= size)(functools.partial(step, done, size))
        size //= 2
    if not last:
        return

    for h in range(heads):
        at = pl.ds(h * slot_tokens, slot_tokens)
        inverse = 1.0 / jnp.sum(total[at, :], axis=1, keepdims=True)
        attended = (acc[at, :HD] * inverse).astype(jnp.bfloat16)
        att_ref[:, h * HD : (h + 1) * HD] = attended
        delta = jnp.sum(
            cot[at, :].astype(jnp.float32) * attended.astype(jnp.float32), axis=1, keepdims=True
        )
        grad = (acc[at, 2 * HD :] - delta * acc[at, HD : 2 * HD]) * (inverse * scale)
        grads[:, h * HD : (h + 1) * HD] = grad.astype(jnp.bfloat16)
    query_gradient = grads[...]
    up = up_ref[pl.ds(adapter_of(ids, row, tokens), RANK), :]
    sent_ref[:, :width] = (ADAPTER_SCALE * dot(latt_ref[...], query_gradient)).astype(jnp.bfloat16)
    sent_ref[:, width:] = (ADAPTER_SCALE * dot_nt(up, query_gradient)).astype(jnp.bfloat16)


def down_kernel(n_slots, n_row, width, *refs):
    parts, hidden, even_ref, odd_ref = refs[:n_slots], refs[n_slots], *refs[n_slots + 1 :]
    row = lax.axis_index("row")
    depth = even_ref.shape[1] - width
    slot_tokens = parts[0].shape[1] - width
    up = parts[0][:, :width].astype(jnp.float32)
    for part in parts[1:]:
        up = up + part[:, :width].astype(jnp.float32)
    up = up.astype(jnp.bfloat16)
    slots = [slot_of(slot_tokens, n_slots, j) for j in range(n_slots)]
    for i in range(n_row):
        out = odd_ref if i & 1 else even_ref
        rows = slice((i >> 1) * RANK, ((i >> 1) + 1) * RANK)
        cols = pl.ds(pl.multiple_of((row ^ i) * depth, depth), depth)
        grad = jnp.zeros((RANK, depth), jnp.float32)
        for j in range(n_slots):
            grad += dot(parts[j][:, width:], hidden[slots[j], cols])
        out[rows, :depth] = grad.astype(jnp.bfloat16)
        out[rows, depth:] = up


def finish_kernel(n_row, tokens, ids, *refs):
    pairs, (down_ref, up_ref, down) = refs[: n_row // 2], refs[n_row // 2 :]
    row = lax.axis_index("row")
    depth = down.shape[1]
    down[...] = jnp.zeros_like(down)
    up_ref[...] = jnp.zeros_like(up_ref)
    for i in range(n_row):
        at = pl.ds(adapter_of(ids, row ^ i, tokens), RANK)
        part = pairs[i >> 1][(i & 1) * RANK : ((i & 1) + 1) * RANK, :]
        down[at, :] += part[:, :depth].astype(jnp.float32)
        up_ref[at, :] += part[:, depth:].astype(jnp.float32)
    down_ref[...] = down[...].T


def place_kernel(n_slots, *refs):
    parts, out, sems = refs[:n_slots], *refs[n_slots:]
    slot_tokens = parts[0].shape[0]
    for copy in fetch(
        [(parts[j], out.at[slot_of(slot_tokens, n_slots, j), :]) for j in range(n_slots)], sems
    ):
        copy.wait()


def shards(
    hidden_in,
    frozen_query_base,
    k_prefix,
    v_prefix,
    tree_mask,
    adapter_ids,
    a_down,
    up_weight_matrix,
    cotangent,
):
    tokens, model = hidden_in.shape
    width = frozen_query_base.shape[1]
    heads = width // HD
    depth, rank_cols = a_down.shape
    local_keys = k_prefix.shape[0]
    n_pre, n_row = lax.axis_size("pre"), lax.axis_size("row")
    n_slots = min(n_pre, tokens // MIN_TOKENS)
    slot_tokens = tokens // n_slots
    bf16, f32 = jnp.bfloat16, jnp.float32
    slices = min(n_row, local_keys // MB)
    drop = (n_row // slices).bit_length() - 1
    part_rows = local_keys // slices
    students, blocks = tree_mask.shape

    away = pl.pallas_call(
        functools.partial(away_kernel, drop, part_rows),
        out_shape=jax.ShapeDtypeStruct((2 * part_rows + mask_rows(tree_mask), HD), bf16),
        in_specs=[HBM] * 3,
        out_specs=VMEM,
        scratch_shapes=[pltpu.VMEM((students, blocks), jnp.int32), pltpu.SemaphoreType.DMA((5,))],
        compiler_params=params(56),
        name="away",
    )(k_prefix, v_prefix, tree_mask)

    away, a_down = lax.optimization_barrier((away, a_down))
    slots = pl.pallas_call(
        functools.partial(pick_kernel, n_row, tokens),
        out_shape=jax.ShapeDtypeStruct((n_row * RANK * depth // HD, HD), bf16),
        in_specs=[SMEM, VMEM],
        out_specs=VMEM,
        scratch_shapes=[pltpu.VMEM((rank_cols, depth), f32)],
        compiler_params=params(16),
        name="pick",
    )(adapter_ids, a_down)
    far_plane = n_pre >> 1
    planes = {0: away, far_plane: swap(away, "pre", far_plane)}
    for bit in range(n_pre.bit_length() - 2)[::-1]:
        for m in sorted(planes):
            planes[m | 1 << bit] = swap(planes[m], "pre", 1 << bit)
    far = list(range(max(drop, 1), n_row.bit_length() - 1))[::-1]
    turn = len(far) // 2
    orders = [order + ([0] if drop == 0 else []) for order in (far, far[turn:] + far[:turn])]

    piece_rows = depth // (2 * HD) * RANK
    columns = [
        [slots[(a * n_row + i) * piece_rows : (a * n_row + i + 1) * piece_rows] for i in range(n_row)]
        for a in range(2)
    ]

    def moved(bit):
        return [i for i in range(n_row) if i >> bit & 1]

    def put(a, bit, got):
        for n, i in enumerate(moved(bit)):
            columns[a][i] = got[n * piece_rows : (n + 1) * piece_rows]

    core = moved(0)
    got = swap(jnp.concatenate([columns[a][i] for a in range(2) for i in core]), "row", 1)
    got, planes[far_plane] = lax.optimization_barrier((got, planes[far_plane]))
    put(0, 0, got[: len(core) * piece_rows])
    put(1, 0, got[len(core) * piece_rows :])
    for a in range(2):
        for bit in range(1, n_row.bit_length() - 1):
            if bit != orders[a][0]:
                put(a, bit, swap(jnp.concatenate([columns[a][i] for i in moved(bit)]), "row", 1 << bit))
    planes = [planes[j] for j in range(1, n_pre)]
    planes, columns = lax.optimization_barrier((planes, columns))
    masks = jnp.stack(
        [tree_mask]
        + [plane[2 * part_rows : 2 * part_rows + students, :blocks].astype(jnp.int32) for plane in planes]
    )

    first = lax.axis_index("pre") % n_slots * slot_tokens
    hid, base, cot = (lax.dynamic_slice_in_dim(x, first, slot_tokens, 0) for x in (hidden_in, frozen_query_base, cotangent))
    up = up_weight_matrix
    rows = heads * slot_tokens
    state = [jax.ShapeDtypeStruct((rows, c), f32) for c in (HD, HD, 3 * HD)]

    def attention(group, first, last, operands, in_specs, out_shape, scratch):
        sources, places = [], []
        for a, i, place in group:
            for array, _ in place:
                if not any(array is other for other in sources):
                    sources.append(array)
            index = [[array is other for other in sources].index(True) for array, _ in place]
            places.append((a, i, [(n, begin) for n, (_, begin) in zip(index, place)]))
        keys = len(places) * (n_pre - 1) * part_rows // 2 + (local_keys if first else 0)
        return pl.pallas_call(
            functools.partial(
                attention_kernel, n_pre, drop, part_rows, places, len(sources), first, last, tokens
            ),
            out_shape=out_shape,
            in_specs=[SMEM, VMEM, VMEM] + in_specs + [VMEM] * len(sources),
            out_specs=[VMEM] * len(out_shape),
            scratch_shapes=[
                pltpu.VMEM((keys, 2 * HD), bf16),
                pltpu.VMEM((rows, HD), bf16),
                pltpu.VMEM((rows, HD), bf16),
            ]
            + scratch,
            compiler_params=params(24 + keys * HD * 8 // MIB),
            cost_estimate=pl.CostEstimate(
                flops=4 * rows * keys * HD, bytes_accessed=keys * HD * 4, transcendentals=rows * keys // 2
            ),
            name="first_keys" if first else "last_keys" if last else "next_keys",
        )(masks, queries, cot, *operands, *sources)

    rounds = len(orders[0])
    away_rows = (n_pre - 1) * part_rows
    parts = [
        {0: jnp.concatenate([plane[a * part_rows : (a + 1) * part_rows] for plane in planes])}
        for a in range(2)
    ]
    groups = [[], [], []]
    for a in range(2):
        groups[0].append((a, 0, [(plane, a * part_rows) for plane in planes]))
    for k in range(rounds):
        got = []
        for a in range(2):
            bit = orders[a][k]
            payload = list(parts[a].values())
            if k == 0:
                payload += [columns[a][i] for i in moved(bit)]
            got.append(swap(jnp.concatenate(payload), "row", 1 << bit))
            if k == 0:
                put(a, bit, got[a][away_rows:])
        if k == 0:
            queries, latent_t = pl.pallas_call(
                functools.partial(query_kernel, n_row, tokens),
                out_shape=[
                    jax.ShapeDtypeStruct((slot_tokens, width), bf16),
                    jax.ShapeDtypeStruct((RANK, slot_tokens), bf16),
                ],
                in_specs=[SMEM] + [VMEM] * 5,
                out_specs=[VMEM] * 2,
                compiler_params=params(16),
                name="queries",
            )(adapter_ids, hid, base, up, *(jnp.concatenate(c) for c in columns))
        if k == rounds - 2:
            held = attention(groups[0], True, False, (k_prefix, v_prefix), [VMEM] * 2, state, [])
            got, held = lax.optimization_barrier((got, held))
        for a in range(2):
            for n, m in enumerate(list(parts[a])):
                there = m | 1 << orders[a][k]
                parts[a][there] = got[a][n * away_rows : (n + 1) * away_rows]
                place = [(got[a], n * away_rows + j * part_rows) for j in range(n_pre - 1)]
                groups[max(0, k + 3 - rounds)].append((a, there >> drop, place))
    held = attention(groups[1], False, False, held, [VMEM] * 3, state, [])
    attended, sent = attention(
        groups[2],
        False,
        True,
        (*held, adapter_ids, latent_t, up),
        [VMEM] * 3 + [SMEM] + [VMEM] * 2,
        [
            jax.ShapeDtypeStruct((slot_tokens, width), bf16),
            jax.ShapeDtypeStruct((RANK, width + slot_tokens), bf16),
        ],
        [pltpu.VMEM(s.shape, s.dtype) for s in state] + [pltpu.VMEM((slot_tokens, width), bf16)],
    )

    far_slot = n_slots >> 1
    attended_parts = {far_slot: swap(attended, "pre", far_slot)}
    shared = [swap(sent, "pre", j) for j in range(n_slots)]

    pairs = n_row // 2
    even, odd = pl.pallas_call(
        functools.partial(down_kernel, n_slots, n_row, width),
        out_shape=[jax.ShapeDtypeStruct((pairs * RANK, depth + width), bf16)] * 2,
        in_specs=[VMEM] * (n_slots + 1),
        out_specs=[VMEM] * 2,
        compiler_params=params(16),
        name="down",
    )(*shared, hidden_in)
    odd = swap(odd, "row", 1)
    spans = [slice(m * RANK, (m + 1) * RANK) for m in range(pairs)]
    pieces = [swap(jnp.concatenate([even[at], odd[at]]), "row", 2 * m) for m, at in enumerate(spans)]

    attended_parts[0] = attended
    pieces, attended_parts[far_slot] = lax.optimization_barrier((pieces, attended_parts[far_slot]))
    for bit in range(n_slots.bit_length() - 2)[::-1]:
        for m in list(attended_parts):
            attended_parts[m | 1 << bit] = swap(attended_parts[m], "pre", 1 << bit)

    grad_a, up_weight_gradient = pl.pallas_call(
        functools.partial(finish_kernel, n_row, tokens),
        out_shape=[
            jax.ShapeDtypeStruct((depth, rank_cols), f32),
            jax.ShapeDtypeStruct((rank_cols, width), f32),
        ],
        in_specs=[SMEM] + [VMEM] * pairs,
        out_specs=[VMEM] * 2,
        scratch_shapes=[pltpu.VMEM((rank_cols, depth), f32)],
        compiler_params=params(16),
        name="finish",
    )(adapter_ids, *pieces)

    attended = pl.pallas_call(
        functools.partial(place_kernel, n_slots),
        out_shape=jax.ShapeDtypeStruct((tokens, width), bf16),
        in_specs=[VMEM] * n_slots,
        out_specs=HBM,
        scratch_shapes=[pltpu.SemaphoreType.DMA((n_slots,))],
        compiler_params=params(16),
        cost_estimate=pl.CostEstimate(
            flops=100 * tokens * width * HD, bytes_accessed=100 * tokens * width, transcendentals=0
        ),
        name="place",
    )(*(attended_parts[j] for j in range(n_slots)))
    return attended, grad_a, up_weight_gradient


def solution(mesh):
    in_specs = (
        P("row", None),
        P("row", None),
        P("pre", None),
        P("pre", None),
        P(None, "pre"),
        P(),
        P("row", None),
        P(),
        P("row", None),
    )
    out_specs = (P("row", None), P("row", None), P())
    return jax.shard_map(shards, mesh=mesh, in_specs=in_specs, out_specs=out_specs, check_vma=False)
```

```python
import functools
import math

import jax
import jax.numpy as jnp
from jax import lax
from jax.experimental import pallas as pl
from jax.experimental.pallas import tpu as pltpu
from jax.sharding import PartitionSpec as P

HD = 128
RANK = 16
CONT = 512
MB = 128
CHUNK = 1024
ROW_TILE = 1024
MIN_TOKENS = 16
ADAPTER_SCALE = 2.0
VERY_LOW = -1e30
LOG2E = 1.4426950408889634
MIB = 1 << 20

NT = (((1,), (1,)), ((), ()))
VMEM = pl.BlockSpec(memory_space=pltpu.VMEM)
SMEM = pl.BlockSpec(memory_space=pltpu.SMEM)
HBM = pl.BlockSpec(memory_space=pltpu.HBM)


def dot(a, b):
    return jnp.dot(a, b, preferred_element_type=jnp.float32)


def dot_nt(a, b):
    return lax.dot_general(a, b, NT, preferred_element_type=jnp.float32)


def swap(x, axis, mask):
    if mask == 0:
        return x
    return lax.ppermute(x, axis, [(s, s ^ mask) for s in range(lax.axis_size(axis))])


def params(mib):
    return pltpu.CompilerParams(vmem_limit_bytes=mib * MIB)


def adapter_of(ids, row, tokens):
    return pl.multiple_of(ids[row * tokens // CONT] * RANK, RANK)


def slot_of(slot_tokens, n_slots, offset=0):
    slot = lax.rem(lax.axis_index("pre"), n_slots) ^ offset
    return pl.ds(pl.multiple_of(slot * slot_tokens, slot_tokens), slot_tokens)


def fetch(pairs, sems):
    copies = [pltpu.make_async_copy(src, dst, sems.at[i]) for i, (src, dst) in enumerate(pairs)]
    for copy in copies:
        copy.start()
    return copies


def mask_rows(mask):
    return -(-mask.shape[0] // 16) * 16


def away_kernel(drop, part_rows, k_ref, v_ref, mask_ref, away_ref, mask_in, sems):
    half = part_rows // 2
    begin = (lax.axis_index("row") >> drop) * part_rows
    pairs = [(mask_ref, mask_in)]
    for a in range(2):
        span = pl.ds(pl.multiple_of(begin + a * half, half), half)
        pairs.append((k_ref.at[span, :], away_ref.at[pl.ds(2 * a * half, half), :]))
        pairs.append((v_ref.at[span, :], away_ref.at[pl.ds((2 * a + 1) * half, half), :]))
    copies = fetch(pairs, sems)
    students, blocks = mask_in.shape
    copies[0].wait()
    away_ref[2 * part_rows :, :] = jnp.zeros_like(away_ref[2 * part_rows :, :])
    away_ref[2 * part_rows : 2 * part_rows + students, :blocks] = mask_in[...].astype(jnp.bfloat16)
    for copy in copies[1:]:
        copy.wait()


def pick_kernel(n_row, tokens, ids, a_ref, slots_ref, at):
    row = lax.axis_index("row")
    cols = a_ref.shape[0] // (2 * HD)
    at[...] = a_ref[...].astype(jnp.float32).T
    for i in range(n_row):
        piece = at[pl.ds(adapter_of(ids, row ^ i, tokens), RANK), :].astype(jnp.bfloat16)
        for half in range(2):
            for c in range(cols):
                first = ((half * n_row + i) * cols + c) * RANK
                lane = (half * cols + c) * HD
                slots_ref[first : first + RANK, :] = piece[:, lane : lane + HD]


def query_kernel(n_row, tokens, ids, hid, base, up_ref, low, high, q_ref, latt_ref):
    row = lax.axis_index("row")
    slot_tokens = q_ref.shape[0]
    cols = low.shape[0] // (n_row * RANK)
    span = cols * HD
    latent = jnp.zeros((slot_tokens, RANK), jnp.float32)
    for i in range(n_row):
        for half, ref in enumerate((low, high)):
            firsts = [(i * cols + c) * RANK for c in range(cols)]
            piece = jnp.concatenate([ref[first : first + RANK, :] for first in firsts], axis=1)
            block = hid[:, pl.ds(pl.multiple_of(((row ^ i) * 2 + half) * span, span), span)]
            latent += dot_nt(block, piece)
    latent = latent.astype(jnp.bfloat16)
    square = (RANK, RANK)
    same = lax.broadcasted_iota(jnp.int32, square, 0) == lax.broadcasted_iota(jnp.int32, square, 1)
    eye = jnp.where(same, 1.0, 0.0).astype(jnp.bfloat16)
    latt_ref[...] = dot_nt(eye, latent).astype(jnp.bfloat16)
    up = up_ref[pl.ds(adapter_of(ids, row, tokens), RANK), :]
    raised = dot(latent, up)
    q_ref[...] = (base[...].astype(jnp.float32) + ADAPTER_SCALE * raised).astype(jnp.bfloat16)


def attention_kernel(n_pre, drop, part_rows, places, n_sources, first, last, tokens, *refs):
    masks, q_ref, cot_ref = refs[:3]
    refs = refs[3:]
    if first:
        k_own, v_own, refs = refs[0], refs[1], refs[2:]
    else:
        held, refs = refs[:3], refs[3:]
    if last:
        ids, latt_ref, up_ref, refs = *refs[:3], refs[3:]
    sources, refs = refs[:n_sources], refs[n_sources:]
    if last:
        att_ref, sent_ref, kv, q, cot, top, total, acc, grads = refs
    else:
        top, total, acc, kv, q, cot = refs
    row = lax.axis_index("row")
    slot_tokens, width = q_ref.shape
    heads = width // HD
    rows = heads * slot_tokens
    tile = min(ROW_TILE, rows)
    scale = 1.0 / math.sqrt(HD)
    factor = scale * LOG2E

    student = row * tokens // CONT
    half = part_rows // 2
    unit = min(MB, half)

    def keep(count, live, key_block, value_block):
        at = pl.ds(pl.multiple_of(count * unit, unit), unit)
        kv[at, :HD] = value_block()
        kv[at, HD:] = key_block()
        return count + live.astype(jnp.int32)

    def own_block(b, count):
        at = pl.ds(pl.multiple_of(b * unit, unit), unit)
        live = masks[0, student, b * unit // MB] > 0
        return keep(count, live, lambda: k_own[at, :], lambda: v_own[at, :])

    def block_of(source, begin):
        return lambda: sources[source][begin : begin + unit, :]

    count = jnp.int32(0)
    if first:
        count = lax.fori_loop(0, k_own.shape[0] // unit, own_block, count)
    for a, i, place in places:
        piece = (row >> drop) ^ i
        for j in range(1, n_pre):
            source, begin = place[j - 1]
            for u in range(half // unit):
                block = (piece * part_rows + a * half + u * unit) // MB
                count = keep(
                    count,
                    masks[j, student, block] > 0,
                    block_of(source, begin + u * unit),
                    block_of(source, begin + half + u * unit),
                )

    for h in range(heads):
        at = pl.ds(h * slot_tokens, slot_tokens)
        q[at, :] = q_ref[:, h * HD : (h + 1) * HD]
        cot[at, :] = cot_ref[:, h * HD : (h + 1) * HD]
    if first:
        top[...] = jnp.full_like(top, VERY_LOW)
        total[...] = jnp.zeros_like(total)
        acc[...] = jnp.zeros_like(acc)
    else:
        for ref, given in zip((top, total, acc), held):
            ref[...] = given[...]

    def step(begin, size):
        both = kv[pl.ds(pl.multiple_of(begin, unit), size), :]
        values, keys = both[:, :HD], both[:, HD:]
        lane = min(size, HD)
        lanes = size // lane
        for r0 in range(0, rows, tile):
            at = pl.ds(r0, tile)
            scores = dot_nt(q[at, :], keys)
            old = top[at, :]
            new = jnp.maximum(old, jnp.max(scores, axis=1, keepdims=True))
            top[at, :] = new
            weights = jnp.exp2((scores - jnp.concatenate([new[:, :lane]] * lanes, axis=1)) * factor)
            shrink = jnp.exp2((old - new) * factor)
            partial = weights[:, :lane]
            for c in range(1, lanes):
                partial = partial + weights[:, c * lane : (c + 1) * lane]
            total[at, :] *= shrink
            total[at, :lane] += partial
            grad_weights = (weights * dot_nt(cot[at, :], values)).astype(jnp.bfloat16)
            first_two = dot(weights.astype(jnp.bfloat16), both)
            last = dot(grad_weights, keys)
            acc[at, :HD] = acc[at, :HD] * shrink + first_two[:, :HD]
            acc[at, HD : 2 * HD] = acc[at, HD : 2 * HD] * shrink + first_two[:, HD:]
            acc[at, 2 * HD :] = acc[at, 2 * HD :] * shrink + last

    per_chunk = CHUNK // unit
    full = count // per_chunk

    def full_step(c, carry):
        step(c * CHUNK, CHUNK)
        return carry

    lax.fori_loop(0, full, full_step, 0)
    size = CHUNK // 2
    while size >= unit:
        done = count // (2 * size // unit) * (2 * size)
        pl.when(count * unit - done >= size)(functools.partial(step, done, size))
        size //= 2
    if not last:
        return

    for h in range(heads):
        at = pl.ds(h * slot_tokens, slot_tokens)
        inverse = 1.0 / jnp.sum(total[at, :], axis=1, keepdims=True)
        attended = (acc[at, :HD] * inverse).astype(jnp.bfloat16)
        att_ref[:, h * HD : (h + 1) * HD] = attended
        delta = jnp.sum(
            cot[at, :].astype(jnp.float32) * attended.astype(jnp.float32), axis=1, keepdims=True
        )
        grad = (acc[at, 2 * HD :] - delta * acc[at, HD : 2 * HD]) * (inverse * scale)
        grads[:, h * HD : (h + 1) * HD] = grad.astype(jnp.bfloat16)
    query_gradient = grads[...]
    up = up_ref[pl.ds(adapter_of(ids, row, tokens), RANK), :]
    sent_ref[:, :width] = (ADAPTER_SCALE * dot(latt_ref[...], query_gradient)).astype(jnp.bfloat16)
    sent_ref[:, width:] = (ADAPTER_SCALE * dot_nt(up, query_gradient)).astype(jnp.bfloat16)


def down_kernel(n_slots, n_row, width, *refs):
    parts, hidden, even_ref, odd_ref = refs[:n_slots], refs[n_slots], *refs[n_slots + 1 :]
    row = lax.axis_index("row")
    depth = even_ref.shape[1] - width
    slot_tokens = parts[0].shape[1] - width
    up = parts[0][:, :width].astype(jnp.float32)
    for part in parts[1:]:
        up = up + part[:, :width].astype(jnp.float32)
    up = up.astype(jnp.bfloat16)
    slots = [slot_of(slot_tokens, n_slots, j) for j in range(n_slots)]
    for i in range(n_row):
        out = odd_ref if i & 1 else even_ref
        rows = slice((i >> 1) * RANK, ((i >> 1) + 1) * RANK)
        cols = pl.ds(pl.multiple_of((row ^ i) * depth, depth), depth)
        grad = jnp.zeros((RANK, depth), jnp.float32)
        for j in range(n_slots):
            grad += dot(parts[j][:, width:], hidden[slots[j], cols])
        out[rows, :depth] = grad.astype(jnp.bfloat16)
        out[rows, depth:] = up


def finish_kernel(n_row, tokens, ids, *refs):
    pairs, (down_ref, up_ref, down) = refs[: n_row // 2], refs[n_row // 2 :]
    row = lax.axis_index("row")
    depth = down.shape[1]
    down[...] = jnp.zeros_like(down)
    up_ref[...] = jnp.zeros_like(up_ref)
    for i in range(n_row):
        at = pl.ds(adapter_of(ids, row ^ i, tokens), RANK)
        part = pairs[i >> 1][(i & 1) * RANK : ((i & 1) + 1) * RANK, :]
        down[at, :] += part[:, :depth].astype(jnp.float32)
        up_ref[at, :] += part[:, depth:].astype(jnp.float32)
    down_ref[...] = down[...].T


def place_kernel(n_slots, *refs):
    parts, out, sems = refs[:n_slots], *refs[n_slots:]
    slot_tokens = parts[0].shape[0]
    for copy in fetch(
        [(parts[j], out.at[slot_of(slot_tokens, n_slots, j), :]) for j in range(n_slots)], sems
    ):
        copy.wait()


def shards(
    hidden_in,
    frozen_query_base,
    k_prefix,
    v_prefix,
    tree_mask,
    adapter_ids,
    a_down,
    up_weight_matrix,
    cotangent,
):
    tokens, model = hidden_in.shape
    width = frozen_query_base.shape[1]
    heads = width // HD
    depth, rank_cols = a_down.shape
    local_keys = k_prefix.shape[0]
    n_pre, n_row = lax.axis_size("pre"), lax.axis_size("row")
    n_slots = min(n_pre, tokens // MIN_TOKENS)
    slot_tokens = tokens // n_slots
    bf16, f32 = jnp.bfloat16, jnp.float32
    slices = min(n_row, local_keys // MB)
    drop = (n_row // slices).bit_length() - 1
    part_rows = local_keys // slices
    students, blocks = tree_mask.shape

    away = pl.pallas_call(
        functools.partial(away_kernel, drop, part_rows),
        out_shape=jax.ShapeDtypeStruct((2 * part_rows + mask_rows(tree_mask), HD), bf16),
        in_specs=[HBM] * 3,
        out_specs=VMEM,
        scratch_shapes=[pltpu.VMEM((students, blocks), jnp.int32), pltpu.SemaphoreType.DMA((5,))],
        compiler_params=params(56),
        name="away",
    )(k_prefix, v_prefix, tree_mask)

    away, a_down = lax.optimization_barrier((away, a_down))
    slots = pl.pallas_call(
        functools.partial(pick_kernel, n_row, tokens),
        out_shape=jax.ShapeDtypeStruct((n_row * RANK * depth // HD, HD), bf16),
        in_specs=[SMEM, VMEM],
        out_specs=VMEM,
        scratch_shapes=[pltpu.VMEM((rank_cols, depth), f32)],
        compiler_params=params(16),
        name="pick",
    )(adapter_ids, a_down)
    far_plane = n_pre >> 1
    planes = {0: away, far_plane: swap(away, "pre", far_plane)}
    for bit in range(n_pre.bit_length() - 2)[::-1]:
        for m in sorted(planes):
            planes[m | 1 << bit] = swap(planes[m], "pre", 1 << bit)
    far = list(range(max(drop, 1), n_row.bit_length() - 1))[::-1]
    turn = len(far) // 2
    orders = [order + ([0] if drop == 0 else []) for order in (far, far[turn:] + far[:turn])]

    piece_rows = depth // (2 * HD) * RANK
    columns = [
        [slots[(a * n_row + i) * piece_rows : (a * n_row + i + 1) * piece_rows] for i in range(n_row)]
        for a in range(2)
    ]

    def moved(bit):
        return [i for i in range(n_row) if i >> bit & 1]

    def put(a, bit, got):
        for n, i in enumerate(moved(bit)):
            columns[a][i] = got[n * piece_rows : (n + 1) * piece_rows]

    core = moved(0)
    got = swap(jnp.concatenate([columns[a][i] for a in range(2) for i in core]), "row", 1)
    got, planes[far_plane] = lax.optimization_barrier((got, planes[far_plane]))
    put(0, 0, got[: len(core) * piece_rows])
    put(1, 0, got[len(core) * piece_rows :])
    for a in range(2):
        for bit in range(1, n_row.bit_length() - 1):
            if bit != orders[a][0]:
                put(a, bit, swap(jnp.concatenate([columns[a][i] for i in moved(bit)]), "row", 1 << bit))
    planes = [planes[j] for j in range(1, n_pre)]
    planes, columns = lax.optimization_barrier((planes, columns))
    masks = jnp.stack(
        [tree_mask]
        + [plane[2 * part_rows : 2 * part_rows + students, :blocks].astype(jnp.int32) for plane in planes]
    )

    first = lax.axis_index("pre") % n_slots * slot_tokens
    hid, base, cot = (lax.dynamic_slice_in_dim(x, first, slot_tokens, 0) for x in (hidden_in, frozen_query_base, cotangent))
    up = up_weight_matrix
    rows = heads * slot_tokens
    state = [jax.ShapeDtypeStruct((rows, c), f32) for c in (HD, HD, 3 * HD)]

    def attention(group, first, last, operands, in_specs, out_shape, scratch):
        sources, places = [], []
        for a, i, place in group:
            for array, _ in place:
                if not any(array is other for other in sources):
                    sources.append(array)
            index = [[array is other for other in sources].index(True) for array, _ in place]
            places.append((a, i, [(n, begin) for n, (_, begin) in zip(index, place)]))
        keys = len(places) * (n_pre - 1) * part_rows // 2 + (local_keys if first else 0)
        return pl.pallas_call(
            functools.partial(
                attention_kernel, n_pre, drop, part_rows, places, len(sources), first, last, tokens
            ),
            out_shape=out_shape,
            in_specs=[SMEM, VMEM, VMEM] + in_specs + [VMEM] * len(sources),
            out_specs=[VMEM] * len(out_shape),
            scratch_shapes=[
                pltpu.VMEM((keys, 2 * HD), bf16),
                pltpu.VMEM((rows, HD), bf16),
                pltpu.VMEM((rows, HD), bf16),
            ]
            + scratch,
            compiler_params=params(24 + keys * HD * 8 // MIB),
            cost_estimate=pl.CostEstimate(
                flops=4 * rows * keys * HD, bytes_accessed=keys * HD * 4, transcendentals=rows * keys // 2
            ),
            name="first_keys" if first else "last_keys" if last else "next_keys",
        )(masks, queries, cot, *operands, *sources)

    rounds = len(orders[0])
    away_rows = (n_pre - 1) * part_rows
    parts = [
        {0: jnp.concatenate([plane[a * part_rows : (a + 1) * part_rows] for plane in planes])}
        for a in range(2)
    ]
    groups = [[], [], []]
    for a in range(2):
        groups[0].append((a, 0, [(plane, a * part_rows) for plane in planes]))
    for k in range(rounds):
        got = []
        for a in range(2):
            bit = orders[a][k]
            payload = list(parts[a].values())
            if k == 0:
                payload += [columns[a][i] for i in moved(bit)]
            got.append(swap(jnp.concatenate(payload), "row", 1 << bit))
            if k == 0:
                put(a, bit, got[a][away_rows:])
        if k == 0:
            queries, latent_t = pl.pallas_call(
                functools.partial(query_kernel, n_row, tokens),
                out_shape=[
                    jax.ShapeDtypeStruct((slot_tokens, width), bf16),
                    jax.ShapeDtypeStruct((RANK, slot_tokens), bf16),
                ],
                in_specs=[SMEM] + [VMEM] * 5,
                out_specs=[VMEM] * 2,
                compiler_params=params(16),
                name="queries",
            )(adapter_ids, hid, base, up, *(jnp.concatenate(c) for c in columns))
        if k == rounds - 2:
            held = attention(groups[0], True, False, (k_prefix, v_prefix), [VMEM] * 2, state, [])
            got, held = lax.optimization_barrier((got, held))
        for a in range(2):
            for n, m in enumerate(list(parts[a])):
                there = m | 1 << orders[a][k]
                parts[a][there] = got[a][n * away_rows : (n + 1) * away_rows]
                place = [(got[a], n * away_rows + j * part_rows) for j in range(n_pre - 1)]
                groups[max(0, k + 3 - rounds)].append((a, there >> drop, place))
    held = attention(groups[1], False, False, held, [VMEM] * 3, state, [])
    attended, sent = attention(
        groups[2],
        False,
        True,
        (*held, adapter_ids, latent_t, up),
        [VMEM] * 3 + [SMEM] + [VMEM] * 2,
        [
            jax.ShapeDtypeStruct((slot_tokens, width), bf16),
            jax.ShapeDtypeStruct((RANK, width + slot_tokens), bf16),
        ],
        [pltpu.VMEM(s.shape, s.dtype) for s in state] + [pltpu.VMEM((slot_tokens, width), bf16)],
    )

    shared = [swap(sent, "pre", j) for j in range(n_slots)]
    attended, shared = lax.optimization_barrier((attended, shared))
    far_slot = n_slots >> 1
    attended_parts = {far_slot: swap(attended, "pre", far_slot)}

    pairs = n_row // 2
    even, odd = pl.pallas_call(
        functools.partial(down_kernel, n_slots, n_row, width),
        out_shape=[jax.ShapeDtypeStruct((pairs * RANK, depth + width), bf16)] * 2,
        in_specs=[VMEM] * (n_slots + 1),
        out_specs=[VMEM] * 2,
        compiler_params=params(16),
        name="down",
    )(*shared, hidden_in)
    odd = swap(odd, "row", 1)
    spans = [slice(m * RANK, (m + 1) * RANK) for m in range(pairs)]
    pieces = [swap(jnp.concatenate([even[at], odd[at]]), "row", 2 * m) for m, at in enumerate(spans)]

    attended_parts[0] = attended
    pieces, attended_parts[far_slot] = lax.optimization_barrier((pieces, attended_parts[far_slot]))
    for bit in range(n_slots.bit_length() - 2)[::-1]:
        for m in list(attended_parts):
            attended_parts[m | 1 << bit] = swap(attended_parts[m], "pre", 1 << bit)

    grad_a, up_weight_gradient = pl.pallas_call(
        functools.partial(finish_kernel, n_row, tokens),
        out_shape=[
            jax.ShapeDtypeStruct((depth, rank_cols), f32),
            jax.ShapeDtypeStruct((rank_cols, width), f32),
        ],
        in_specs=[SMEM] + [VMEM] * pairs,
        out_specs=[VMEM] * 2,
        scratch_shapes=[pltpu.VMEM((rank_cols, depth), f32)],
        compiler_params=params(16),
        name="finish",
    )(adapter_ids, *pieces)

    attended = pl.pallas_call(
        functools.partial(place_kernel, n_slots),
        out_shape=jax.ShapeDtypeStruct((tokens, width), bf16),
        in_specs=[VMEM] * n_slots,
        out_specs=HBM,
        scratch_shapes=[pltpu.SemaphoreType.DMA((n_slots,))],
        compiler_params=params(16),
        cost_estimate=pl.CostEstimate(
            flops=100 * tokens * width * HD, bytes_accessed=100 * tokens * width, transcendentals=0
        ),
        name="place",
    )(*(attended_parts[j] for j in range(n_slots)))
    return attended, grad_a, up_weight_gradient


def solution(mesh):
    in_specs = (
        P("row", None),
        P("row", None),
        P("pre", None),
        P("pre", None),
        P(None, "pre"),
        P(),
        P("row", None),
        P(),
        P("row", None),
    )
    out_specs = (P("row", None), P("row", None), P())
    return jax.shard_map(shards, mesh=mesh, in_specs=in_specs, out_specs=out_specs, check_vma=False)
```

```python
import functools
import math

import jax
import jax.numpy as jnp
from jax import lax
from jax.experimental import pallas as pl
from jax.experimental.pallas import tpu as pltpu
from jax.sharding import PartitionSpec as P

HD = 128
RANK = 16
CONT = 512
MB = 128
CHUNK = 1024
ROW_TILE = 1024
MIN_TOKENS = 16
ADAPTER_SCALE = 2.0
VERY_LOW = -1e30
LOG2E = 1.4426950408889634
MIB = 1 << 20

NT = (((1,), (1,)), ((), ()))
VMEM = pl.BlockSpec(memory_space=pltpu.VMEM)
SMEM = pl.BlockSpec(memory_space=pltpu.SMEM)
HBM = pl.BlockSpec(memory_space=pltpu.HBM)


def dot(a, b):
    return jnp.dot(a, b, preferred_element_type=jnp.float32)


def dot_nt(a, b):
    return lax.dot_general(a, b, NT, preferred_element_type=jnp.float32)


def swap(x, axis, mask):
    if mask == 0:
        return x
    return lax.ppermute(x, axis, [(s, s ^ mask) for s in range(lax.axis_size(axis))])


def params(mib):
    return pltpu.CompilerParams(vmem_limit_bytes=mib * MIB)


def adapter_of(ids, row, tokens):
    return pl.multiple_of(ids[row * tokens // CONT] * RANK, RANK)


def slot_of(slot_tokens, n_slots, offset=0):
    slot = lax.rem(lax.axis_index("pre"), n_slots) ^ offset
    return pl.ds(pl.multiple_of(slot * slot_tokens, slot_tokens), slot_tokens)


def fetch(pairs, sems):
    copies = [pltpu.make_async_copy(src, dst, sems.at[i]) for i, (src, dst) in enumerate(pairs)]
    for copy in copies:
        copy.start()
    return copies


def mask_rows(mask):
    return -(-mask.shape[0] // 16) * 16


def away_kernel(drop, part_rows, k_ref, v_ref, mask_ref, away_ref, mask_in, sems):
    half = part_rows // 2
    begin = (lax.axis_index("row") >> drop) * part_rows
    pairs = [(mask_ref, mask_in)]
    for a in range(2):
        span = pl.ds(pl.multiple_of(begin + a * half, half), half)
        pairs.append((k_ref.at[span, :], away_ref.at[pl.ds(2 * a * half, half), :]))
        pairs.append((v_ref.at[span, :], away_ref.at[pl.ds((2 * a + 1) * half, half), :]))
    copies = fetch(pairs, sems)
    students, blocks = mask_in.shape
    copies[0].wait()
    away_ref[2 * part_rows :, :] = jnp.zeros_like(away_ref[2 * part_rows :, :])
    away_ref[2 * part_rows : 2 * part_rows + students, :blocks] = mask_in[...].astype(jnp.bfloat16)
    for copy in copies[1:]:
        copy.wait()


def pick_kernel(n_row, tokens, ids, a_ref, slots_ref, at):
    row = lax.axis_index("row")
    cols = a_ref.shape[0] // (2 * HD)
    at[...] = a_ref[...].astype(jnp.float32).T
    for i in range(n_row):
        piece = at[pl.ds(adapter_of(ids, row ^ i, tokens), RANK), :].astype(jnp.bfloat16)
        for half in range(2):
            for c in range(cols):
                first = ((half * n_row + i) * cols + c) * RANK
                lane = (half * cols + c) * HD
                slots_ref[first : first + RANK, :] = piece[:, lane : lane + HD]


def query_kernel(n_row, tokens, ids, hid, base, up_ref, low, high, q_ref, latt_ref):
    row = lax.axis_index("row")
    slot_tokens = q_ref.shape[0]
    cols = low.shape[0] // (n_row * RANK)
    span = cols * HD
    latent = jnp.zeros((slot_tokens, RANK), jnp.float32)
    for i in range(n_row):
        for half, ref in enumerate((low, high)):
            firsts = [(i * cols + c) * RANK for c in range(cols)]
            piece = jnp.concatenate([ref[first : first + RANK, :] for first in firsts], axis=1)
            block = hid[:, pl.ds(pl.multiple_of(((row ^ i) * 2 + half) * span, span), span)]
            latent += dot_nt(block, piece)
    latent = latent.astype(jnp.bfloat16)
    square = (RANK, RANK)
    same = lax.broadcasted_iota(jnp.int32, square, 0) == lax.broadcasted_iota(jnp.int32, square, 1)
    eye = jnp.where(same, 1.0, 0.0).astype(jnp.bfloat16)
    latt_ref[...] = dot_nt(eye, latent).astype(jnp.bfloat16)
    up = up_ref[pl.ds(adapter_of(ids, row, tokens), RANK), :]
    raised = dot(latent, up)
    q_ref[...] = (base[...].astype(jnp.float32) + ADAPTER_SCALE * raised).astype(jnp.bfloat16)


def attention_kernel(n_pre, drop, part_rows, places, n_sources, first, last, tokens, *refs):
    masks, q_ref, cot_ref = refs[:3]
    refs = refs[3:]
    if first:
        k_own, v_own, refs = refs[0], refs[1], refs[2:]
    else:
        held, refs = refs[:3], refs[3:]
    if last:
        ids, latt_ref, up_ref, refs = *refs[:3], refs[3:]
    sources, refs = refs[:n_sources], refs[n_sources:]
    if last:
        att_ref, sent_ref, kv, q, cot, top, total, acc, grads = refs
    else:
        top, total, acc, kv, q, cot = refs
    row = lax.axis_index("row")
    slot_tokens, width = q_ref.shape
    heads = width // HD
    rows = heads * slot_tokens
    tile = min(ROW_TILE, rows)
    scale = 1.0 / math.sqrt(HD)
    factor = scale * LOG2E

    student = row * tokens // CONT
    half = part_rows // 2
    unit = min(MB, half)

    def keep(count, live, key_block, value_block):
        at = pl.ds(pl.multiple_of(count * unit, unit), unit)
        kv[at, :HD] = value_block()
        kv[at, HD:] = key_block()
        return count + live.astype(jnp.int32)

    def own_block(b, count):
        at = pl.ds(pl.multiple_of(b * unit, unit), unit)
        live = masks[0, student, b * unit // MB] > 0
        return keep(count, live, lambda: k_own[at, :], lambda: v_own[at, :])

    def block_of(source, begin):
        return lambda: sources[source][begin : begin + unit, :]

    count = jnp.int32(0)
    if first:
        count = lax.fori_loop(0, k_own.shape[0] // unit, own_block, count)
    for a, i, place in places:
        piece = (row >> drop) ^ i
        for j in range(1, n_pre):
            source, begin = place[j - 1]
            for u in range(half // unit):
                block = (piece * part_rows + a * half + u * unit) // MB
                count = keep(
                    count,
                    masks[j, student, block] > 0,
                    block_of(source, begin + u * unit),
                    block_of(source, begin + half + u * unit),
                )

    for h in range(heads):
        at = pl.ds(h * slot_tokens, slot_tokens)
        q[at, :] = q_ref[:, h * HD : (h + 1) * HD]
        cot[at, :] = cot_ref[:, h * HD : (h + 1) * HD]
    if first:
        top[...] = jnp.full_like(top, VERY_LOW)
        total[...] = jnp.zeros_like(total)
        acc[...] = jnp.zeros_like(acc)
    else:
        for ref, given in zip((top, total, acc), held):
            ref[...] = given[...]

    def step(begin, size):
        both = kv[pl.ds(pl.multiple_of(begin, unit), size), :]
        values, keys = both[:, :HD], both[:, HD:]
        lane = min(size, HD)
        lanes = size // lane
        for r0 in range(0, rows, tile):
            at = pl.ds(r0, tile)
            scores = dot_nt(q[at, :], keys)
            old = top[at, :]
            new = jnp.maximum(old, jnp.max(scores, axis=1, keepdims=True))
            top[at, :] = new
            weights = jnp.exp2((scores - jnp.concatenate([new[:, :lane]] * lanes, axis=1)) * factor)
            shrink = jnp.exp2((old - new) * factor)
            partial = weights[:, :lane]
            for c in range(1, lanes):
                partial = partial + weights[:, c * lane : (c + 1) * lane]
            total[at, :] *= shrink
            total[at, :lane] += partial
            grad_weights = (weights * dot_nt(cot[at, :], values)).astype(jnp.bfloat16)
            first_two = dot(weights.astype(jnp.bfloat16), both)
            last = dot(grad_weights, keys)
            acc[at, :HD] = acc[at, :HD] * shrink + first_two[:, :HD]
            acc[at, HD : 2 * HD] = acc[at, HD : 2 * HD] * shrink + first_two[:, HD:]
            acc[at, 2 * HD :] = acc[at, 2 * HD :] * shrink + last

    per_chunk = CHUNK // unit
    full = count // per_chunk

    def full_step(c, carry):
        step(c * CHUNK, CHUNK)
        return carry

    lax.fori_loop(0, full, full_step, 0)
    rest = count * unit - full * CHUNK
    for blocks in range(1, CHUNK // MB):
        pl.when(rest // MB == blocks)(functools.partial(step, full * CHUNK, blocks * MB))
    if unit < MB:
        pl.when(rest % MB > 0)(functools.partial(step, (count - 1) * unit, unit))
    if not last:
        return

    for h in range(heads):
        at = pl.ds(h * slot_tokens, slot_tokens)
        inverse = 1.0 / jnp.sum(total[at, :], axis=1, keepdims=True)
        attended = (acc[at, :HD] * inverse).astype(jnp.bfloat16)
        att_ref[:, h * HD : (h + 1) * HD] = attended
        delta = jnp.sum(
            cot[at, :].astype(jnp.float32) * attended.astype(jnp.float32), axis=1, keepdims=True
        )
        grad = (acc[at, 2 * HD :] - delta * acc[at, HD : 2 * HD]) * (inverse * scale)
        grads[:, h * HD : (h + 1) * HD] = grad.astype(jnp.bfloat16)
    query_gradient = grads[...]
    up = up_ref[pl.ds(adapter_of(ids, row, tokens), RANK), :]
    sent_ref[:, :width] = (ADAPTER_SCALE * dot(latt_ref[...], query_gradient)).astype(jnp.bfloat16)
    sent_ref[:, width:] = (ADAPTER_SCALE * dot_nt(up, query_gradient)).astype(jnp.bfloat16)


def down_kernel(n_slots, n_row, width, *refs):
    parts, hidden, even_ref, odd_ref = refs[:n_slots], refs[n_slots], *refs[n_slots + 1 :]
    row = lax.axis_index("row")
    depth = even_ref.shape[1] - width
    slot_tokens = parts[0].shape[1] - width
    up = parts[0][:, :width].astype(jnp.float32)
    for part in parts[1:]:
        up = up + part[:, :width].astype(jnp.float32)
    up = up.astype(jnp.bfloat16)
    slots = [slot_of(slot_tokens, n_slots, j) for j in range(n_slots)]
    for i in range(n_row):
        out = odd_ref if i & 1 else even_ref
        rows = slice((i >> 1) * RANK, ((i >> 1) + 1) * RANK)
        cols = pl.ds(pl.multiple_of((row ^ i) * depth, depth), depth)
        grad = jnp.zeros((RANK, depth), jnp.float32)
        for j in range(n_slots):
            grad += dot(parts[j][:, width:], hidden[slots[j], cols])
        out[rows, :depth] = grad.astype(jnp.bfloat16)
        out[rows, depth:] = up


def finish_kernel(n_row, tokens, ids, *refs):
    pairs, (down_ref, up_ref, down) = refs[: n_row // 2], refs[n_row // 2 :]
    row = lax.axis_index("row")
    depth = down.shape[1]
    down[...] = jnp.zeros_like(down)
    up_ref[...] = jnp.zeros_like(up_ref)
    for i in range(n_row):
        at = pl.ds(adapter_of(ids, row ^ i, tokens), RANK)
        part = pairs[i >> 1][(i & 1) * RANK : ((i & 1) + 1) * RANK, :]
        down[at, :] += part[:, :depth].astype(jnp.float32)
        up_ref[at, :] += part[:, depth:].astype(jnp.float32)
    down_ref[...] = down[...].T


def place_kernel(n_slots, *refs):
    parts, out, sems = refs[:n_slots], *refs[n_slots:]
    slot_tokens = parts[0].shape[0]
    for copy in fetch(
        [(parts[j], out.at[slot_of(slot_tokens, n_slots, j), :]) for j in range(n_slots)], sems
    ):
        copy.wait()


def shards(
    hidden_in,
    frozen_query_base,
    k_prefix,
    v_prefix,
    tree_mask,
    adapter_ids,
    a_down,
    up_weight_matrix,
    cotangent,
):
    tokens, model = hidden_in.shape
    width = frozen_query_base.shape[1]
    heads = width // HD
    depth, rank_cols = a_down.shape
    local_keys = k_prefix.shape[0]
    n_pre, n_row = lax.axis_size("pre"), lax.axis_size("row")
    n_slots = min(n_pre, tokens // MIN_TOKENS)
    slot_tokens = tokens // n_slots
    bf16, f32 = jnp.bfloat16, jnp.float32
    slices = min(n_row, local_keys // MB)
    drop = (n_row // slices).bit_length() - 1
    part_rows = local_keys // slices
    students, blocks = tree_mask.shape

    away = pl.pallas_call(
        functools.partial(away_kernel, drop, part_rows),
        out_shape=jax.ShapeDtypeStruct((2 * part_rows + mask_rows(tree_mask), HD), bf16),
        in_specs=[HBM] * 3,
        out_specs=VMEM,
        scratch_shapes=[pltpu.VMEM((students, blocks), jnp.int32), pltpu.SemaphoreType.DMA((5,))],
        compiler_params=params(56),
        name="away",
    )(k_prefix, v_prefix, tree_mask)

    away, a_down = lax.optimization_barrier((away, a_down))
    slots = pl.pallas_call(
        functools.partial(pick_kernel, n_row, tokens),
        out_shape=jax.ShapeDtypeStruct((n_row * RANK * depth // HD, HD), bf16),
        in_specs=[SMEM, VMEM],
        out_specs=VMEM,
        scratch_shapes=[pltpu.VMEM((rank_cols, depth), f32)],
        compiler_params=params(16),
        name="pick",
    )(adapter_ids, a_down)
    far_plane = n_pre >> 1
    planes = {0: away, far_plane: swap(away, "pre", far_plane)}
    for bit in range(n_pre.bit_length() - 2)[::-1]:
        for m in sorted(planes):
            planes[m | 1 << bit] = swap(planes[m], "pre", 1 << bit)
    far = list(range(max(drop, 1), n_row.bit_length() - 1))[::-1]
    turn = len(far) // 2
    orders = [order + ([0] if drop == 0 else []) for order in (far, far[turn:] + far[:turn])]

    piece_rows = depth // (2 * HD) * RANK
    columns = [
        [slots[(a * n_row + i) * piece_rows : (a * n_row + i + 1) * piece_rows] for i in range(n_row)]
        for a in range(2)
    ]

    def moved(bit):
        return [i for i in range(n_row) if i >> bit & 1]

    def put(a, bit, got):
        for n, i in enumerate(moved(bit)):
            columns[a][i] = got[n * piece_rows : (n + 1) * piece_rows]

    core = moved(0)
    got = swap(jnp.concatenate([columns[a][i] for a in range(2) for i in core]), "row", 1)
    got, planes[far_plane] = lax.optimization_barrier((got, planes[far_plane]))
    put(0, 0, got[: len(core) * piece_rows])
    put(1, 0, got[len(core) * piece_rows :])
    for a in range(2):
        for bit in range(1, n_row.bit_length() - 1):
            if bit != orders[a][0]:
                put(a, bit, swap(jnp.concatenate([columns[a][i] for i in moved(bit)]), "row", 1 << bit))
    planes = [planes[j] for j in range(1, n_pre)]
    planes, columns = lax.optimization_barrier((planes, columns))
    masks = jnp.stack(
        [tree_mask]
        + [plane[2 * part_rows : 2 * part_rows + students, :blocks].astype(jnp.int32) for plane in planes]
    )

    first = lax.axis_index("pre") % n_slots * slot_tokens
    hid, base, cot = (lax.dynamic_slice_in_dim(x, first, slot_tokens, 0) for x in (hidden_in, frozen_query_base, cotangent))
    up = up_weight_matrix
    rows = heads * slot_tokens
    state = [jax.ShapeDtypeStruct((rows, c), f32) for c in (HD, HD, 3 * HD)]

    def attention(group, first, last, operands, in_specs, out_shape, scratch):
        sources, places = [], []
        for a, i, place in group:
            for array, _ in place:
                if not any(array is other for other in sources):
                    sources.append(array)
            index = [[array is other for other in sources].index(True) for array, _ in place]
            places.append((a, i, [(n, begin) for n, (_, begin) in zip(index, place)]))
        keys = len(places) * (n_pre - 1) * part_rows // 2 + (local_keys if first else 0)
        return pl.pallas_call(
            functools.partial(
                attention_kernel, n_pre, drop, part_rows, places, len(sources), first, last, tokens
            ),
            out_shape=out_shape,
            in_specs=[SMEM, VMEM, VMEM] + in_specs + [VMEM] * len(sources),
            out_specs=[VMEM] * len(out_shape),
            scratch_shapes=[
                pltpu.VMEM((keys, 2 * HD), bf16),
                pltpu.VMEM((rows, HD), bf16),
                pltpu.VMEM((rows, HD), bf16),
            ]
            + scratch,
            compiler_params=params(24 + keys * HD * 8 // MIB),
            cost_estimate=pl.CostEstimate(
                flops=4 * rows * keys * HD, bytes_accessed=keys * HD * 4, transcendentals=rows * keys // 2
            ),
            name="first_keys" if first else "last_keys" if last else "next_keys",
        )(masks, queries, cot, *operands, *sources)

    rounds = len(orders[0])
    away_rows = (n_pre - 1) * part_rows
    parts = [
        {0: jnp.concatenate([plane[a * part_rows : (a + 1) * part_rows] for plane in planes])}
        for a in range(2)
    ]
    groups = [[], [], []]
    for a in range(2):
        groups[0].append((a, 0, [(plane, a * part_rows) for plane in planes]))
    for k in range(rounds):
        got = []
        for a in range(2):
            bit = orders[a][k]
            payload = list(parts[a].values())
            if k == 0:
                payload += [columns[a][i] for i in moved(bit)]
            got.append(swap(jnp.concatenate(payload), "row", 1 << bit))
            if k == 0:
                put(a, bit, got[a][away_rows:])
        if k == 0:
            queries, latent_t = pl.pallas_call(
                functools.partial(query_kernel, n_row, tokens),
                out_shape=[
                    jax.ShapeDtypeStruct((slot_tokens, width), bf16),
                    jax.ShapeDtypeStruct((RANK, slot_tokens), bf16),
                ],
                in_specs=[SMEM] + [VMEM] * 5,
                out_specs=[VMEM] * 2,
                compiler_params=params(16),
                name="queries",
            )(adapter_ids, hid, base, up, *(jnp.concatenate(c) for c in columns))
        if k == rounds - 2:
            held = attention(groups[0], True, False, (k_prefix, v_prefix), [VMEM] * 2, state, [])
            got, held = lax.optimization_barrier((got, held))
        for a in range(2):
            for n, m in enumerate(list(parts[a])):
                there = m | 1 << orders[a][k]
                parts[a][there] = got[a][n * away_rows : (n + 1) * away_rows]
                place = [(got[a], n * away_rows + j * part_rows) for j in range(n_pre - 1)]
                groups[max(0, k + 3 - rounds)].append((a, there >> drop, place))
    held = attention(groups[1], False, False, held, [VMEM] * 3, state, [])
    attended, sent = attention(
        groups[2],
        False,
        True,
        (*held, adapter_ids, latent_t, up),
        [VMEM] * 3 + [SMEM] + [VMEM] * 2,
        [
            jax.ShapeDtypeStruct((slot_tokens, width), bf16),
            jax.ShapeDtypeStruct((RANK, width + slot_tokens), bf16),
        ],
        [pltpu.VMEM(s.shape, s.dtype) for s in state] + [pltpu.VMEM((slot_tokens, width), bf16)],
    )

    shared = [swap(sent, "pre", j) for j in range(n_slots)]
    attended, shared = lax.optimization_barrier((attended, shared))
    far_slot = n_slots >> 1
    attended_parts = {far_slot: swap(attended, "pre", far_slot)}

    pairs = n_row // 2
    even, odd = pl.pallas_call(
        functools.partial(down_kernel, n_slots, n_row, width),
        out_shape=[jax.ShapeDtypeStruct((pairs * RANK, depth + width), bf16)] * 2,
        in_specs=[VMEM] * (n_slots + 1),
        out_specs=[VMEM] * 2,
        compiler_params=params(16),
        name="down",
    )(*shared, hidden_in)
    odd = swap(odd, "row", 1)
    spans = [slice(m * RANK, (m + 1) * RANK) for m in range(pairs)]
    pieces = [swap(jnp.concatenate([even[at], odd[at]]), "row", 2 * m) for m, at in enumerate(spans)]

    attended_parts[0] = attended
    pieces, attended_parts[far_slot] = lax.optimization_barrier((pieces, attended_parts[far_slot]))
    for bit in range(n_slots.bit_length() - 2)[::-1]:
        for m in list(attended_parts):
            attended_parts[m | 1 << bit] = swap(attended_parts[m], "pre", 1 << bit)

    grad_a, up_weight_gradient = pl.pallas_call(
        functools.partial(finish_kernel, n_row, tokens),
        out_shape=[
            jax.ShapeDtypeStruct((depth, rank_cols), f32),
            jax.ShapeDtypeStruct((rank_cols, width), f32),
        ],
        in_specs=[SMEM] + [VMEM] * pairs,
        out_specs=[VMEM] * 2,
        scratch_shapes=[pltpu.VMEM((rank_cols, depth), f32)],
        compiler_params=params(16),
        name="finish",
    )(adapter_ids, *pieces)

    attended = pl.pallas_call(
        functools.partial(place_kernel, n_slots),
        out_shape=jax.ShapeDtypeStruct((tokens, width), bf16),
        in_specs=[VMEM] * n_slots,
        out_specs=HBM,
        scratch_shapes=[pltpu.SemaphoreType.DMA((n_slots,))],
        compiler_params=params(16),
        cost_estimate=pl.CostEstimate(
            flops=100 * tokens * width * HD, bytes_accessed=100 * tokens * width, transcendentals=0
        ),
        name="place",
    )(*(attended_parts[j] for j in range(n_slots)))
    return attended, grad_a, up_weight_gradient


def solution(mesh):
    in_specs = (
        P("row", None),
        P("row", None),
        P("pre", None),
        P("pre", None),
        P(None, "pre"),
        P(),
        P("row", None),
        P(),
        P("row", None),
    )
    out_specs = (P("row", None), P("row", None), P())
    return jax.shard_map(shards, mesh=mesh, in_specs=in_specs, out_specs=out_specs, check_vma=False)
```
